512 devices in a mesh: gx: 64 (over x, z_lo, core), gy: 8 (over z_hi, y).
Axes of the slice: x: 4, y: 4, z: 16 (z_hi: 2, z_lo: 8; z = z_hi * 8 + z_lo), core: 2. Of those that a mesh axis runs over, the one named last changes fastest.
Arguments:
- species: float32 [8, 16, 1024, 1024], P(None, None, 'gx', 'gy'), may hold values from 0.1 to 2
- porosity: float32 [16, 1024, 1024], P(None, 'gx', 'gy'), may hold values from 0.15 to 0.35
- pressure_old: float32 [16, 1024, 1024], P(None, 'gx', 'gy'), may hold values from -6 to 6
- source: float32 [16, 1024, 1024], P(None, 'gx', 'gy'), may hold values from -2 to 2
- zone_label: int32 [16, 1024, 1024], P(None, 'gx', 'gy'), may hold values from 0 to 3
- fixed_cell: int32 [16, 1024, 1024], P(None, 'gx', 'gy'), may hold values 0 or 1
Outputs:
- concentration: float32 [8, 16, 1024, 1024], P(None, None, 'gx', 'gy')
- pressure: float32 [16, 1024, 1024], P(None, 'gx', 'gy')
- porosity_next: float32 [16, 1024, 1024], P(None, 'gx', 'gy')
The draws below stay inside these ranges and needn't reach their ends.
Inputs may be any that keep to these rules, and one draw needn't show every extreme that they name: `zone_label`: one of four mineral zones.
All inputs are finite; a program needn't handle non-finite values. No bound on the sum of `fixed_cell` on one device may be relied on, other than what follows from the above.
Results may differ from the reference program's by a relative error of at most 0.0003.
Values sent between devices are 32-bit elements; how exact they have to be, the bound alone decides.
A program may use at most 128 MiB of HBM per device.

```python
import math
import jax
import jax.numpy as jnp

NSPEC = 8
NZ = 16
SWEEPS = 3
NX = 1024
NY = 1024


def draw_source(key, part):
    key = jax.random.fold_in(key, 11)
    rough_part = jax.random.normal(key, (NZ, NX, NY), jnp.float32)
    values = 0.5 * rough_part
    return jnp.clip(values, -2.0, 2.0)


def with_ends(values, own_key, smallest, largest):
    shape = values.shape
    index_at = [jax.random.randint(jax.random.fold_in(own_key, axis), (), 0, shape[axis]) for axis in range(len(shape))]
    values = values.at[tuple(index_at)].set(smallest)
    longest = shape.index(max(shape))
    index_at[longest] = (index_at[longest] + 1) % shape[longest]
    return values.at[tuple(index_at)].set(largest)


def levels(key, extent, pieces, smallest, top_value):
    level = 1.0
    for dim, blocks in pieces:
        draws = jax.random.uniform(jax.random.fold_in(jax.random.fold_in(key, 6), dim), (blocks,), jnp.float32, smallest / len(pieces), top_value / len(pieces))
        level = level * jnp.repeat(jnp.exp(draws), extent[dim] // blocks).reshape((-1,) + (1,) * (len(extent) - 1 - dim))
    return level


def noise(key, shape, width, reach, cuts=(), kind=jnp.bfloat16):
    loudness = levels(key, shape, cuts, -0.22, 0.18) if cuts else 1.0
    drawn = jax.random.normal(key, shape, jnp.float32) * width * loudness
    return jnp.minimum(jnp.maximum(drawn, -reach), reach).astype(kind)


def setup_inputs(seed: int = 0) -> dict:
    keys = jax.random.split(jax.random.key(seed), 7)
    species = jnp.clip(jnp.exp(math.log(2.0) - 2.9957323 * jax.random.uniform(keys[0], (NSPEC, NZ, NX, NY), jnp.float32) ** levels(keys[0], (NSPEC, NZ, NX, NY), ((2, 64), (3, 8)), -0.2, 0.2)), 0.1, 2.0)
    porosity = jnp.clip(0.15 + 0.19999999 * jax.random.uniform(keys[1], (NZ, NX, NY), jnp.float32) ** levels(keys[1], (NZ, NX, NY), ((1, 64), (2, 8)), -0.2, 0.2), 0.15, 0.35)
    pressure_old = noise(keys[2], (NZ, NX, NY), 1.0, 6.0, ((1, 64), (2, 8)), jnp.float32)
    source = draw_source(jax.random.fold_in(keys[6], 71), 0)
    zone_label = with_ends(jax.random.randint(keys[4], (NZ, NX, NY), 0, 4), jax.random.fold_in(keys[4], 1), 0, 3).astype(jnp.int32)
    fixed_cell = with_ends((jax.random.randint(keys[5], (NZ, NX, NY), 0, 8) < 1).astype(jnp.int32), jax.random.fold_in(keys[5], 1), 0, 1)
    return dict(species=species, porosity=porosity, pressure_old=pressure_old, source=source, zone_label=zone_label, fixed_cell=fixed_cell)


ZONE_RATES = (0.02, 0.05, 0.1, 0.2)
ZONE_PERMEABILITY = (5.0, 10.0, 20.0, 40.0)
SOLUBILITY = 0.5
MOLAR_VOLUME = 0.05
STORAGE_COEF = 0.2
TIME_STEP = 0.2
CHEB_SPREAD = 0.92
STOICHIOMETRY = (-1.0, -1.0, 0.0, 0.0, 0.0, 0.0, 0.0, 0.0)


def lookup(labels, table):
    total = jnp.zeros(labels.shape, jnp.float32)
    for label_level, level_value in enumerate(table):
        total = total + jnp.where(labels == label_level, jnp.float32(level_value), jnp.float32(0.0))
    return total


def beside_all(extended):
    centre = extended[..., 1:-1, 1:-1]
    widths = [(0, 0)] * (centre.ndim - 3) + [(1, 1), (0, 0), (0, 0)]
    zpadded = jnp.pad(centre, widths)
    sides = [extended[..., :-2, 1:-1], extended[..., 2:, 1:-1], extended[..., 1:-1, :-2], extended[..., 1:-1, 2:], zpadded[..., :-2, :, :], zpadded[..., 2:, :, :]]
    return centre, sides


def pad_plane(values_in):
    widths = [(0, 0)] * (values_in.ndim - 2) + [(1, 1), (1, 1)]
    return jnp.pad(values_in, widths)


def diagonal_of(storage, transmit):
    total = storage
    for term in transmit:
        total = total + term
    return total


def apply_operator(pressure_ext, transmit, storage):
    centre, sides = beside_all(pressure_ext)
    applied = storage * centre
    for term, beside in zip(transmit, sides):
        applied = applied + term * (centre - beside)
    return applied


def relax_weight(iteration):
    return 1.0 / (1.0 + CHEB_SPREAD * math.cos(math.pi * (2 * iteration + 1) / (2 * SWEEPS)))


def reference(species, porosity, pressure_old, source, zone_label, fixed_cell):
    reaction = lookup(zone_label, ZONE_RATES) * (species[0] * species[1] - SOLUBILITY)
    porosity_next = porosity - MOLAR_VOLUME * reaction
    permeab = lookup(zone_label, ZONE_PERMEABILITY) * porosity_next ** 3 / (1.0 - porosity_next) ** 2
    centre_k, sides_k = beside_all(pad_plane(permeab))
    transmit = [2.0 * centre_k * beside / (centre_k + beside) for beside in sides_k]
    storage = STORAGE_COEF * porosity_next
    diagonal_sum = diagonal_of(storage, transmit)
    rhs_field = storage * pressure_old + source
    free_mask = 1.0 - fixed_cell.astype(jnp.float32)
    pressure = pressure_old
    for iteration in range(SWEEPS):
        residual = (rhs_field - apply_operator(pad_plane(pressure), transmit, storage)) * free_mask
        pressure = pressure + relax_weight(iteration) * residual / diagonal_sum
    flow_centre, flow_sides = beside_all(pad_plane(pressure))
    centre_c, sides_c = beside_all(pad_plane(species))
    change = jnp.zeros(species.shape, jnp.float32)
    for term, beside_p, beside_c in zip(transmit, flow_sides, sides_c):
        outflow = term * (flow_centre - beside_p)
        change = change + outflow * jnp.where(outflow > 0, centre_c, beside_c)
    stoich = jnp.array(STOICHIOMETRY, jnp.float32)[:, None, None, None]
    concentration = species - (TIME_STEP / porosity_next) * change + stoich * reaction
    return concentration, pressure, porosity_next
```

```python
import math

import jax
import jax.numpy as jnp
from jax import lax
from jax.experimental import pallas as pl
from jax.experimental.pallas import tpu as pltpu
from jax.sharding import PartitionSpec as P

SWEEPS = 3
NSPEC, NZ, RX, LY = 8, 16, 16, 128
EX = RX + 8
FIELDS = 5
TINY = 1e-30

ZONE_RATES = (0.02, 0.05, 0.1, 0.2)
ZONE_PERMEABILITY = (5.0, 10.0, 20.0, 40.0)
SOLUBILITY = 0.5
MOLAR_VOLUME = 0.05
STORAGE_COEF = 0.2
TIME_STEP = 0.2
CHEB_SPREAD = 0.92
STOICHIOMETRY = (-1.0, -1.0, 0.0, 0.0, 0.0, 0.0, 0.0, 0.0)

F32 = jnp.float32
MESH = pl.DeviceIdType.MESH
DIRS = ((-1, 0), (1, 0), (0, -1), (0, 1), (-1, -1), (1, -1), (-1, 1), (1, 1))
OPPOSITE = tuple(DIRS.index((-a, -b)) for a, b in DIRS)


def relax_weight(iteration):
    return 1.0 / (1.0 + CHEB_SPREAD * math.cos(math.pi * (2 * iteration + 1) / (2 * SWEEPS)))


def lookup(labels, table):
    out = jnp.where(labels == 0, F32(table[0]), F32(table[1]))
    out = jnp.where(labels == 2, F32(table[2]), out)
    return jnp.where(labels == 3, F32(table[3]), out)


def inverse(x):
    guess = pl.reciprocal(x, approx=True)
    guess = guess * (2.0 - x * guess)
    return guess * (2.0 - x * guess)


def harmonic(a, b):
    return (2.0 * a * b) * inverse(jnp.maximum(a + b, TINY))


def lanes(x, shift):
    return pltpu.roll(x, shift % LY if isinstance(shift, int) else lax.rem(shift + 2 * LY, LY), 1)


def before(x):
    return pltpu.roll(x, 1, 0)


def after(x):
    return pltpu.roll(x, x.shape[0] - 1, 0)


def iota(rows, dim):
    return lax.broadcasted_iota(jnp.int32, (rows, LY), dim)


def flow_kernel(sizes, sp_in, por_in, old_in, src_in, zone_in, fix_in,
                sp, phi, rea, pa, tx, tyl, tyr, tz, edge, side, row_lo, row_hi,
                por, zone, fix, pb, perm, stor, rhs, gain,
                sx, sy, sc, ssx, ssy, rx, ry, rc, rsx, rsy,
                in_sem, send_sem, recv_sem, s_send, s_recv):
    gx, gy = lax.axis_index("gx"), lax.axis_index("gy")
    spots = []
    for dx, dy in DIRS:
        there = None
        for here, step, size in ((gx, dx, sizes[0]), (gy, dy, sizes[1])):
            if step:
                ok = here > 0 if step < 0 else here < size - 1
                there = ok if there is None else there & ok
        spots.append(((gx + dx, gy + dy), there))

    barrier = pltpu.get_barrier_semaphore()
    for where, there in spots:
        @pl.when(there)
        def _():
            pl.semaphore_signal(barrier, inc=1, device_id=where, device_id_type=MESH)

    loads = [
        pltpu.make_async_copy(sp_in.at[pl.ds(0, 2)], sp.at[pl.ds(0, 2)], in_sem.at[0]),
        pltpu.make_async_copy(por_in, por, in_sem.at[1]),
        pltpu.make_async_copy(zone_in, zone, in_sem.at[2]),
        pltpu.make_async_copy(old_in, pa.at[pl.ds(1, NZ), pl.ds(0, RX)], in_sem.at[3]),
        pltpu.make_async_copy(src_in, rhs.at[:, pl.ds(0, RX)], in_sem.at[4]),
        pltpu.make_async_copy(fix_in, fix, in_sem.at[5]),
        pltpu.make_async_copy(sp_in.at[pl.ds(2, NSPEC - 2)], sp.at[pl.ds(2, NSPEC - 2)], in_sem.at[6]),
    ]
    for c in loads:
        c.start()

    for i in range(8):
        @pl.when(jnp.logical_not(spots[i][1]))
        def _():
            if i < 2:
                rx[i] = jnp.zeros(rx.shape[1:], F32)
                rsx[i] = jnp.zeros(rsx.shape[1:], F32)
            elif i < 4:
                ry[i - 2] = jnp.zeros(ry.shape[1:], F32)
                rsy[i - 2] = jnp.zeros(rsy.shape[1:], F32)
            else:
                rc[i - 4] = jnp.zeros(rc.shape[1:], F32)
    plane = jnp.zeros((EX, LY), F32)
    for ref in (perm, pa, pb):
        ref[0] = plane
        ref[NZ + 1] = plane

    lane = iota(RX, 1)
    group = lax.shift_right_logical(lane, 3)
    low = (lane & 7) < 4
    for c in loads[:6]:
        c.wait()

    def own(z, packs):
        c0, c1 = sp[0, z], sp[1, z]
        label = zone[z]
        reaction = lookup(label, ZONE_RATES) * (c0 * c1 - SOLUBILITY)
        new = por[z] - MOLAR_VOLUME * reaction
        solid = 1.0 - new
        k = lookup(label, ZONE_PERMEABILITY) * (new * new * new) * inverse(solid * solid)
        s = STORAGE_COEF * new
        free = 1.0 - fix[z].astype(F32)
        p, q = pa[z + 1, :RX], rhs[z, :RX]
        rea[z] = reaction
        phi[z] = new
        perm[z + 1, :RX] = k
        stor[z, :RX] = s
        gain[z, :RX] = free
        out = []
        for f, (v, pack) in enumerate(zip((k, p, s, q, free), packs)):
            sx[0, f, z] = v[:4]
            sx[1, f, z] = v[12:]
            out.append(jnp.where(group == z, lanes(v, 8 * z + 4), pack))
        return tuple(out)

    zero = jnp.zeros((RX, LY), F32)
    packs = lax.fori_loop(0, NZ, own, (zero,) * FIELDS, unroll=2)
    for j in range(3):
        a, b = packs[2 * j], packs[2 * j + 1] if j < 2 else zero
        down = jnp.where(low, lanes(a, -4), b)
        up = jnp.where(low, a, lanes(b, 4))
        sy[0, j] = down
        sy[1, j] = up
        sc[0, j], sc[1, j] = down[:4], down[12:]
        sc[2, j], sc[3, j] = up[:4], up[12:]

    def parts(i):
        if i < 2:
            return sx.at[i], rx, i
        if i < 4:
            return sy.at[i - 2], ry, i - 2
        return sc.at[i - 4], rc, i - 4

    def copy(i):
        src, _, _ = parts(i)
        _, dst, at = parts(OPPOSITE[i])
        return pltpu.make_async_remote_copy(
            src_ref=src, dst_ref=dst.at[at], send_sem=send_sem.at[i],
            recv_sem=recv_sem.at[OPPOSITE[i]], device_id=spots[i][0], device_id_type=MESH)

    def arrival(i):
        src, dst, at = parts(i)
        return pltpu.make_async_remote_copy(
            src_ref=src, dst_ref=dst.at[at], send_sem=send_sem.at[i],
            recv_sem=recv_sem.at[i], device_id=spots[i][0], device_id_type=MESH)

    def sparts(i):
        return (ssx.at[i], rsx, i) if i < 2 else (ssy.at[i - 2], rsy, i - 2)

    def scopy(i):
        src, _, _ = sparts(i)
        _, dst, at = sparts(OPPOSITE[i])
        return pltpu.make_async_remote_copy(
            src_ref=src, dst_ref=dst.at[at], send_sem=s_send.at[i],
            recv_sem=s_recv.at[OPPOSITE[i]], device_id=spots[i][0], device_id_type=MESH)

    def sarrival(i):
        src, dst, at = sparts(i)
        return pltpu.make_async_remote_copy(
            src_ref=src, dst_ref=dst.at[at], send_sem=s_send.at[i],
            recv_sem=s_recv.at[i], device_id=spots[i][0], device_id_type=MESH)

    pl.semaphore_wait(barrier, sum(there.astype(jnp.int32) for _, there in spots))
    for i in (2, 3, 4, 5, 6, 7, 0, 1):
        @pl.when(spots[i][1])
        def _():
            copy(i).start()

    loads[6].wait()
    for s in range(NSPEC):
        for z in range(NZ):
            ssx[0, s, pl.ds(z, 1)] = sp[s, z, pl.ds(0, 1)]
            ssx[1, s, pl.ds(z, 1)] = sp[s, z, pl.ds(RX - 1, 1)]
    pair = lax.shift_right_logical(lane, 1)
    odd = (lane & 1) == 1

    def species_edge(z, packs):
        lo, hi = packs
        for s in range(NSPEC):
            m = lax.rem(z, 8) * 8 + s
            turned = lanes(sp[s, z], 2 * m + 1)
            lo = jnp.where((pair == m) & (z < 8), turned, lo)
            hi = jnp.where((pair == m) & (z >= 8), turned, hi)
        return lo, hi

    lo, hi = lax.fori_loop(0, NZ, species_edge, (zero, zero))
    ssy[0] = jnp.where(odd, lo, lanes(hi, -1))
    ssy[1] = jnp.where(odd, lanes(hi, 1), lo)
    for i in (2, 3, 0, 1):
        @pl.when(spots[i][1])
        def _():
            scopy(i).start()

    for i in range(8):
        @pl.when(spots[i][1])
        def _():
            arrival(i).wait_recv()

    lane8, lane24 = iota(8, 1), iota(EX, 1)
    group8 = lax.shift_right_logical(lane8, 3)
    low24 = (lane24 & 7) < 4

    def rows(z, packs):
        out = []
        for f, pack in enumerate(packs):
            tail = jnp.concatenate([rx[1, f, z], rx[0, f, z]], axis=0)
            if f == 0:
                perm[z + 1, RX:] = tail
            elif f == 1:
                pa[z + 1, RX:] = tail
            else:
                (stor, rhs, gain)[f - 2][z, RX:] = tail
            out.append(jnp.where(group8 == z, lanes(tail, 8 * z + 4), pack))
        return tuple(out)

    tails = lax.fori_loop(0, NZ, rows, (jnp.zeros((8, LY), F32),) * FIELDS, unroll=2)
    whole = [jnp.concatenate([a, b], axis=0) for a, b in zip(packs, tails)]

    strips = []
    for d in range(2):
        fields = []
        for f in range(FIELDS):
            j = f // 2
            halo = jnp.concatenate([ry[d, j], rc[2 * d + 1, j], rc[2 * d, j]], axis=0)
            if d == 0:
                fields.append(jnp.where(low24, halo if f % 2 == 0 else lanes(halo, -4), whole[f]))
            else:
                fields.append(jnp.where(low24, whole[f], lanes(halo, 4) if f % 2 == 0 else halo))
        k, p, s, q, free = fields
        fx_t = harmonic(k, before(k))
        fy_t = harmonic(k, lanes(k, 1))
        fz_t = jnp.where(lane24 < 8, 0.0, harmonic(k, lanes(k, 8)))
        total = s + fx_t + after(fx_t) + fy_t + lanes(fy_t, -1) + fz_t + lanes(fz_t, -8)
        g = free * inverse(jnp.maximum(total, TINY))
        right = s * p + q
        history = [p]
        for it in range(SWEEPS):
            fx = fx_t * (p - before(p))
            fy = fy_t * (p - lanes(p, 1))
            fz = fz_t * (p - lanes(p, 8))
            r = right - s * p - fx + after(fx) - fy + lanes(fy, -1) - fz + lanes(fz, -8)
            p = p + F32(relax_weight(it)) * g * r
            history.append(p)
        strips.append((fy_t, history))
    column = lane24 & 7
    faces = jnp.where(column == 4, strips[0][0], lanes(strips[1][0], -1))
    edges = [jnp.where(column == 3, a, lanes(b, -2)) for a, b in zip(strips[0][1], strips[1][1])]
    edge[...] = edges[SWEEPS][:RX]

    first, last = lane24 == 0, lane24 == LY - 1

    def coefficients(z, tz_lo):
        k = perm[z + 1]
        tz_hi = harmonic(k, perm[z + 2])
        turned = lanes(faces, -(8 * z + 4))
        t_x = harmonic(k, before(k))
        t_lo = jnp.where(first, turned, harmonic(k, lanes(k, 1)))
        t_hi = jnp.where(last, turned, lanes(t_lo, -1))
        s = stor[z]
        total = s + t_x + after(t_x) + t_lo + t_hi + tz_lo + tz_hi
        tx[z], tyl[z], tyr[z], tz[z] = t_x, t_lo, t_hi, tz_lo
        gain[z] = gain[z] * inverse(jnp.maximum(total, TINY))
        rhs[z] = s * pa[z + 1] + rhs[z]
        return tz_hi

    tz[NZ] = lax.fori_loop(0, NZ, coefficients, plane)

    for it in range(SWEEPS):
        src, dst = (pa, pb) if it % 2 == 0 else (pb, pa)

        def sweep(z, flow_lo):
            p = src[z + 1]
            turned = lanes(edges[it], -(8 * z + 3))
            fx = tx[z] * (p - before(p))
            f_lo = tyl[z] * (p - jnp.where(first, turned, lanes(p, 1)))
            f_hi = tyr[z] * (jnp.where(last, turned, lanes(p, -1)) - p)
            flow_hi = tz[z + 1] * (src[z + 2] - p)
            r = rhs[z] - stor[z] * p - fx + after(fx) - f_lo + f_hi - flow_lo + flow_hi
            dst[z + 1] = p + F32(relax_weight(it)) * gain[z] * r
            return flow_hi

        lax.fori_loop(0, NZ, sweep, plane)
    if SWEEPS % 2:
        def back(z, c):
            pa[z + 1] = pb[z + 1]
            return c
        lax.fori_loop(0, NZ, back, 0)

    for i in range(4):
        @pl.when(spots[i][1])
        def _():
            sarrival(i).wait_recv()
    m_lo, m_hi = rsy[0], rsy[1]
    side[0] = jnp.where(odd, lanes(m_lo, 1), lanes(m_hi, -1))
    side[1] = jnp.where(odd, m_lo, m_hi)
    row_lo[...] = rsx[0]
    row_hi[...] = rsx[1]
    for i in range(8):
        @pl.when(spots[i][1])
        def _():
            copy(i).wait_send()
            if i < 4:
                scopy(i).wait_send()


def transport_kernel(sp, phi, rea, p_ref, tx, tyl, tyr, tz, edge, side, row_lo, row_hi,
                     conc_out, p_out, phi_out, conc, sem):
    outs = [
        pltpu.make_async_copy(p_ref.at[pl.ds(1, NZ), pl.ds(0, RX)], p_out, sem.at[0]),
        pltpu.make_async_copy(phi, phi_out, sem.at[1]),
    ]
    for c in outs:
        c.start()
    lane, row = iota(RX, 1), iota(RX, 0)
    first, last = lane == 0, lane == LY - 1
    top, bottom = row == 0, row == RX - 1

    def body(z, carry):
        wide = p_ref[z + 1]
        p = wide[:RX]
        turned = lanes(edge[...], -(8 * z + 3))
        t_x = tx[z]
        flows = [
            t_x[:RX] * (p - before(wide)[:RX]),
            after(t_x)[:RX] * (p - after(wide)[:RX]),
            tyl[z, :RX] * (p - jnp.where(first, turned, lanes(p, 1))),
            tyr[z, :RX] * (p - jnp.where(last, turned, lanes(p, -1))),
            tz[z, :RX] * (p - p_ref[z, :RX]),
            tz[z + 1, :RX] * (p - p_ref[z + 2, :RX]),
        ]
        scale = TIME_STEP * inverse(phi[z])
        out = jnp.maximum(flows[0], 0.0)
        for f in flows[1:]:
            out = out + jnp.maximum(f, 0.0)
        keep = 1.0 - scale * out
        take = [-scale * jnp.minimum(f, 0.0) for f in flows]
        reaction = rea[z]
        z_lo, z_hi = jnp.maximum(z - 1, 0), jnp.minimum(z + 1, NZ - 1)
        half = side[lax.div(z, 8)]
        for s in range(NSPEC):
            c = sp[s, z]
            turned_c = lanes(half, -(2 * (lax.rem(z, 8) * 8 + s) + 1))
            total = c * keep
            total = total + take[0] * jnp.where(top, row_lo[s, pl.ds(z, 1)], before(c))
            total = total + take[1] * jnp.where(bottom, row_hi[s, pl.ds(z, 1)], after(c))
            total = total + take[2] * jnp.where(first, turned_c, lanes(c, 1))
            total = total + take[3] * jnp.where(last, turned_c, lanes(c, -1))
            total = total + take[4] * sp[s, z_lo]
            total = total + take[5] * sp[s, z_hi]
            if STOICHIOMETRY[s]:
                total = total + STOICHIOMETRY[s] * reaction
            conc[s, z] = total
        return carry

    for part in range(4):
        lax.fori_loop(4 * part, 4 * part + 4, body, 0)
        at = pl.ds(4 * part, 4)
        c = pltpu.make_async_copy(conc.at[:, at], conc_out.at[:, at], sem.at[2 + part])
        c.start()
        outs.append(c)
    for c in outs:
        c.wait()


def build(sizes):
    tile = (NZ, RX, LY)
    wide = (NZ, EX, LY)
    species = (NSPEC, NZ, RX, LY)
    vmem = pl.BlockSpec(memory_space=pltpu.VMEM)
    hbm = pl.BlockSpec(memory_space=pltpu.HBM)

    def shards(sp, por, old, src, zone, fix):
        middle = [
            species, tile, tile, (NZ + 2, EX, LY), wide, wide, wide, (NZ + 1, EX, LY),
            (RX, LY), (2, RX, LY), (NSPEC, NZ, LY), (NSPEC, NZ, LY),
        ]
        shared = pl.pallas_call(
            lambda *refs: flow_kernel(sizes, *refs),
            out_shape=[pltpu.VMEM(shape, F32) for shape in middle],
            in_specs=[hbm] * 6,
            out_specs=[vmem] * len(middle),
            scratch_shapes=[
                pltpu.VMEM(tile, F32), pltpu.VMEM(tile, jnp.int32), pltpu.VMEM(tile, jnp.int32),
                pltpu.VMEM((NZ + 2, EX, LY), F32), pltpu.VMEM((NZ + 2, EX, LY), F32),
                pltpu.VMEM(wide, F32), pltpu.VMEM(wide, F32), pltpu.VMEM(wide, F32),
                pltpu.VMEM((2, FIELDS, NZ, 4, LY), F32), pltpu.VMEM((2, 3, RX, LY), F32),
                pltpu.VMEM((4, 3, 4, LY), F32), pltpu.VMEM((2, NSPEC, NZ, LY), F32),
                pltpu.VMEM((2, RX, LY), F32),
                pltpu.VMEM((2, FIELDS, NZ, 4, LY), F32), pltpu.VMEM((2, 3, RX, LY), F32),
                pltpu.VMEM((4, 3, 4, LY), F32), pltpu.VMEM((2, NSPEC, NZ, LY), F32),
                pltpu.VMEM((2, RX, LY), F32),
                pltpu.SemaphoreType.DMA((7,)), pltpu.SemaphoreType.DMA((8,)),
                pltpu.SemaphoreType.DMA((8,)), pltpu.SemaphoreType.DMA((4,)),
                pltpu.SemaphoreType.DMA((4,)),
            ],
            compiler_params=pltpu.CompilerParams(
                collective_id=0, has_side_effects=True, vmem_limit_bytes=32 * 2**20),
            name="flow",
        )(sp, por, old, src, zone, fix)
        return tuple(pl.pallas_call(
            transport_kernel,
            out_shape=[jax.ShapeDtypeStruct(s, F32) for s in (species, tile, tile)],
            in_specs=[vmem] * len(middle),
            out_specs=[hbm] * 3,
            scratch_shapes=[pltpu.VMEM(species, F32), pltpu.SemaphoreType.DMA((6,))],
            compiler_params=pltpu.CompilerParams(vmem_limit_bytes=16 * 2**20),
            name="transport",
        )(*shared))

    return shards


def solution(mesh):
    specs = (P(None, None, "gx", "gy"),) + (P(None, "gx", "gy"),) * 5
    outs = (P(None, None, "gx", "gy"), P(None, "gx", "gy"), P(None, "gx", "gy"))
    sizes = (mesh.shape["gx"], mesh.shape["gy"])
    return jax.shard_map(build(sizes), mesh=mesh, in_specs=specs, out_specs=outs, check_vma=False)
```

```python
import math

import jax
import jax.numpy as jnp
from jax import lax
from jax.experimental import pallas as pl
from jax.experimental.pallas import tpu as pltpu
from jax.sharding import PartitionSpec as P

SWEEPS = 3
NSPEC, NZ, RX, LY = 8, 16, 16, 128
EX = RX + 8
FIELDS = 5
TINY = 1e-30

ZONE_RATES = (0.02, 0.05, 0.1, 0.2)
ZONE_PERMEABILITY = (5.0, 10.0, 20.0, 40.0)
SOLUBILITY = 0.5
MOLAR_VOLUME = 0.05
STORAGE_COEF = 0.2
TIME_STEP = 0.2
CHEB_SPREAD = 0.92
STOICHIOMETRY = (-1.0, -1.0, 0.0, 0.0, 0.0, 0.0, 0.0, 0.0)

F32 = jnp.float32
MESH = pl.DeviceIdType.MESH
DIRS = ((-1, 0), (1, 0), (0, -1), (0, 1), (-1, -1), (1, -1), (-1, 1), (1, 1))
OPPOSITE = tuple(DIRS.index((-a, -b)) for a, b in DIRS)


def relax_weight(iteration):
    return 1.0 / (1.0 + CHEB_SPREAD * math.cos(math.pi * (2 * iteration + 1) / (2 * SWEEPS)))


def lookup(labels, table):
    out = jnp.where(labels == 0, F32(table[0]), F32(table[1]))
    out = jnp.where(labels == 2, F32(table[2]), out)
    return jnp.where(labels == 3, F32(table[3]), out)


def inverse(x):
    guess = pl.reciprocal(x, approx=True)
    guess = guess * (2.0 - x * guess)
    return guess * (2.0 - x * guess)


def harmonic(a, b):
    return (2.0 * a * b) * inverse(jnp.maximum(a + b, TINY))


def lanes(x, shift):
    return pltpu.roll(x, shift % LY if isinstance(shift, int) else lax.rem(shift + 2 * LY, LY), 1)


def before(x):
    return pltpu.roll(x, 1, 0)


def after(x):
    return pltpu.roll(x, x.shape[0] - 1, 0)


def iota(rows, dim):
    return lax.broadcasted_iota(jnp.int32, (rows, LY), dim)


def flow_kernel(sizes, sp_in, por_in, old_in, src_in, zone_in, fix_in,
                sp, phi, rea, pb, tx, tyl, tyr, tz, edge, side, row_lo, row_hi,
                por, zone, fix, pa, perm, stor, rhs, gain,
                sx, sy, sc, ssx, ssy, rx, ry, rc, rsx, rsy,
                in_sem, send_sem, recv_sem, s_send, s_recv):
    gx, gy = lax.axis_index("gx"), lax.axis_index("gy")
    spots = []
    for dx, dy in DIRS:
        there = None
        for here, step, size in ((gx, dx, sizes[0]), (gy, dy, sizes[1])):
            if step:
                ok = here > 0 if step < 0 else here < size - 1
                there = ok if there is None else there & ok
        spots.append(((gx + dx, gy + dy), there))

    barrier = pltpu.get_barrier_semaphore()
    for where, there in spots:
        @pl.when(there)
        def _():
            pl.semaphore_signal(barrier, inc=1, device_id=where, device_id_type=MESH)

    loads = [
        pltpu.make_async_copy(sp_in.at[pl.ds(0, 2)], sp.at[pl.ds(0, 2)], in_sem.at[0]),
        pltpu.make_async_copy(por_in, por, in_sem.at[1]),
        pltpu.make_async_copy(zone_in, zone, in_sem.at[2]),
        pltpu.make_async_copy(old_in, pa.at[pl.ds(1, NZ), pl.ds(0, RX)], in_sem.at[3]),
        pltpu.make_async_copy(src_in, rhs.at[:, pl.ds(0, RX)], in_sem.at[4]),
        pltpu.make_async_copy(fix_in, fix, in_sem.at[5]),
        pltpu.make_async_copy(sp_in.at[pl.ds(2, NSPEC - 2)], sp.at[pl.ds(2, NSPEC - 2)], in_sem.at[6]),
    ]
    for c in loads:
        c.start()

    for i in range(8):
        @pl.when(jnp.logical_not(spots[i][1]))
        def _():
            if i < 2:
                rx[i] = jnp.zeros(rx.shape[1:], F32)
                rsx[i] = jnp.zeros(rsx.shape[1:], F32)
            elif i < 4:
                ry[i - 2] = jnp.zeros(ry.shape[1:], F32)
                rsy[i - 2] = jnp.zeros(rsy.shape[1:], F32)
            else:
                rc[i - 4] = jnp.zeros(rc.shape[1:], F32)
    plane = jnp.zeros((EX, LY), F32)
    for ref in (perm, pa, pb):
        ref[0] = plane
        ref[NZ + 1] = plane

    lane = iota(RX, 1)
    group = lax.shift_right_logical(lane, 3)
    low = (lane & 7) < 4
    for c in loads[:6]:
        c.wait()

    def own(z, packs):
        c0, c1 = sp[0, z], sp[1, z]
        label = zone[z]
        reaction = lookup(label, ZONE_RATES) * (c0 * c1 - SOLUBILITY)
        new = por[z] - MOLAR_VOLUME * reaction
        solid = 1.0 - new
        k = lookup(label, ZONE_PERMEABILITY) * (new * new * new) * inverse(solid * solid)
        s = STORAGE_COEF * new
        free = 1.0 - fix[z].astype(F32)
        p, q = pa[z + 1, :RX], rhs[z, :RX]
        rea[z] = reaction
        phi[z] = new
        perm[z + 1, :RX] = k
        stor[z, :RX] = s
        gain[z, :RX] = free
        out = []
        for f, (v, pack) in enumerate(zip((k, p, s, q, free), packs)):
            sx[0, f, z] = v[:4]
            sx[1, f, z] = v[12:]
            out.append(jnp.where(group == z, lanes(v, 8 * z + 4), pack))
        return tuple(out)

    zero = jnp.zeros((RX, LY), F32)
    packs = lax.fori_loop(0, NZ, own, (zero,) * FIELDS, unroll=8)
    for j in range(3):
        a, b = packs[2 * j], packs[2 * j + 1] if j < 2 else zero
        down = jnp.where(low, lanes(a, -4), b)
        up = jnp.where(low, a, lanes(b, 4))
        sy[0, j] = down
        sy[1, j] = up
        sc[0, j], sc[1, j] = down[:4], down[12:]
        sc[2, j], sc[3, j] = up[:4], up[12:]

    def parts(i):
        if i < 2:
            return sx.at[i], rx, i
        if i < 4:
            return sy.at[i - 2], ry, i - 2
        return sc.at[i - 4], rc, i - 4

    def copy(i):
        src, _, _ = parts(i)
        _, dst, at = parts(OPPOSITE[i])
        return pltpu.make_async_remote_copy(
            src_ref=src, dst_ref=dst.at[at], send_sem=send_sem.at[i],
            recv_sem=recv_sem.at[OPPOSITE[i]], device_id=spots[i][0], device_id_type=MESH)

    def arrival(i):
        src, dst, at = parts(i)
        return pltpu.make_async_remote_copy(
            src_ref=src, dst_ref=dst.at[at], send_sem=send_sem.at[i],
            recv_sem=recv_sem.at[i], device_id=spots[i][0], device_id_type=MESH)

    def sparts(i):
        return (ssx.at[i], rsx, i) if i < 2 else (ssy.at[i - 2], rsy, i - 2)

    def scopy(i):
        src, _, _ = sparts(i)
        _, dst, at = sparts(OPPOSITE[i])
        return pltpu.make_async_remote_copy(
            src_ref=src, dst_ref=dst.at[at], send_sem=s_send.at[i],
            recv_sem=s_recv.at[OPPOSITE[i]], device_id=spots[i][0], device_id_type=MESH)

    def sarrival(i):
        src, dst, at = sparts(i)
        return pltpu.make_async_remote_copy(
            src_ref=src, dst_ref=dst.at[at], send_sem=s_send.at[i],
            recv_sem=s_recv.at[i], device_id=spots[i][0], device_id_type=MESH)

    pl.semaphore_wait(barrier, sum(there.astype(jnp.int32) for _, there in spots))
    for i in (2, 3, 4, 5, 6, 7, 0, 1):
        @pl.when(spots[i][1])
        def _():
            copy(i).start()

    loads[6].wait()
    for s in range(NSPEC):
        for z in range(NZ):
            ssx[0, s, pl.ds(z, 1)] = sp[s, z, pl.ds(0, 1)]
            ssx[1, s, pl.ds(z, 1)] = sp[s, z, pl.ds(RX - 1, 1)]
    pair = lax.shift_right_logical(lane, 1)
    odd = (lane & 1) == 1

    def species_edge(z, packs):
        lo, hi = packs
        for s in range(NSPEC):
            m = lax.rem(z, 8) * 8 + s
            turned = lanes(sp[s, z], 2 * m + 1)
            lo = jnp.where((pair == m) & (z < 8), turned, lo)
            hi = jnp.where((pair == m) & (z >= 8), turned, hi)
        return lo, hi

    lo, hi = lax.fori_loop(0, NZ, species_edge, (zero, zero), unroll=2)
    ssy[0] = jnp.where(odd, lo, lanes(hi, -1))
    ssy[1] = jnp.where(odd, lanes(hi, 1), lo)
    for i in (2, 3, 0, 1):
        @pl.when(spots[i][1])
        def _():
            scopy(i).start()

    for i in range(8):
        @pl.when(spots[i][1])
        def _():
            arrival(i).wait_recv()

    lane8, lane24 = iota(8, 1), iota(EX, 1)
    group8 = lax.shift_right_logical(lane8, 3)
    low24 = (lane24 & 7) < 4

    def rows(z, packs):
        out = []
        for f, pack in enumerate(packs):
            tail = jnp.concatenate([rx[1, f, z], rx[0, f, z]], axis=0)
            if f == 0:
                perm[z + 1, RX:] = tail
            elif f == 1:
                pa[z + 1, RX:] = tail
            else:
                (stor, rhs, gain)[f - 2][z, RX:] = tail
            out.append(jnp.where(group8 == z, lanes(tail, 8 * z + 4), pack))
        return tuple(out)

    tails = lax.fori_loop(0, NZ, rows, (jnp.zeros((8, LY), F32),) * FIELDS, unroll=8)
    whole = [jnp.concatenate([a, b], axis=0) for a, b in zip(packs, tails)]

    strips = []
    for d in range(2):
        fields = []
        for f in range(FIELDS):
            j = f // 2
            halo = jnp.concatenate([ry[d, j], rc[2 * d + 1, j], rc[2 * d, j]], axis=0)
            if d == 0:
                fields.append(jnp.where(low24, halo if f % 2 == 0 else lanes(halo, -4), whole[f]))
            else:
                fields.append(jnp.where(low24, whole[f], lanes(halo, 4) if f % 2 == 0 else halo))
        k, p, s, q, free = fields
        fx_t = harmonic(k, before(k))
        fy_t = harmonic(k, lanes(k, 1))
        fz_t = jnp.where(lane24 < 8, 0.0, harmonic(k, lanes(k, 8)))
        total = s + fx_t + after(fx_t) + fy_t + lanes(fy_t, -1) + fz_t + lanes(fz_t, -8)
        g = free * inverse(jnp.maximum(total, TINY))
        right = s * p + q
        history = [p]
        for it in range(SWEEPS):
            fx = fx_t * (p - before(p))
            fy = fy_t * (p - lanes(p, 1))
            fz = fz_t * (p - lanes(p, 8))
            r = right - s * p - fx + after(fx) - fy + lanes(fy, -1) - fz + lanes(fz, -8)
            p = p + F32(relax_weight(it)) * g * r
            history.append(p)
        strips.append((fy_t, history))
    column = lane24 & 7
    faces = jnp.where(column == 4, strips[0][0], lanes(strips[1][0], -1))
    edges = [jnp.where(column == 3, a, lanes(b, -2)) for a, b in zip(strips[0][1], strips[1][1])]
    edge[...] = edges[SWEEPS][:RX]

    first, last = lane24 == 0, lane24 == LY - 1

    def coefficients(z, tz_lo):
        k = perm[z + 1]
        tz_hi = harmonic(k, perm[z + 2])
        turned = lanes(faces, -(8 * z + 4))
        t_x = harmonic(k, before(k))
        t_lo = jnp.where(first, turned, harmonic(k, lanes(k, 1)))
        t_hi = jnp.where(last, turned, lanes(t_lo, -1))
        s = stor[z]
        total = s + t_x + after(t_x) + t_lo + t_hi + tz_lo + tz_hi
        tx[z], tyl[z], tyr[z], tz[z] = t_x, t_lo, t_hi, tz_lo
        gain[z] = gain[z] * inverse(jnp.maximum(total, TINY))
        rhs[z] = s * pa[z + 1] + rhs[z]
        return tz_hi

    tz[NZ] = lax.fori_loop(0, NZ, coefficients, plane, unroll=NZ)

    for it in range(SWEEPS):
        src, dst = (pa, pb) if it % 2 == 0 else (pb, pa)

        def sweep(z, flow_lo):
            p = src[z + 1]
            turned = lanes(edges[it], -(8 * z + 3))
            fx = tx[z] * (p - before(p))
            f_lo = tyl[z] * (p - jnp.where(first, turned, lanes(p, 1)))
            f_hi = tyr[z] * (jnp.where(last, turned, lanes(p, -1)) - p)
            flow_hi = tz[z + 1] * (src[z + 2] - p)
            r = rhs[z] - stor[z] * p - fx + after(fx) - f_lo + f_hi - flow_lo + flow_hi
            dst[z + 1] = p + F32(relax_weight(it)) * gain[z] * r
            return flow_hi

        lax.fori_loop(0, NZ, sweep, plane, unroll=NZ)

    for i in range(4):
        @pl.when(spots[i][1])
        def _():
            sarrival(i).wait_recv()
    m_lo, m_hi = rsy[0], rsy[1]
    side[0] = jnp.where(odd, lanes(m_lo, 1), lanes(m_hi, -1))
    side[1] = jnp.where(odd, m_lo, m_hi)
    row_lo[...] = rsx[0]
    row_hi[...] = rsx[1]
    for i in range(8):
        @pl.when(spots[i][1])
        def _():
            copy(i).wait_send()
            if i < 4:
                scopy(i).wait_send()


def transport_kernel(sp, phi, rea, p_ref, tx, tyl, tyr, tz, edge, side, row_lo, row_hi,
                     conc_out, p_out, phi_out, conc, sem):
    outs = [
        pltpu.make_async_copy(p_ref.at[pl.ds(1, NZ), pl.ds(0, RX)], p_out, sem.at[0]),
        pltpu.make_async_copy(phi, phi_out, sem.at[1]),
    ]
    for c in outs:
        c.start()
    lane, row = iota(RX, 1), iota(RX, 0)
    first, last = lane == 0, lane == LY - 1
    top, bottom = row == 0, row == RX - 1

    def body(z, carry):
        wide = p_ref[z + 1]
        p = wide[:RX]
        turned = lanes(edge[...], -(8 * z + 3))
        t_x = tx[z]
        flows = [
            t_x[:RX] * (p - before(wide)[:RX]),
            after(t_x)[:RX] * (p - after(wide)[:RX]),
            tyl[z, :RX] * (p - jnp.where(first, turned, lanes(p, 1))),
            tyr[z, :RX] * (p - jnp.where(last, turned, lanes(p, -1))),
            tz[z, :RX] * (p - p_ref[z, :RX]),
            tz[z + 1, :RX] * (p - p_ref[z + 2, :RX]),
        ]
        scale = TIME_STEP * inverse(phi[z])
        out = jnp.maximum(flows[0], 0.0)
        for f in flows[1:]:
            out = out + jnp.maximum(f, 0.0)
        keep = 1.0 - scale * out
        take = [-scale * jnp.minimum(f, 0.0) for f in flows]
        reaction = rea[z]
        z_lo, z_hi = jnp.maximum(z - 1, 0), jnp.minimum(z + 1, NZ - 1)
        half = side[lax.div(z, 8)]
        for s in range(NSPEC):
            c = sp[s, z]
            turned_c = lanes(half, -(2 * (lax.rem(z, 8) * 8 + s) + 1))
            total = c * keep
            total = total + take[0] * jnp.where(top, row_lo[s, pl.ds(z, 1)], before(c))
            total = total + take[1] * jnp.where(bottom, row_hi[s, pl.ds(z, 1)], after(c))
            total = total + take[2] * jnp.where(first, turned_c, lanes(c, 1))
            total = total + take[3] * jnp.where(last, turned_c, lanes(c, -1))
            total = total + take[4] * sp[s, z_lo]
            total = total + take[5] * sp[s, z_hi]
            if STOICHIOMETRY[s]:
                total = total + STOICHIOMETRY[s] * reaction
            conc[s, z] = total
        return carry

    for part in range(4):
        lax.fori_loop(4 * part, 4 * part + 4, body, 0, unroll=4)
        at = pl.ds(4 * part, 4)
        c = pltpu.make_async_copy(conc.at[:, at], conc_out.at[:, at], sem.at[2 + part])
        c.start()
        outs.append(c)
    for c in outs:
        c.wait()


def build(sizes):
    tile = (NZ, RX, LY)
    wide = (NZ, EX, LY)
    species = (NSPEC, NZ, RX, LY)
    vmem = pl.BlockSpec(memory_space=pltpu.VMEM)
    hbm = pl.BlockSpec(memory_space=pltpu.HBM)

    def shards(*args):
        args = [pltpu.with_memory_space_constraint(a, pltpu.HBM) for a in args]
        middle = [
            species, tile, tile, (NZ + 2, EX, LY), wide, wide, wide, (NZ + 1, EX, LY),
            (RX, LY), (2, RX, LY), (NSPEC, NZ, LY), (NSPEC, NZ, LY),
        ]
        shared = pl.pallas_call(
            lambda *refs: flow_kernel(sizes, *refs),
            out_shape=[pltpu.VMEM(shape, F32) for shape in middle],
            in_specs=[hbm] * 6,
            out_specs=[vmem] * len(middle),
            scratch_shapes=[
                pltpu.VMEM(tile, F32), pltpu.VMEM(tile, jnp.int32), pltpu.VMEM(tile, jnp.int32),
                pltpu.VMEM((NZ + 2, EX, LY), F32), pltpu.VMEM((NZ + 2, EX, LY), F32),
                pltpu.VMEM(wide, F32), pltpu.VMEM(wide, F32), pltpu.VMEM(wide, F32),
                pltpu.VMEM((2, FIELDS, NZ, 4, LY), F32), pltpu.VMEM((2, 3, RX, LY), F32),
                pltpu.VMEM((4, 3, 4, LY), F32), pltpu.VMEM((2, NSPEC, NZ, LY), F32),
                pltpu.VMEM((2, RX, LY), F32),
                pltpu.VMEM((2, FIELDS, NZ, 4, LY), F32), pltpu.VMEM((2, 3, RX, LY), F32),
                pltpu.VMEM((4, 3, 4, LY), F32), pltpu.VMEM((2, NSPEC, NZ, LY), F32),
                pltpu.VMEM((2, RX, LY), F32),
                pltpu.SemaphoreType.DMA((7,)), pltpu.SemaphoreType.DMA((8,)),
                pltpu.SemaphoreType.DMA((8,)), pltpu.SemaphoreType.DMA((4,)),
                pltpu.SemaphoreType.DMA((4,)),
            ],
            compiler_params=pltpu.CompilerParams(
                collective_id=0, has_side_effects=True, vmem_limit_bytes=32 * 2**20),
            name="flow",
        )(*args)
        return tuple(pl.pallas_call(
            transport_kernel,
            out_shape=[jax.ShapeDtypeStruct(s, F32) for s in (species, tile, tile)],
            in_specs=[vmem] * len(middle),
            out_specs=[hbm] * 3,
            scratch_shapes=[pltpu.VMEM(species, F32), pltpu.SemaphoreType.DMA((6,))],
            compiler_params=pltpu.CompilerParams(vmem_limit_bytes=16 * 2**20),
            name="transport",
        )(*shared))

    return shards


def solution(mesh):
    specs = (P(None, None, "gx", "gy"),) + (P(None, "gx", "gy"),) * 5
    outs = (P(None, None, "gx", "gy"), P(None, "gx", "gy"), P(None, "gx", "gy"))
    sizes = (mesh.shape["gx"], mesh.shape["gy"])
    return jax.shard_map(build(sizes), mesh=mesh, in_specs=specs, out_specs=outs, check_vma=False)
```

```python
import math

import jax
import jax.numpy as jnp
from jax import lax
from jax.experimental import pallas as pl
from jax.experimental.pallas import tpu as pltpu
from jax.sharding import PartitionSpec as P

SWEEPS = 3
NSPEC, NZ, RX, LY = 8, 16, 16, 128
EX = RX + 8
FIELDS = 5
TINY = 1e-30

ZONE_RATES = (0.02, 0.05, 0.1, 0.2)
ZONE_PERMEABILITY = (5.0, 10.0, 20.0, 40.0)
SOLUBILITY = 0.5
MOLAR_VOLUME = 0.05
STORAGE_COEF = 0.2
TIME_STEP = 0.2
CHEB_SPREAD = 0.92
STOICHIOMETRY = (-1.0, -1.0, 0.0, 0.0, 0.0, 0.0, 0.0, 0.0)

F32 = jnp.float32
MESH = pl.DeviceIdType.MESH
DIRS = ((-1, 0), (1, 0), (0, -1), (0, 1), (-1, -1), (1, -1), (-1, 1), (1, 1))
OPPOSITE = tuple(DIRS.index((-a, -b)) for a, b in DIRS)


def relax_weight(iteration):
    return 1.0 / (1.0 + CHEB_SPREAD * math.cos(math.pi * (2 * iteration + 1) / (2 * SWEEPS)))


def lookup(labels, table):
    out = jnp.where(labels == 0, F32(table[0]), F32(table[1]))
    out = jnp.where(labels == 2, F32(table[2]), out)
    return jnp.where(labels == 3, F32(table[3]), out)


def inverse(x):
    guess = pl.reciprocal(x, approx=True)
    guess = guess * (2.0 - x * guess)
    return guess * (2.0 - x * guess)


def harmonic(a, b):
    return (2.0 * a * b) * inverse(jnp.maximum(a + b, TINY))


def lanes(x, shift):
    return pltpu.roll(x, shift % LY if isinstance(shift, int) else lax.rem(shift + 2 * LY, LY), 1)


def before(x):
    return pltpu.roll(x, 1, 0)


def after(x):
    return pltpu.roll(x, x.shape[0] - 1, 0)


def iota(rows, dim):
    return lax.broadcasted_iota(jnp.int32, (rows, LY), dim)


def flow_kernel(sizes, sp_in, por_in, old_in, src_in, zone_in, fix_in,
                sp, phi, rea, pb, tx, tyl, tyr, tz, edge, side, row_lo, row_hi,
                por, zone, fix, pa, perm, stor, rhs, gain,
                sx, sy, sc, ssx, ssy, rx, ry, rc, rsx, rsy,
                in_sem, send_sem, recv_sem, s_send, s_recv, ready):
    gx, gy = lax.axis_index("gx"), lax.axis_index("gy")
    spots = []
    for dx, dy in DIRS:
        there = None
        for here, step, size in ((gx, dx, sizes[0]), (gy, dy, sizes[1])):
            if step:
                ok = here > 0 if step < 0 else here < size - 1
                there = ok if there is None else there & ok
        spots.append(((gx + dx, gy + dy), there))

    seam = sizes[1] // 2
    split = jnp.bool_(sizes[1] >= 4)
    at_lo, at_hi = (gy == seam - 1) & split, (gy == seam) & split
    at_seam = at_lo | at_hi
    barrier = pltpu.get_barrier_semaphore()
    expected = 0
    for i, (where, there) in enumerate(spots):
        far = (at_lo & (DIRS[i][1] > 0)) | (at_hi & (DIRS[i][1] < 0))
        counts = split & ((where[1] == seam - 1) | (where[1] == seam))
        beside = there & (far | jnp.logical_not(counts))

        @pl.when(beside)
        def _():
            pl.semaphore_signal(barrier, inc=1, device_id=where, device_id_type=MESH)
        expected = expected + (there & (far | jnp.logical_not(at_seam))).astype(jnp.int32)

    loads = [
        pltpu.make_async_copy(sp_in.at[pl.ds(0, 2)], sp.at[pl.ds(0, 2)], in_sem.at[0]),
        pltpu.make_async_copy(por_in, por, in_sem.at[1]),
        pltpu.make_async_copy(zone_in, zone, in_sem.at[2]),
        pltpu.make_async_copy(old_in, pa.at[pl.ds(1, NZ), pl.ds(0, RX)], in_sem.at[3]),
        pltpu.make_async_copy(src_in, rhs.at[:, pl.ds(0, RX)], in_sem.at[4]),
        pltpu.make_async_copy(fix_in, fix, in_sem.at[5]),
        pltpu.make_async_copy(sp_in.at[pl.ds(2, NSPEC - 2)], sp.at[pl.ds(2, NSPEC - 2)], in_sem.at[6]),
    ]
    for c in loads:
        c.start()

    for i in range(8):
        @pl.when(jnp.logical_not(spots[i][1]))
        def _():
            if i < 2:
                rx[i] = jnp.zeros(rx.shape[1:], F32)
                rsx[i] = jnp.zeros(rsx.shape[1:], F32)
            elif i < 4:
                ry[i - 2] = jnp.zeros(ry.shape[1:], F32)
                rsy[i - 2] = jnp.zeros(rsy.shape[1:], F32)
            else:
                rc[i - 4] = jnp.zeros(rc.shape[1:], F32)
    plane = jnp.zeros((EX, LY), F32)
    for ref in (perm, pa, pb):
        ref[0] = plane
        ref[NZ + 1] = plane

    lane = iota(RX, 1)
    group = lax.shift_right_logical(lane, 3)
    low = (lane & 7) < 4
    for c in loads[:6]:
        c.wait()

    def own(z, packs):
        c0, c1 = sp[0, z], sp[1, z]
        label = zone[z]
        reaction = lookup(label, ZONE_RATES) * (c0 * c1 - SOLUBILITY)
        new = por[z] - MOLAR_VOLUME * reaction
        solid = 1.0 - new
        k = lookup(label, ZONE_PERMEABILITY) * (new * new * new) * inverse(solid * solid)
        s = STORAGE_COEF * new
        free = 1.0 - fix[z].astype(F32)
        p, q = pa[z + 1, :RX], rhs[z, :RX]
        rea[z] = reaction
        phi[z] = new
        perm[z + 1, :RX] = k
        stor[z, :RX] = s
        gain[z, :RX] = free
        out = []
        for f, (v, pack) in enumerate(zip((k, p, s, q, free), packs)):
            sx[0, f, z] = v[:4]
            sx[1, f, z] = v[12:]
            out.append(jnp.where(group == z, lanes(v, 8 * z + 4), pack))
        return tuple(out)

    zero = jnp.zeros((RX, LY), F32)
    packs = lax.fori_loop(0, NZ, own, (zero,) * FIELDS, unroll=8)
    for j in range(3):
        a, b = packs[2 * j], packs[2 * j + 1] if j < 2 else zero
        down = jnp.where(low, lanes(a, -4), b)
        up = jnp.where(low, a, lanes(b, 4))
        sy[0, j] = down
        sy[1, j] = up
        sc[0, j], sc[1, j] = down[:4], down[12:]
        sc[2, j], sc[3, j] = up[:4], up[12:]

    def parts(i):
        if i < 2:
            return sx.at[i], rx, i
        if i < 4:
            return sy.at[i - 2], ry, i - 2
        return sc.at[i - 4], rc, i - 4

    def copy(i):
        src, _, _ = parts(i)
        _, dst, at = parts(OPPOSITE[i])
        return pltpu.make_async_remote_copy(
            src_ref=src, dst_ref=dst.at[at], send_sem=send_sem.at[i],
            recv_sem=recv_sem.at[OPPOSITE[i]], device_id=spots[i][0], device_id_type=MESH)

    def arrival(i):
        src, dst, at = parts(i)
        return pltpu.make_async_remote_copy(
            src_ref=src, dst_ref=dst.at[at], send_sem=send_sem.at[i],
            recv_sem=recv_sem.at[i], device_id=spots[i][0], device_id_type=MESH)

    def sparts(i):
        return (ssx.at[i], rsx, i) if i < 2 else (ssy.at[i - 2], rsy, i - 2)

    def scopy(i):
        src, _, _ = sparts(i)
        _, dst, at = sparts(OPPOSITE[i])
        return pltpu.make_async_remote_copy(
            src_ref=src, dst_ref=dst.at[at], send_sem=s_send.at[i],
            recv_sem=s_recv.at[OPPOSITE[i]], device_id=spots[i][0], device_id_type=MESH)

    def sarrival(i):
        src, dst, at = sparts(i)
        return pltpu.make_async_remote_copy(
            src_ref=src, dst_ref=dst.at[at], send_sem=s_send.at[i],
            recv_sem=s_recv.at[i], device_id=spots[i][0], device_id_type=MESH)

    def send(only, order, make):
        for i in order:
            @pl.when(spots[i][1] & only)
            def _():
                make(i).start()

    inner = jnp.logical_not(at_seam)

    @pl.when(at_hi)
    def _():
        pl.semaphore_wait(barrier, expected)
    send(at_hi, (2, 4, 5), copy)

    @pl.when(inner)
    def _():
        pl.semaphore_wait(barrier, expected)
    for edge_row, step in ((seam - 2, 1), (seam + 1, -1)):
        @pl.when((gy == edge_row) & split)
        def _():
            pl.semaphore_signal(ready, inc=1, device_id=(gx, gy + step), device_id_type=MESH)

    @pl.when(at_seam)
    def _():
        pl.semaphore_wait(ready, 1)
    send(inner | at_lo, (2, 4, 5), copy)
    send(inner | at_hi, (3, 6, 7), copy)
    send(True, (0, 1), copy)

    loads[6].wait()
    for s in range(NSPEC):
        for z in range(NZ):
            ssx[0, s, pl.ds(z, 1)] = sp[s, z, pl.ds(0, 1)]
            ssx[1, s, pl.ds(z, 1)] = sp[s, z, pl.ds(RX - 1, 1)]
    pair = lax.shift_right_logical(lane, 1)
    odd = (lane & 1) == 1

    def species_edge(z, packs):
        lo, hi = packs
        for s in range(NSPEC):
            m = lax.rem(z, 8) * 8 + s
            turned = lanes(sp[s, z], 2 * m + 1)
            lo = jnp.where((pair == m) & (z < 8), turned, lo)
            hi = jnp.where((pair == m) & (z >= 8), turned, hi)
        return lo, hi

    lo, hi = lax.fori_loop(0, NZ, species_edge, (zero, zero), unroll=2)
    ssy[0] = jnp.where(odd, lo, lanes(hi, -1))
    ssy[1] = jnp.where(odd, lanes(hi, 1), lo)
    send(True, (2, 0, 1), scopy)
    send(inner | at_hi, (3,), scopy)

    @pl.when(at_lo)
    def _():
        pl.semaphore_wait(barrier, expected)
    send(at_lo, (3, 6, 7), copy)
    send(at_lo, (3,), scopy)

    for i in range(8):
        @pl.when(spots[i][1])
        def _():
            arrival(i).wait_recv()

    lane8, lane24 = iota(8, 1), iota(EX, 1)
    group8 = lax.shift_right_logical(lane8, 3)
    low24 = (lane24 & 7) < 4

    def rows(z, packs):
        out = []
        for f, pack in enumerate(packs):
            tail = jnp.concatenate([rx[1, f, z], rx[0, f, z]], axis=0)
            if f == 0:
                perm[z + 1, RX:] = tail
            elif f == 1:
                pa[z + 1, RX:] = tail
            else:
                (stor, rhs, gain)[f - 2][z, RX:] = tail
            out.append(jnp.where(group8 == z, lanes(tail, 8 * z + 4), pack))
        return tuple(out)

    tails = lax.fori_loop(0, NZ, rows, (jnp.zeros((8, LY), F32),) * FIELDS, unroll=8)
    whole = [jnp.concatenate([a, b], axis=0) for a, b in zip(packs, tails)]

    strips = []
    for d in range(2):
        fields = []
        for f in range(FIELDS):
            j = f // 2
            halo = jnp.concatenate([ry[d, j], rc[2 * d + 1, j], rc[2 * d, j]], axis=0)
            if d == 0:
                fields.append(jnp.where(low24, halo if f % 2 == 0 else lanes(halo, -4), whole[f]))
            else:
                fields.append(jnp.where(low24, whole[f], lanes(halo, 4) if f % 2 == 0 else halo))
        k, p, s, q, free = fields
        fx_t = harmonic(k, before(k))
        fy_t = harmonic(k, lanes(k, 1))
        fz_t = jnp.where(lane24 < 8, 0.0, harmonic(k, lanes(k, 8)))
        total = s + fx_t + after(fx_t) + fy_t + lanes(fy_t, -1) + fz_t + lanes(fz_t, -8)
        g = free * inverse(jnp.maximum(total, TINY))
        right = s * p + q
        history = [p]
        for it in range(SWEEPS):
            fx = fx_t * (p - before(p))
            fy = fy_t * (p - lanes(p, 1))
            fz = fz_t * (p - lanes(p, 8))
            r = right - s * p - fx + after(fx) - fy + lanes(fy, -1) - fz + lanes(fz, -8)
            p = p + F32(relax_weight(it)) * g * r
            history.append(p)
        strips.append((fy_t, history))
    column = lane24 & 7
    faces = jnp.where(column == 4, strips[0][0], lanes(strips[1][0], -1))
    edges = [jnp.where(column == 3, a, lanes(b, -2)) for a, b in zip(strips[0][1], strips[1][1])]
    edge[...] = edges[SWEEPS][:RX]

    first, last = lane24 == 0, lane24 == LY - 1

    def coefficients(z, tz_lo):
        k = perm[z + 1]
        tz_hi = harmonic(k, perm[z + 2])
        turned = lanes(faces, -(8 * z + 4))
        t_x = harmonic(k, before(k))
        t_lo = jnp.where(first, turned, harmonic(k, lanes(k, 1)))
        t_hi = jnp.where(last, turned, lanes(t_lo, -1))
        s = stor[z]
        total = s + t_x + after(t_x) + t_lo + t_hi + tz_lo + tz_hi
        tx[z], tyl[z], tyr[z], tz[z] = t_x, t_lo, t_hi, tz_lo
        gain[z] = gain[z] * inverse(jnp.maximum(total, TINY))
        rhs[z] = s * pa[z + 1] + rhs[z]
        return tz_hi

    tz[NZ] = lax.fori_loop(0, NZ, coefficients, plane, unroll=NZ)

    for it in range(SWEEPS):
        src, dst = (pa, pb) if it % 2 == 0 else (pb, pa)

        def sweep(z, flow_lo):
            p = src[z + 1]
            turned = lanes(edges[it], -(8 * z + 3))
            fx = tx[z] * (p - before(p))
            f_lo = tyl[z] * (p - jnp.where(first, turned, lanes(p, 1)))
            f_hi = tyr[z] * (jnp.where(last, turned, lanes(p, -1)) - p)
            flow_hi = tz[z + 1] * (src[z + 2] - p)
            r = rhs[z] - stor[z] * p - fx + after(fx) - f_lo + f_hi - flow_lo + flow_hi
            dst[z + 1] = p + F32(relax_weight(it)) * gain[z] * r
            return flow_hi

        lax.fori_loop(0, NZ, sweep, plane, unroll=NZ)

    for i in range(4):
        @pl.when(spots[i][1])
        def _():
            sarrival(i).wait_recv()
    m_lo, m_hi = rsy[0], rsy[1]
    side[0] = jnp.where(odd, lanes(m_lo, 1), lanes(m_hi, -1))
    side[1] = jnp.where(odd, m_lo, m_hi)
    row_lo[...] = rsx[0]
    row_hi[...] = rsx[1]
    for i in range(8):
        @pl.when(spots[i][1])
        def _():
            copy(i).wait_send()
            if i < 4:
                scopy(i).wait_send()


def transport_kernel(sp, phi, rea, p_ref, tx, tyl, tyr, tz, edge, side, row_lo, row_hi,
                     conc_out, p_out, phi_out, conc, sem):
    outs = [
        pltpu.make_async_copy(p_ref.at[pl.ds(1, NZ), pl.ds(0, RX)], p_out, sem.at[0]),
        pltpu.make_async_copy(phi, phi_out, sem.at[1]),
    ]
    for c in outs:
        c.start()
    lane, row = iota(RX, 1), iota(RX, 0)
    first, last = lane == 0, lane == LY - 1
    top, bottom = row == 0, row == RX - 1

    def body(z, carry):
        wide = p_ref[z + 1]
        p = wide[:RX]
        turned = lanes(edge[...], -(8 * z + 3))
        t_x = tx[z]
        flows = [
            t_x[:RX] * (p - before(wide)[:RX]),
            after(t_x)[:RX] * (p - after(wide)[:RX]),
            tyl[z, :RX] * (p - jnp.where(first, turned, lanes(p, 1))),
            tyr[z, :RX] * (p - jnp.where(last, turned, lanes(p, -1))),
            tz[z, :RX] * (p - p_ref[z, :RX]),
            tz[z + 1, :RX] * (p - p_ref[z + 2, :RX]),
        ]
        scale = TIME_STEP * inverse(phi[z])
        out = jnp.maximum(flows[0], 0.0)
        for f in flows[1:]:
            out = out + jnp.maximum(f, 0.0)
        keep = 1.0 - scale * out
        take = [-scale * jnp.minimum(f, 0.0) for f in flows]
        reaction = rea[z]
        z_lo, z_hi = jnp.maximum(z - 1, 0), jnp.minimum(z + 1, NZ - 1)
        half = side[lax.div(z, 8)]
        for s in range(NSPEC):
            c = sp[s, z]
            turned_c = lanes(half, -(2 * (lax.rem(z, 8) * 8 + s) + 1))
            total = c * keep
            total = total + take[0] * jnp.where(top, row_lo[s, pl.ds(z, 1)], before(c))
            total = total + take[1] * jnp.where(bottom, row_hi[s, pl.ds(z, 1)], after(c))
            total = total + take[2] * jnp.where(first, turned_c, lanes(c, 1))
            total = total + take[3] * jnp.where(last, turned_c, lanes(c, -1))
            total = total + take[4] * sp[s, z_lo]
            total = total + take[5] * sp[s, z_hi]
            if STOICHIOMETRY[s]:
                total = total + STOICHIOMETRY[s] * reaction
            conc[s, z] = total
        return carry

    for part in range(4):
        lax.fori_loop(4 * part, 4 * part + 4, body, 0, unroll=4)
        at = pl.ds(4 * part, 4)
        c = pltpu.make_async_copy(conc.at[:, at], conc_out.at[:, at], sem.at[2 + part])
        c.start()
        outs.append(c)
    for c in outs:
        c.wait()


def build(sizes):
    tile = (NZ, RX, LY)
    wide = (NZ, EX, LY)
    species = (NSPEC, NZ, RX, LY)
    vmem = pl.BlockSpec(memory_space=pltpu.VMEM)
    hbm = pl.BlockSpec(memory_space=pltpu.HBM)

    def shards(*args):
        args = [pltpu.with_memory_space_constraint(a, pltpu.HBM) for a in args]
        middle = [
            species, tile, tile, (NZ + 2, EX, LY), wide, wide, wide, (NZ + 1, EX, LY),
            (RX, LY), (2, RX, LY), (NSPEC, NZ, LY), (NSPEC, NZ, LY),
        ]
        shared = pl.pallas_call(
            lambda *refs: flow_kernel(sizes, *refs),
            out_shape=[pltpu.VMEM(shape, F32) for shape in middle],
            in_specs=[hbm] * 6,
            out_specs=[vmem] * len(middle),
            scratch_shapes=[
                pltpu.VMEM(tile, F32), pltpu.VMEM(tile, jnp.int32), pltpu.VMEM(tile, jnp.int32),
                pltpu.VMEM((NZ + 2, EX, LY), F32), pltpu.VMEM((NZ + 2, EX, LY), F32),
                pltpu.VMEM(wide, F32), pltpu.VMEM(wide, F32), pltpu.VMEM(wide, F32),
                pltpu.VMEM((2, FIELDS, NZ, 4, LY), F32), pltpu.VMEM((2, 3, RX, LY), F32),
                pltpu.VMEM((4, 3, 4, LY), F32), pltpu.VMEM((2, NSPEC, NZ, LY), F32),
                pltpu.VMEM((2, RX, LY), F32),
                pltpu.VMEM((2, FIELDS, NZ, 4, LY), F32), pltpu.VMEM((2, 3, RX, LY), F32),
                pltpu.VMEM((4, 3, 4, LY), F32), pltpu.VMEM((2, NSPEC, NZ, LY), F32),
                pltpu.VMEM((2, RX, LY), F32),
                pltpu.SemaphoreType.DMA((7,)), pltpu.SemaphoreType.DMA((8,)),
                pltpu.SemaphoreType.DMA((8,)), pltpu.SemaphoreType.DMA((4,)),
                pltpu.SemaphoreType.DMA((4,)), pltpu.SemaphoreType.REGULAR,
            ],
            compiler_params=pltpu.CompilerParams(
                collective_id=0, has_side_effects=True, vmem_limit_bytes=32 * 2**20),
            name="flow",
        )(*args)
        return tuple(pl.pallas_call(
            transport_kernel,
            out_shape=[jax.ShapeDtypeStruct(s, F32) for s in (species, tile, tile)],
            in_specs=[vmem] * len(middle),
            out_specs=[hbm] * 3,
            scratch_shapes=[pltpu.VMEM(species, F32), pltpu.SemaphoreType.DMA((6,))],
            compiler_params=pltpu.CompilerParams(vmem_limit_bytes=16 * 2**20),
            name="transport",
        )(*shared))

    return shards


def solution(mesh):
    specs = (P(None, None, "gx", "gy"),) + (P(None, "gx", "gy"),) * 5
    outs = (P(None, None, "gx", "gy"), P(None, "gx", "gy"), P(None, "gx", "gy"))
    sizes = (mesh.shape["gx"], mesh.shape["gy"])
    return jax.shard_map(build(sizes), mesh=mesh, in_specs=specs, out_specs=outs, check_vma=False)
```

```python
import math

import jax
import jax.numpy as jnp
from jax import lax
from jax.experimental import pallas as pl
from jax.experimental.pallas import tpu as pltpu
from jax.sharding import PartitionSpec as P

SWEEPS = 3
NSPEC, NZ, RX, LY = 8, 16, 16, 128
EX = RX + 8
FIELDS = 5
TINY = 1e-30
PLANES = [(f, d) for f in range(FIELDS) for d in range(4 if f < 2 else 3)]

ZONE_RATES = (0.02, 0.05, 0.1, 0.2)
ZONE_PERMEABILITY = (5.0, 10.0, 20.0, 40.0)
SOLUBILITY = 0.5
MOLAR_VOLUME = 0.05
STORAGE_COEF = 0.2
TIME_STEP = 0.2
CHEB_SPREAD = 0.92
STOICHIOMETRY = (-1.0, -1.0, 0.0, 0.0, 0.0, 0.0, 0.0, 0.0)

F32 = jnp.float32
MESH = pl.DeviceIdType.MESH
DIRS = ((-1, 0), (1, 0), (0, -1), (0, 1), (-1, -1), (1, -1), (-1, 1), (1, 1))
OPPOSITE = tuple(DIRS.index((-a, -b)) for a, b in DIRS)


def relax_weight(iteration):
    return 1.0 / (1.0 + CHEB_SPREAD * math.cos(math.pi * (2 * iteration + 1) / (2 * SWEEPS)))


def lookup(labels, table):
    out = jnp.where(labels == 0, F32(table[0]), F32(table[1]))
    out = jnp.where(labels == 2, F32(table[2]), out)
    return jnp.where(labels == 3, F32(table[3]), out)


def inverse(x):
    guess = pl.reciprocal(x, approx=True)
    guess = guess * (2.0 - x * guess)
    return guess * (2.0 - x * guess)


def harmonic(a, b):
    return (2.0 * a * b) * inverse(jnp.maximum(a + b, TINY))


def lanes(x, shift):
    return pltpu.roll(x, shift % LY if isinstance(shift, int) else lax.rem(shift + 2 * LY, LY), 1)


def before(x):
    return pltpu.roll(x, 1, 0)


def after(x):
    return pltpu.roll(x, x.shape[0] - 1, 0)


def iota(rows, dim):
    return lax.broadcasted_iota(jnp.int32, (rows, LY), dim)


def flow_kernel(sizes, sp_in, por_in, old_in, src_in, zone_in, fix_in,
                sp, phi, rea, pb, tx, ty, tz, face, edge, side, row_lo, row_hi,
                por, zone, fix, old, src, pa, perm, stor, rhs, gain,
                sx, sy, sc, ssx, ssy, rx, ry, rc, rsx, rsy,
                in_sem, send_sem, recv_sem, s_send, s_recv, ready):
    gx, gy = lax.axis_index("gx"), lax.axis_index("gy")
    spots = []
    for dx, dy in DIRS:
        there = None
        for here, step, size in ((gx, dx, sizes[0]), (gy, dy, sizes[1])):
            if step:
                ok = here > 0 if step < 0 else here < size - 1
                there = ok if there is None else there & ok
        spots.append(((gx + dx, gy + dy), there))

    seam = sizes[1] // 2
    split = jnp.bool_(sizes[1] >= 4)
    at_lo, at_hi = (gy == seam - 1) & split, (gy == seam) & split
    at_seam = at_lo | at_hi
    barrier = pltpu.get_barrier_semaphore()
    expected = 0
    for i, (where, there) in enumerate(spots):
        far = (at_lo & (DIRS[i][1] > 0)) | (at_hi & (DIRS[i][1] < 0))
        counts = split & ((where[1] == seam - 1) | (where[1] == seam))
        beside = there & (far | jnp.logical_not(counts))

        @pl.when(beside)
        def _():
            pl.semaphore_signal(barrier, inc=1, device_id=where, device_id_type=MESH)
        expected = expected + (there & (far | jnp.logical_not(at_seam))).astype(jnp.int32)

    loads = [
        pltpu.make_async_copy(sp_in.at[pl.ds(0, 2)], sp.at[pl.ds(0, 2)], in_sem.at[0]),
        pltpu.make_async_copy(zone_in, zone, in_sem.at[1]),
        pltpu.make_async_copy(por_in, por, in_sem.at[2]),
        pltpu.make_async_copy(old_in, old, in_sem.at[3]),
        pltpu.make_async_copy(src_in, src, in_sem.at[4]),
        pltpu.make_async_copy(fix_in, fix, in_sem.at[5]),
        pltpu.make_async_copy(sp_in.at[pl.ds(2, NSPEC - 2)], sp.at[pl.ds(2, NSPEC - 2)], in_sem.at[6]),
    ]
    for c in loads:
        c.start()

    for i in range(8):
        @pl.when(jnp.logical_not(spots[i][1]))
        def _():
            if i < 2:
                rx[i] = jnp.zeros(rx.shape[1:], F32)
                rsx[i] = jnp.zeros(rsx.shape[1:], F32)
            elif i < 4:
                ry[i - 2] = jnp.zeros(ry.shape[1:], F32)
                rsy[i - 2] = jnp.zeros(rsy.shape[1:], F32)
            else:
                rc[i - 4] = jnp.zeros(rc.shape[1:], F32)
    plane = jnp.zeros((EX, LY), F32)
    for ref in (perm, pa, pb):
        ref[pl.ds(0, EX)] = plane
        ref[pl.ds((NZ + 1) * EX, EX)] = plane
    for ref in (stor, rhs, gain):
        for z in range(NZ):
            ref[pl.ds(z * EX + RX, 8)] = plane[:8]

    lane = iota(RX, 1)
    group = lax.shift_right_logical(lane, 3)
    low = (lane & 7) < 4
    for c in loads[:6]:
        c.wait()

    def at(z, rows=EX, skip=0):
        return pl.ds(pl.multiple_of(z * EX + skip, 8), rows)

    def own(z, packs):
        rows = pl.ds(pl.multiple_of(z * RX, 8), RX)
        c0, c1 = sp[0, rows], sp[1, rows]
        label = zone[z]
        reaction = lookup(label, ZONE_RATES) * (c0 * c1 - SOLUBILITY)
        new = por[z] - MOLAR_VOLUME * reaction
        solid = 1.0 - new
        k = lookup(label, ZONE_PERMEABILITY) * (new * new * new) * inverse(solid * solid)
        s = STORAGE_COEF * new
        free = 1.0 - fix[z].astype(F32)
        p, q = old[z], src[z]
        rea[z] = reaction
        phi[z] = new
        perm[at(z + 1, RX)] = k
        pa[at(z + 1, RX)] = p
        stor[at(z, RX)] = s
        rhs[at(z, RX)] = q
        gain[at(z, RX)] = free
        return tuple(jnp.where(group == z, lanes(v, 8 * z + 4), pack) for v, pack in zip((k, p, s, q, free), packs))

    zero = jnp.zeros((RX, LY), F32)
    packs = lax.fori_loop(0, NZ, own, (zero,) * FIELDS, unroll=NZ)
    k, p, s, q, free = packs
    low8 = low[:8]
    for side_y in range(2):
        if side_y == 0:
            a, b = jnp.where(low, lanes(k, -4), p), jnp.where(low, lanes(s, -4), q)
            m = jnp.where(low8, lanes(free[:8], -4), free[8:])
        else:
            a, b = jnp.where(low, k, lanes(p, 4)), jnp.where(low, s, lanes(q, 4))
            m = jnp.where(low8, free[:8], lanes(free[8:], 4))
        sy[side_y, pl.ds(0, RX)] = a
        sy[side_y, pl.ds(RX, RX)] = b
        sy[side_y, pl.ds(2 * RX, 8)] = m
        for side_x in range(2):
            j = 2 * side_y + side_x
            if side_x == 0:
                parts_c = (a[:3], b[:2], free[:2])
            else:
                parts_c = (a[RX - 3:], b[RX - 2:], free[RX - 2:])
            sc[j, pl.ds(0, 3)] = parts_c[0]
            sc[j, pl.ds(3, 2)] = parts_c[1]
            sc[j, pl.ds(5, 2)] = parts_c[2]
            sc[j, pl.ds(7, 1)] = parts_c[2][:1]

    def strided(ref, z0, row):
        return ref.at[pl.ds(z0 * EX + row, NZ, stride=EX)]

    fields = ((perm, 1), (pa, 1), (stor, 0), (rhs, 0), (gain, 0))
    for n, (f, d) in enumerate(PLANES):
        ref, z0 = fields[f]
        sx[0, n] = strided(ref, z0, d)[...]
        sx[1, n] = strided(ref, z0, RX - 1 - d)[...]

    def parts(i):
        if i < 2:
            return sx.at[i], rx, i
        if i < 4:
            return sy.at[i - 2], ry, i - 2
        return sc.at[i - 4], rc, i - 4

    def copy(i):
        from_ref, _, _ = parts(i)
        _, dst, slot = parts(OPPOSITE[i])
        return pltpu.make_async_remote_copy(
            src_ref=from_ref, dst_ref=dst.at[slot], send_sem=send_sem.at[i],
            recv_sem=recv_sem.at[OPPOSITE[i]], device_id=spots[i][0], device_id_type=MESH)

    def arrival(i):
        from_ref, dst, slot = parts(i)
        return pltpu.make_async_remote_copy(
            src_ref=from_ref, dst_ref=dst.at[slot], send_sem=send_sem.at[i],
            recv_sem=recv_sem.at[i], device_id=spots[i][0], device_id_type=MESH)

    def sparts(i):
        return (ssx.at[i], rsx, i) if i < 2 else (ssy.at[i - 2], rsy, i - 2)

    def scopy(i):
        from_ref, _, _ = sparts(i)
        _, dst, slot = sparts(OPPOSITE[i])
        return pltpu.make_async_remote_copy(
            src_ref=from_ref, dst_ref=dst.at[slot], send_sem=s_send.at[i],
            recv_sem=s_recv.at[OPPOSITE[i]], device_id=spots[i][0], device_id_type=MESH)

    def sarrival(i):
        from_ref, dst, slot = sparts(i)
        return pltpu.make_async_remote_copy(
            src_ref=from_ref, dst_ref=dst.at[slot], send_sem=s_send.at[i],
            recv_sem=s_recv.at[i], device_id=spots[i][0], device_id_type=MESH)

    def send(only, order, make):
        for i in order:
            @pl.when(spots[i][1] & only)
            def _():
                make(i).start()

    inner = jnp.logical_not(at_seam)

    @pl.when(at_hi)
    def _():
        pl.semaphore_wait(barrier, expected)
    send(at_hi, (2, 4, 5), copy)

    @pl.when(inner)
    def _():
        pl.semaphore_wait(barrier, expected)
    for edge_row, step in ((seam - 2, 1), (seam + 1, -1)):
        @pl.when((gy == edge_row) & split)
        def _():
            pl.semaphore_signal(ready, inc=1, device_id=(gx, gy + step), device_id_type=MESH)

    @pl.when(at_seam)
    def _():
        pl.semaphore_wait(ready, 1)
    send(True, (0, 1), copy)
    send(inner | at_lo, (2, 4, 5), copy)
    send(inner | at_hi, (3, 6, 7), copy)

    loads[6].wait()
    for s in range(NSPEC):
        ssx[0, s] = sp[s, pl.ds(0, NZ, stride=RX)]
        ssx[1, s] = sp[s, pl.ds(RX - 1, NZ, stride=RX)]
    pair = lax.shift_right_logical(lane, 1)
    odd = (lane & 1) == 1

    def species_edge(z, packs):
        lo, hi = packs
        for s in range(NSPEC):
            m = lax.rem(z, 8) * 8 + s
            turned = lanes(sp[s, pl.ds(pl.multiple_of(z * RX, 8), RX)], 2 * m + 1)
            lo = jnp.where((pair == m) & (z < 8), turned, lo)
            hi = jnp.where((pair == m) & (z >= 8), turned, hi)
        return lo, hi

    lo, hi = lax.fori_loop(0, NZ, species_edge, (zero, zero), unroll=2)
    ssy[0] = jnp.where(odd, lo, lanes(hi, -1))
    ssy[1] = jnp.where(odd, lanes(hi, 1), lo)
    send(True, (2, 0, 1), scopy)
    send(inner | at_hi, (3,), scopy)

    @pl.when(at_lo)
    def _():
        pl.semaphore_wait(barrier, expected)
    send(at_lo, (3, 6, 7), copy)
    send(at_lo, (3,), scopy)

    for i in range(2):
        @pl.when(spots[i][1])
        def _():
            arrival(i).wait_recv()
    for n, (f, d) in enumerate(PLANES):
        ref, z0 = fields[f]
        strided(ref, z0, RX + d)[...] = rx[1, n]
        strided(ref, z0, EX - 1 - d)[...] = rx[0, n]
    lane8, lane24 = iota(8, 1), iota(EX, 1)
    group8 = lax.shift_right_logical(lane8, 3)

    def rows(z, packs):
        return tuple(
            jnp.where(group8 == z, lanes(ref[at(z + z0, 8, RX)], 8 * z + 4), pack)
            for (ref, z0), pack in zip(fields, packs))

    tails = lax.fori_loop(0, NZ, rows, (jnp.zeros((8, LY), F32),) * FIELDS, unroll=8)
    whole = [jnp.concatenate([a, b], axis=0) for a, b in zip(packs, tails)]

    def feed(z, v, pack):
        spot = (lane24 - 8 * z) & (LY - 1)
        return jnp.where((spot == 8) | (spot == LY - 1), lanes(v, 8 * z + 4), pack)

    inside = lane24 > 0

    def coefficients(z, carry):
        tz_lo, pack = carry
        k = perm[at(z + 1)]
        tz_hi = harmonic(k, perm[at(z + 2)])
        t_x = harmonic(k, before(k))
        t_y = jnp.where(inside, harmonic(k, lanes(k, 1)), 0.0)
        s = stor[at(z)]
        total = s + t_x + after(t_x) + t_y + lanes(t_y, -1) + tz_lo + tz_hi
        tx[z], ty[z], tz[z] = t_x, t_y, tz_lo
        gain[at(z)] = gain[at(z)] * inverse(jnp.maximum(total, TINY))
        rhs[at(z)] = s * pa[at(z + 1)] + rhs[at(z)]
        return tz_hi, feed(z, k, pack)

    tz[NZ], fed_k = lax.fori_loop(0, NZ, coefficients, (plane, plane), unroll=NZ)

    fed = []
    for it in range(SWEEPS):
        now, new = (pa, pb) if it % 2 == 0 else (pb, pa)

        def sweep(z, carry):
            flow_lo, pack = carry
            p = now[at(z + 1)]
            fx = tx[z] * (p - before(p))
            fy = ty[z] * (p - lanes(p, 1))
            flow_hi = tz[z + 1] * (now[at(z + 2)] - p)
            r = rhs[at(z)] - stor[at(z)] * p - fx + after(fx) - fy + lanes(fy, -1) - flow_lo + flow_hi
            new[at(z + 1)] = p + F32(relax_weight(it)) * gain[at(z)] * r
            return flow_hi, feed(z, p, pack)

        fed.append(lax.fori_loop(0, NZ, sweep, (plane, plane), unroll=NZ)[1])

    for i in range(2, 8):
        @pl.when(spots[i][1])
        def _():
            arrival(i).wait_recv()

    column = lane24 & 7
    low24 = column < 4
    pad2, pad4 = jnp.zeros((2, LY), F32), jnp.zeros((4, LY), F32)
    strips = []
    for d in range(2):
        left, right = rc.at[2 * d], rc.at[2 * d + 1]
        a = jnp.concatenate([ry[d, pl.ds(0, RX)], right[pl.ds(0, 3)], pad2, left[pl.ds(0, 3)]], axis=0)
        b = jnp.concatenate([ry[d, pl.ds(RX, RX)], right[pl.ds(3, 2)], pad4, left[pl.ds(3, 2)]], axis=0)
        m = ry[d, pl.ds(2 * RX, 8)]
        m_tail = [right[pl.ds(5, 2)], pad4, left[pl.ds(5, 2)]]
        if d == 0:
            halos = (a, lanes(a, -4), b, lanes(b, -4), jnp.concatenate([m, lanes(m, -4)] + m_tail, axis=0))
        else:
            halos = (lanes(a, 4), a, lanes(b, 4), b, jnp.concatenate([lanes(m, 4), m] + m_tail, axis=0))
        k, p, s, q, free = (
            jnp.where(low24, h, w) if d == 0 else jnp.where(low24, w, h) for h, w in zip(halos, whole))
        fx_t = harmonic(k, before(k))
        fz_t = jnp.where(lane24 < 8, 0.0, harmonic(k, lanes(k, 8)))
        end = column == (7 if d == 0 else 0)
        turn = -1 if d == 0 else 1
        t_lo = harmonic(k, lanes(k, 1))
        t_end = harmonic(k, lanes(fed_k, turn))
        if d == 0:
            t_hi = jnp.where(end, t_end, lanes(t_lo, -1))
        else:
            t_lo = jnp.where(end, t_end, t_lo)
            t_hi = lanes(t_lo, -1)
        total = s + fx_t + after(fx_t) + t_lo + t_hi + fz_t + lanes(fz_t, -8)
        g = free * inverse(jnp.maximum(total, TINY))
        right_side = s * p + q
        for it in range(SWEEPS):
            p_lo, p_hi = lanes(p, 1), lanes(p, -1)
            beyond = lanes(fed[it], turn)
            if d == 0:
                p_hi = jnp.where(end, beyond, p_hi)
            else:
                p_lo = jnp.where(end, beyond, p_lo)
            fx = fx_t * (p - before(p))
            fz = fz_t * (p - lanes(p, 8))
            r = (right_side - s * p - fx + after(fx) - t_lo * (p - p_lo) + t_hi * (p_hi - p)
                 - fz + lanes(fz, -8))
            p = p + F32(relax_weight(it)) * g * r
        strips.append((t_lo, p))
    face[...] = jnp.where(column == 4, strips[0][0], lanes(strips[1][0], -1))[:RX]
    edge[...] = jnp.where(column == 3, strips[0][1], lanes(strips[1][1], -2))[:RX]
    own_edge = jnp.where(low24, strips[1][1], strips[0][1])
    outer = (lane24 < 3) | (lane24 > LY - 4)

    def overlay(z, c):
        pb[at(z + 1)] = jnp.where(outer, lanes(own_edge, -(8 * z + 4)), pb[at(z + 1)])
        return c

    lax.fori_loop(0, NZ, overlay, 0, unroll=NZ)

    for i in range(4):
        @pl.when(spots[i][1])
        def _():
            sarrival(i).wait_recv()
    m_lo, m_hi = rsy[0], rsy[1]
    side[0] = jnp.where(odd, lanes(m_lo, 1), lanes(m_hi, -1))
    side[1] = jnp.where(odd, m_lo, m_hi)
    row_lo[...] = rsx[0]
    row_hi[...] = rsx[1]
    for i in range(8):
        @pl.when(spots[i][1])
        def _():
            copy(i).wait_send()
            if i < 4:
                scopy(i).wait_send()


def transport_kernel(sp, phi, rea, p_ref, tx, ty, tz, face, edge, side, row_lo, row_hi,
                     conc_out, p_out, phi_out, conc, sem):
    outs = [
        pltpu.make_async_copy(p_ref.at[pl.ds(1, NZ), pl.ds(0, RX)], p_out, sem.at[0]),
        pltpu.make_async_copy(phi, phi_out, sem.at[1]),
    ]
    for c in outs:
        c.start()
    lane, row = iota(RX, 1), iota(RX, 0)
    first, last = lane == 0, lane == LY - 1
    top, bottom = row == 0, row == RX - 1

    def body(z, carry):
        wide = p_ref[z + 1]
        p = wide[:RX]
        turned = lanes(edge[...], -(8 * z + 3))
        t_x = tx[z]
        crossing = lanes(face[...], -(8 * z + 4))
        t_lo = jnp.where(first, crossing, ty[z, :RX])
        t_hi = jnp.where(last, crossing, lanes(t_lo, -1))
        flows = [
            t_x[:RX] * (p - before(wide)[:RX]),
            after(t_x)[:RX] * (p - after(wide)[:RX]),
            t_lo * (p - jnp.where(first, turned, lanes(p, 1))),
            t_hi * (p - jnp.where(last, turned, lanes(p, -1))),
            tz[z, :RX] * (p - p_ref[z, :RX]),
            tz[z + 1, :RX] * (p - p_ref[z + 2, :RX]),
        ]
        scale = TIME_STEP * inverse(phi[z])
        out = jnp.maximum(flows[0], 0.0)
        for f in flows[1:]:
            out = out + jnp.maximum(f, 0.0)
        keep = 1.0 - scale * out
        take = [-scale * jnp.minimum(f, 0.0) for f in flows]
        reaction = rea[z]
        z_lo, z_hi = jnp.maximum(z - 1, 0), jnp.minimum(z + 1, NZ - 1)
        half = side[lax.div(z, 8)]
        for s in range(NSPEC):
            c = sp[s, pl.ds(pl.multiple_of(z * RX, 8), RX)]
            turned_c = lanes(half, -(2 * (lax.rem(z, 8) * 8 + s) + 1))
            total = c * keep
            total = total + take[0] * jnp.where(top, row_lo[s, pl.ds(z, 1)], before(c))
            total = total + take[1] * jnp.where(bottom, row_hi[s, pl.ds(z, 1)], after(c))
            total = total + take[2] * jnp.where(first, turned_c, lanes(c, 1))
            total = total + take[3] * jnp.where(last, turned_c, lanes(c, -1))
            total = total + take[4] * sp[s, pl.ds(pl.multiple_of(z_lo * RX, 8), RX)]
            total = total + take[5] * sp[s, pl.ds(pl.multiple_of(z_hi * RX, 8), RX)]
            if STOICHIOMETRY[s]:
                total = total + STOICHIOMETRY[s] * reaction
            conc[s, z] = total
        return carry

    for part in range(4):
        lax.fori_loop(4 * part, 4 * part + 4, body, 0, unroll=4)
        at = pl.ds(4 * part, 4)
        c = pltpu.make_async_copy(conc.at[:, at], conc_out.at[:, at], sem.at[2 + part])
        c.start()
        outs.append(c)
    for c in outs:
        c.wait()


def build(sizes):
    tile, wide = (NZ, RX, LY), (NZ, EX, LY)
    flat, padded = (NZ * EX, LY), ((NZ + 2) * EX, LY)
    species = (NSPEC, NZ, RX, LY)
    halo = [
        (2, len(PLANES), NZ, LY), (2, 2 * RX + 8, LY), (4, 8, LY), (2, NSPEC, NZ, LY), (2, RX, LY),
    ]
    vmem = pl.BlockSpec(memory_space=pltpu.VMEM)
    hbm = pl.BlockSpec(memory_space=pltpu.HBM)
    middle = [
        (NSPEC, NZ * RX, LY), tile, tile, padded, wide, wide, (NZ + 1, EX, LY),
        (RX, LY), (RX, LY), (2, RX, LY), (NSPEC, NZ, LY), (NSPEC, NZ, LY),
    ]
    dma = pltpu.SemaphoreType.DMA

    def shards(sp, *args):
        args = [pltpu.with_memory_space_constraint(a, pltpu.HBM) for a in (sp.reshape(middle[0]), *args)]
        shared = pl.pallas_call(
            lambda *refs: flow_kernel(sizes, *refs),
            out_shape=[pltpu.VMEM(shape, F32) for shape in middle],
            in_specs=[hbm] * 6,
            out_specs=[vmem] * len(middle),
            scratch_shapes=[
                pltpu.VMEM(tile, F32), pltpu.VMEM(tile, jnp.int32), pltpu.VMEM(tile, jnp.int32),
                pltpu.VMEM(tile, F32), pltpu.VMEM(tile, F32),
                pltpu.VMEM(padded, F32), pltpu.VMEM(padded, F32),
                pltpu.VMEM(flat, F32), pltpu.VMEM(flat, F32), pltpu.VMEM(flat, F32),
                *[pltpu.VMEM(shape, F32) for shape in halo + halo],
                dma((7,)), dma((8,)), dma((8,)), dma((4,)), dma((4,)), pltpu.SemaphoreType.REGULAR,
            ],
            compiler_params=pltpu.CompilerParams(
                collective_id=0, has_side_effects=True, vmem_limit_bytes=32 * 2**20),
            name="flow",
        )(*args)
        shared = list(shared)
        shared[3] = shared[3].reshape(NZ + 2, EX, LY)
        return tuple(pl.pallas_call(
            transport_kernel,
            out_shape=[jax.ShapeDtypeStruct(s, F32) for s in (species, tile, tile)],
            in_specs=[vmem] * len(middle),
            out_specs=[hbm] * 3,
            scratch_shapes=[pltpu.VMEM(species, F32), dma((6,))],
            compiler_params=pltpu.CompilerParams(vmem_limit_bytes=16 * 2**20),
            name="transport",
        )(*shared))

    return shards


def solution(mesh):
    specs = (P(None, None, "gx", "gy"),) + (P(None, "gx", "gy"),) * 5
    outs = (P(None, None, "gx", "gy"), P(None, "gx", "gy"), P(None, "gx", "gy"))
    sizes = (mesh.shape["gx"], mesh.shape["gy"])
    return jax.shard_map(build(sizes), mesh=mesh, in_specs=specs, out_specs=outs, check_vma=False)
```

```python
import math

import jax
import jax.numpy as jnp
from jax import lax
from jax.experimental import pallas as pl
from jax.experimental.pallas import tpu as pltpu
from jax.sharding import PartitionSpec as P

SWEEPS = 3
NSPEC, NZ, RX, LY = 8, 16, 16, 128
EX = RX + 8
FIELDS = 5
TINY = 1e-30
PLANES = [(f, d) for f in range(FIELDS) for d in range(4 if f < 2 else 3)]

ZONE_RATES = (0.02, 0.05, 0.1, 0.2)
ZONE_PERMEABILITY = (5.0, 10.0, 20.0, 40.0)
SOLUBILITY = 0.5
MOLAR_VOLUME = 0.05
STORAGE_COEF = 0.2
TIME_STEP = 0.2
CHEB_SPREAD = 0.92
STOICHIOMETRY = (-1.0, -1.0, 0.0, 0.0, 0.0, 0.0, 0.0, 0.0)

F32 = jnp.float32
MESH = pl.DeviceIdType.MESH
DIRS = ((-1, 0), (1, 0), (0, -1), (0, 1), (-1, -1), (1, -1), (-1, 1), (1, 1))
OPPOSITE = tuple(DIRS.index((-a, -b)) for a, b in DIRS)


def relax_weight(iteration):
    return 1.0 / (1.0 + CHEB_SPREAD * math.cos(math.pi * (2 * iteration + 1) / (2 * SWEEPS)))


def lookup(labels, table):
    out = jnp.where(labels == 0, F32(table[0]), F32(table[1]))
    out = jnp.where(labels == 2, F32(table[2]), out)
    return jnp.where(labels == 3, F32(table[3]), out)


def inverse(x):
    guess = pl.reciprocal(x, approx=True)
    return guess * (2.0 - x * guess)


def harmonic(a, b):
    return (2.0 * a * b) * inverse(jnp.maximum(a + b, TINY))


def lanes(x, shift):
    return pltpu.roll(x, shift % LY if isinstance(shift, int) else lax.rem(shift + 2 * LY, LY), 1)


def before(x):
    return pltpu.roll(x, 1, 0)


def after(x):
    return pltpu.roll(x, x.shape[0] - 1, 0)


def iota(rows, dim):
    return lax.broadcasted_iota(jnp.int32, (rows, LY), dim)


def flow_kernel(sizes, sp_in, por_in, old_in, src_in, zone_in, fix_in,
                spx, left, right, phi, rea, pd, tx, ty, tz, cross, side,
                sp, por, zone, fix, old, src, pa, p1, p2, perm, stor, rhs, gain, step, known,
                sx, sy, sc, ssx, ssy, rx, ry, rc, rsx, rsy,
                in_sem, send_sem, recv_sem, s_send, s_recv, ready):
    gx, gy = lax.axis_index("gx"), lax.axis_index("gy")
    spots = []
    for dx, dy in DIRS:
        there = None
        for here, move, size in ((gx, dx, sizes[0]), (gy, dy, sizes[1])):
            if move:
                ok = here > 0 if move < 0 else here < size - 1
                there = ok if there is None else there & ok
        spots.append(((gx + dx, gy + dy), there))

    seam = sizes[1] // 2
    split = jnp.bool_(sizes[1] >= 4)
    at_lo, at_hi = (gy == seam - 1) & split, (gy == seam) & split
    at_seam = at_lo | at_hi
    barrier = pltpu.get_barrier_semaphore()
    expected = 0
    for i, (where, there) in enumerate(spots):
        far = (at_lo & (DIRS[i][1] > 0)) | (at_hi & (DIRS[i][1] < 0))
        counts = split & ((where[1] == seam - 1) | (where[1] == seam))
        beside = there & (far | jnp.logical_not(counts))

        @pl.when(beside)
        def _():
            pl.semaphore_signal(barrier, inc=1, device_id=where, device_id_type=MESH)
        expected = expected + (there & (far | jnp.logical_not(at_seam))).astype(jnp.int32)

    loads = [
        pltpu.make_async_copy(sp_in.at[pl.ds(0, 2)], sp.at[pl.ds(0, 2)], in_sem.at[0]),
        pltpu.make_async_copy(zone_in, zone, in_sem.at[1]),
        pltpu.make_async_copy(por_in, por, in_sem.at[2]),
        pltpu.make_async_copy(old_in, old, in_sem.at[3]),
        pltpu.make_async_copy(src_in, src, in_sem.at[4]),
        pltpu.make_async_copy(fix_in, fix, in_sem.at[5]),
        pltpu.make_async_copy(sp_in.at[pl.ds(2, NSPEC - 2)], sp.at[pl.ds(2, NSPEC - 2)], in_sem.at[6]),
    ]
    for c in loads:
        c.start()

    for i in range(8):
        @pl.when(jnp.logical_not(spots[i][1]))
        def _():
            if i < 2:
                rx[i] = jnp.zeros(rx.shape[1:], F32)
                rsx[i] = jnp.zeros(rsx.shape[1:], F32)
            elif i < 4:
                ry[i - 2] = jnp.zeros(ry.shape[1:], F32)
                rsy[i - 2] = jnp.zeros(rsy.shape[1:], F32)
            else:
                rc[i - 4] = jnp.zeros(rc.shape[1:], F32)
    plane = jnp.zeros((EX, LY), F32)
    for ref in (perm, pa, p1, p2, pd):
        ref[pl.ds(0, EX)] = plane
        ref[pl.ds((NZ + 1) * EX, EX)] = plane
    for ref in (stor, rhs, gain):
        for z in range(NZ):
            ref[pl.ds(z * EX + RX, 8)] = plane[:8]

    lane = iota(RX, 1)
    group = lax.shift_right_logical(lane, 3)
    low = (lane & 7) < 4
    for c in loads[:6]:
        c.wait()

    def at(z, rows=EX, skip=0):
        return pl.ds(pl.multiple_of(z * EX + skip, 8), rows)

    def plane_at(r, up=0):
        return pl.ds((1 + up) * EX + r % EX, NZ, stride=EX)

    def feed_mask(z):
        spot = (iota(8, 1) - 8 * z) & (LY - 1)
        return (spot == 8) | (spot == LY - 1)

    def own(z, packs):
        rows = pl.ds(pl.multiple_of(z * RX, 8), RX)
        c0, c1 = sp[0, rows], sp[1, rows]
        label = zone[z]
        reaction = lookup(label, ZONE_RATES) * (c0 * c1 - SOLUBILITY)
        new = por[z] - MOLAR_VOLUME * reaction
        solid = 1.0 - new
        k = lookup(label, ZONE_PERMEABILITY) * (new * new * new) * inverse(solid * solid)
        s = STORAGE_COEF * new
        free = 1.0 - fix[z].astype(F32)
        p, q = old[z], src[z]
        rea[rows] = reaction
        phi[rows] = new
        perm[at(z + 1, RX)] = k
        pa[at(z + 1, RX)] = p
        stor[at(z, RX)] = s
        rhs[at(z, RX)] = q
        gain[at(z, RX)] = free
        turned = [lanes(v, 8 * z + 4) for v in (k, p, s, q, free)]
        mask = feed_mask(z)
        fed_new = [jnp.where(mask, turned[f][8 * t:8 * t + 8], packs[FIELDS + 2 * f + t]) for f in range(2) for t in range(2)]
        return tuple(jnp.where(group == z, v, pack) for v, pack in zip(turned, packs)) + tuple(fed_new)

    zero, zero8 = jnp.zeros((RX, LY), F32), jnp.zeros((8, LY), F32)
    packs = lax.fori_loop(0, NZ, own, (zero,) * FIELDS + (zero8,) * 4, unroll=8)
    own_fed = packs[FIELDS:]
    packs = packs[:FIELDS]
    k, p, s, q, free = packs
    low8 = low[:8]
    for side_y in range(2):
        if side_y == 0:
            a, b = jnp.where(low, lanes(k, -4), p), jnp.where(low, lanes(s, -4), q)
            m = jnp.where(low8, lanes(free[:8], -4), free[8:])
        else:
            a, b = jnp.where(low, k, lanes(p, 4)), jnp.where(low, s, lanes(q, 4))
            m = jnp.where(low8, free[:8], lanes(free[8:], 4))
        sy[side_y, pl.ds(0, RX)] = a
        sy[side_y, pl.ds(RX, RX)] = b
        sy[side_y, pl.ds(2 * RX, 8)] = m
        for side_x in range(2):
            j = 2 * side_y + side_x
            if side_x == 0:
                parts_c = (a[:3], b[:2], free[:2])
            else:
                parts_c = (a[RX - 3:], b[RX - 2:], free[RX - 2:])
            sc[j, pl.ds(0, 3)] = parts_c[0]
            sc[j, pl.ds(3, 2)] = parts_c[1]
            sc[j, pl.ds(5, 2)] = parts_c[2]
            sc[j, pl.ds(7, 1)] = parts_c[2][:1]

    def strided(ref, z0, row):
        return ref.at[pl.ds(z0 * EX + row, NZ, stride=EX)]

    fields = ((perm, 1), (pa, 1), (stor, 0), (rhs, 0), (gain, 0))
    for n, (f, d) in enumerate(PLANES):
        ref, z0 = fields[f]
        sx[0, n] = strided(ref, z0, d)[...]
        sx[1, n] = strided(ref, z0, RX - 1 - d)[...]

    def parts(i):
        if i < 2:
            return sx.at[i], rx, i
        if i < 4:
            return sy.at[i - 2], ry, i - 2
        return sc.at[i - 4], rc, i - 4

    def copy(i):
        from_ref, _, _ = parts(i)
        _, dst, slot = parts(OPPOSITE[i])
        return pltpu.make_async_remote_copy(
            src_ref=from_ref, dst_ref=dst.at[slot], send_sem=send_sem.at[i],
            recv_sem=recv_sem.at[OPPOSITE[i]], device_id=spots[i][0], device_id_type=MESH)

    def arrival(i):
        from_ref, dst, slot = parts(i)
        return pltpu.make_async_remote_copy(
            src_ref=from_ref, dst_ref=dst.at[slot], send_sem=send_sem.at[i],
            recv_sem=recv_sem.at[i], device_id=spots[i][0], device_id_type=MESH)

    def sparts(i):
        return (ssx.at[i], rsx, i) if i < 2 else (ssy.at[i - 2], rsy, i - 2)

    def scopy(i):
        from_ref, _, _ = sparts(i)
        _, dst, slot = sparts(OPPOSITE[i])
        return pltpu.make_async_remote_copy(
            src_ref=from_ref, dst_ref=dst.at[slot], send_sem=s_send.at[i],
            recv_sem=s_recv.at[OPPOSITE[i]], device_id=spots[i][0], device_id_type=MESH)

    def sarrival(i):
        from_ref, dst, slot = sparts(i)
        return pltpu.make_async_remote_copy(
            src_ref=from_ref, dst_ref=dst.at[slot], send_sem=s_send.at[i],
            recv_sem=s_recv.at[i], device_id=spots[i][0], device_id_type=MESH)

    def send(only, order, make):
        for i in order:
            @pl.when(spots[i][1] & only)
            def _():
                make(i).start()

    inner = jnp.logical_not(at_seam)

    @pl.when(at_hi)
    def _():
        pl.semaphore_wait(barrier, expected)
    send(at_hi, (2, 4, 5), copy)

    loads[6].wait()
    for s in range(NSPEC):
        ssx[0, s] = sp[s, pl.ds(0, NZ, stride=RX)]
        ssx[1, s] = sp[s, pl.ds(RX - 1, NZ, stride=RX)]
    pair = lax.shift_right_logical(lane, 1)
    odd = (lane & 1) == 1

    halves = [zero, zero]
    for x in range(RX):
        for s in range(NSPEC):
            m = (x % 8) * 8 + s
            turned = lanes(sp[s, pl.ds(x, NZ, stride=RX)], 2 * m + 1)
            halves[x // 8] = jnp.where(pair == m, turned, halves[x // 8])
    lo, hi = halves
    ssy[0] = jnp.where(odd, lo, lanes(hi, -1))
    ssy[1] = jnp.where(odd, lanes(hi, 1), lo)
    send(at_hi, (2,), scopy)

    @pl.when(inner)
    def _():
        pl.semaphore_wait(barrier, expected)
    for edge_row, toward in ((seam - 2, 1), (seam + 1, -1)):
        @pl.when((gy == edge_row) & split)
        def _():
            pl.semaphore_signal(ready, inc=1, device_id=(gx, gy + toward), device_id_type=MESH)

    @pl.when(at_seam)
    def _():
        pl.semaphore_wait(ready, 1)
    send(True, (0, 1), copy)
    send(inner | at_lo, (2, 4, 5), copy)
    send(inner | at_hi, (3, 6, 7), copy)

    send(True, (0, 1), scopy)
    send(inner | at_lo, (2,), scopy)
    send(inner | at_hi, (3,), scopy)

    for s in range(NSPEC):
        for x in range(RX):
            c = sp[s, pl.ds(x, NZ, stride=RX)]
            spx[s, pl.ds(NZ * (x + 1), NZ)] = c
            left[s, pl.ds(NZ * x, NZ)] = lanes(c, 1)
            right[s, pl.ds(NZ * x, NZ)] = lanes(c, -1)

    def face_x(r):
        tx[r % EX] = harmonic(perm[plane_at(r)], perm[plane_at(r - 1)])

    def in_plane(r):
        k = perm[plane_at(r)]
        ty[0, r % EX] = jnp.where(lane > 0, harmonic(k, lanes(k, 1)), 0.0)
        ty[1, r % EX] = jnp.where(lane < LY - 1, harmonic(k, lanes(k, -1)), 0.0)
        tz[0, r % EX] = harmonic(k, perm[plane_at(r, -1)])
        tz[1, r % EX] = harmonic(k, perm[plane_at(r, 1)])

    def coefficients(r):
        at_r = r % EX
        s = stor[plane_at(r, -1)]
        total = (s + tx[at_r] + tx[(r + 1) % EX]) + (ty[0, at_r] + ty[1, at_r]) + (tz[0, at_r] + tz[1, at_r])
        step[at_r] = gain[plane_at(r, -1)] * inverse(jnp.maximum(total, TINY))
        known[at_r] = s * pa[plane_at(r)] + rhs[plane_at(r, -1)]

    def relax(it, r):
        now, new, at_r = levels[it], levels[it + 1], r % EX
        p = now[plane_at(r)]
        out = stor[plane_at(r, -1)] * p
        out = out + tx[at_r] * (p - now[plane_at(r - 1)])
        out = out + tx[(r + 1) % EX] * (p - now[plane_at(r + 1)])
        out = out + tz[0, at_r] * (p - now[plane_at(r, -1)])
        out = out + tz[1, at_r] * (p - now[plane_at(r, 1)])
        out = out + ty[0, at_r] * (p - lanes(p, 1))
        out = out + ty[1, at_r] * (p - lanes(p, -1))
        new[plane_at(r)] = p + F32(relax_weight(it)) * step[at_r] * (known[at_r] - out)

    levels = (pa, p1, p2, pd)
    for r in range(1, RX):
        face_x(r)
    for r in range(RX):
        in_plane(r)
    for r in range(1, RX - 1):
        coefficients(r)
    for it in range(SWEEPS):
        for r in range(1 + it, RX - 1 - it):
            relax(it, r)

    @pl.when(at_lo)
    def _():
        pl.semaphore_wait(barrier, expected)
    send(at_lo, (3, 6, 7), copy)
    send(at_lo, (3,), scopy)

    for i in range(2):
        @pl.when(spots[i][1])
        def _():
            arrival(i).wait_recv()
    for n, (f, d) in enumerate(PLANES):
        ref, z0 = fields[f]
        strided(ref, z0, RX + d)[...] = rx[1, n]
        strided(ref, z0, EX - 1 - d)[...] = rx[0, n]
    for r in (-3, -2, -1, 0, RX, RX + 1, RX + 2, RX + 3):
        face_x(r)
    for r in (-3, -2, -1, RX, RX + 1, RX + 2):
        in_plane(r)
    for r in (-3, -2, -1, 0, RX - 1, RX, RX + 1, RX + 2):
        coefficients(r)
    for it in range(SWEEPS):
        for j in range(4):
            relax(it, it - 3 + j)
            relax(it, RX - 1 - it + j)

    lane24 = iota(EX, 1)
    group8 = lax.shift_right_logical(iota(8, 1), 3)
    tails, tail_fed, fed_1, fed_2 = [zero8] * FIELDS, [zero8] * 2, [zero8] * 3, [zero8] * 3
    for z in range(NZ):
        mask = feed_mask(z)
        for f, (ref, z0) in enumerate(fields):
            turned = lanes(ref[at(z + z0, 8, RX)], 8 * z + 4)
            tails[f] = jnp.where(group8 == z, turned, tails[f])
            if f < 2:
                tail_fed[f] = jnp.where(mask, turned, tail_fed[f])
        for ref, pack in ((p1, fed_1), (p2, fed_2)):
            for t in range(3):
                pack[t] = jnp.where(mask, lanes(ref[at(z + 1, 8, 8 * t)], 8 * z + 4), pack[t])
    whole = [jnp.concatenate([a, b], axis=0) for a, b in zip(packs, tails)]
    fed_k = jnp.concatenate([own_fed[0], own_fed[1], tail_fed[0]], axis=0)
    fed = [
        jnp.concatenate([own_fed[2], own_fed[3], tail_fed[1]], axis=0),
        jnp.concatenate(fed_1, axis=0), jnp.concatenate(fed_2, axis=0),
    ]

    for i in range(2, 8):
        @pl.when(spots[i][1])
        def _():
            arrival(i).wait_recv()

    column = lane24 & 7
    low24 = column < 4
    pad2, pad4 = jnp.zeros((2, LY), F32), jnp.zeros((4, LY), F32)
    strips = []
    for d in range(2):
        minus, plus = rc.at[2 * d], rc.at[2 * d + 1]
        a = jnp.concatenate([ry[d, pl.ds(0, RX)], plus[pl.ds(0, 3)], pad2, minus[pl.ds(0, 3)]], axis=0)
        b = jnp.concatenate([ry[d, pl.ds(RX, RX)], plus[pl.ds(3, 2)], pad4, minus[pl.ds(3, 2)]], axis=0)
        m = ry[d, pl.ds(2 * RX, 8)]
        m_tail = [plus[pl.ds(5, 2)], pad4, minus[pl.ds(5, 2)]]
        if d == 0:
            halos = (a, lanes(a, -4), b, lanes(b, -4), jnp.concatenate([m, lanes(m, -4)] + m_tail, axis=0))
        else:
            halos = (lanes(a, 4), a, lanes(b, 4), b, jnp.concatenate([lanes(m, 4), m] + m_tail, axis=0))
        k, p, s, q, free = (
            jnp.where(low24, h, w) if d == 0 else jnp.where(low24, w, h) for h, w in zip(halos, whole))
        end = column == (7 if d == 0 else 0)
        turn = -1 if d == 0 else 1
        beyond = [lanes(v, turn) for v in [fed_k] + fed]

        def sides(v, outer_v):
            lo, hi = lanes(v, 1), lanes(v, -1)
            if d == 0:
                hi = jnp.where(end, outer_v, hi)
            else:
                lo = jnp.where(end, outer_v, lo)
            return before(v), after(v), lo, hi, lanes(v, 8), lanes(v, -8)

        terms = [harmonic(k, v) for v in sides(k, beyond[0])]
        terms[4] = jnp.where(lane24 < 8, 0.0, terms[4])
        terms[5] = jnp.where(lane24 < LY - 8, terms[5], 0.0)
        total = s + ((terms[0] + terms[1]) + (terms[2] + terms[3])) + (terms[4] + terms[5])
        g = free * inverse(jnp.maximum(total, TINY))
        right_side = s * p + q
        for it in range(SWEEPS):
            flows = [t * (p - v) for t, v in zip(terms, sides(p, beyond[1 + it]))]
            r = (right_side - s * p) - ((flows[0] + flows[1]) + (flows[2] + flows[3])) - (flows[4] + flows[5])
            p = p + F32(relax_weight(it)) * g * r
        across = terms[2] * (p - lanes(p, 1)) if d == 0 else terms[3] * (p - lanes(p, -1))
        strips.append((across, p))
    own_edge = jnp.where(low24, strips[1][1], strips[0][1])
    own_flow = jnp.where(low24, strips[1][0], strips[0][0])
    outer = (lane24 < 3) | (lane24 > LY - 4)
    for z in range(NZ):
        pd[at(z + 1)] = jnp.where(outer, lanes(own_edge, -(8 * z + 4)), pd[at(z + 1)])
        cross[at(z, RX)] = lanes(own_flow[:RX], -(8 * z + 4))

    for i in range(4):
        @pl.when(spots[i][1])
        def _():
            sarrival(i).wait_recv()
    m_lo, m_hi = rsy[0], rsy[1]
    side[0] = jnp.where(odd, lanes(m_lo, 1), lanes(m_hi, -1))
    side[1] = jnp.where(odd, m_lo, m_hi)
    for s in range(NSPEC):
        spx[s, pl.ds(0, NZ)] = rsx[0, s]
        spx[s, pl.ds(NZ * (RX + 1), NZ)] = rsx[1, s]
    for i in range(8):
        @pl.when(spots[i][1])
        def _():
            copy(i).wait_send()
            if i < 4:
                scopy(i).wait_send()


def transport_kernel(spx, left, right, phi, rea, p_ref, tx, ty, tz, cross, side,
                     conc_out, p_out, phi_out, conc, final, weight, sem):
    outs = [pltpu.make_async_copy(phi, phi_out, sem.at[0]), pltpu.make_async_copy(final, p_out, sem.at[1])]
    outs[0].start()
    lane = iota(RX, 1)
    first, last = lane == 0, lane == LY - 1

    def plane_at(r, up=0):
        return pl.ds((1 + up) * EX + r % EX, NZ, stride=EX)

    for x in range(RX):
        p = p_ref[plane_at(x)]
        final[pl.ds(x, NZ, stride=RX)] = p
        through = cross[plane_at(x, -1)]
        flows = [
            tx[x] * (p - p_ref[plane_at(x - 1)]),
            tx[x + 1] * (p - p_ref[plane_at(x + 1)]),
            jnp.where(first, through, ty[0, x] * (p - lanes(p, 1))),
            jnp.where(last, through, ty[1, x] * (p - lanes(p, -1))),
            tz[0, x] * (p - p_ref[plane_at(x, -1)]),
            tz[1, x] * (p - p_ref[plane_at(x, 1)]),
        ]
        scale = TIME_STEP * inverse(phi[pl.ds(x, NZ, stride=RX)])
        out = [jnp.maximum(f, 0.0) for f in flows]
        out = ((out[0] + out[1]) + (out[2] + out[3])) + (out[4] + out[5])
        weight[0, x] = 1.0 - scale * out
        for n, f in enumerate(flows):
            weight[n + 1, x] = -scale * jnp.minimum(f, 0.0)
    outs[1].start()

    group = 2
    for s0 in range(0, NSPEC, group):
        for x in range(RX):
            w = [weight[n, x] for n in range(7)]
            for s in range(s0, s0 + group):
                def row(shift):
                    return spx[s, pl.ds(NZ * (x + 1) + shift, NZ)]

                turned = lanes(side[x // 8], -(2 * ((x % 8) * 8 + s) + 1))
                around = [
                    row(-NZ), row(NZ),
                    jnp.where(first, turned, left[s, pl.ds(NZ * x, NZ)]),
                    jnp.where(last, turned, right[s, pl.ds(NZ * x, NZ)]),
                    row(-1), row(1),
                ]
                total = row(0) * w[0]
                for a, b in zip(w[1:], around):
                    total = total + a * b
                if STOICHIOMETRY[s]:
                    total = total + STOICHIOMETRY[s] * rea[pl.ds(x, NZ, stride=RX)]
                conc[s, pl.ds(x, NZ, stride=RX)] = total
        some = pl.ds(s0, group)
        c = pltpu.make_async_copy(conc.at[some], conc_out.at[some], sem.at[2 + s0 // group])
        c.start()
        outs.append(c)
    for c in outs:
        c.wait()


def build(sizes):
    tile, rows = (NZ, RX, LY), (NZ * RX, LY)
    flat, padded, planes = (NZ * EX, LY), ((NZ + 2) * EX, LY), (EX, NZ, LY)
    species, turned = (NSPEC, NZ, RX, LY), (NSPEC, NZ * RX, LY)
    halo = [
        (2, len(PLANES), NZ, LY), (2, 2 * RX + 8, LY), (4, 8, LY), (2, NSPEC, NZ, LY), (2, NZ, LY),
    ]
    vmem = pl.BlockSpec(memory_space=pltpu.VMEM)
    hbm = pl.BlockSpec(memory_space=pltpu.HBM)
    middle = [
        (NSPEC, (RX + 2) * NZ, LY), turned, turned, rows, rows, padded, planes, (2,) + planes, (2,) + planes,
        flat, (2, NZ, LY),
    ]
    dma = pltpu.SemaphoreType.DMA

    def shards(sp, *args):
        args = [pltpu.with_memory_space_constraint(a, pltpu.HBM) for a in (sp.reshape(turned), *args)]
        shared = pl.pallas_call(
            lambda *refs: flow_kernel(sizes, *refs),
            out_shape=[pltpu.VMEM(shape, F32) for shape in middle],
            in_specs=[hbm] * 6,
            out_specs=[vmem] * len(middle),
            scratch_shapes=[
                pltpu.VMEM(turned, F32),
                pltpu.VMEM(tile, F32), pltpu.VMEM(tile, jnp.int32), pltpu.VMEM(tile, jnp.int32),
                pltpu.VMEM(tile, F32), pltpu.VMEM(tile, F32),
                *[pltpu.VMEM(padded, F32)] * 4, *[pltpu.VMEM(flat, F32)] * 3, *[pltpu.VMEM(planes, F32)] * 2,
                *[pltpu.VMEM(shape, F32) for shape in halo + halo],
                dma((7,)), dma((8,)), dma((8,)), dma((4,)), dma((4,)), pltpu.SemaphoreType.REGULAR,
            ],
            compiler_params=pltpu.CompilerParams(
                collective_id=0, has_side_effects=True, vmem_limit_bytes=32 * 2**20),
            name="flow",
        )(*args)
        conc, pressure, porosity = pl.pallas_call(
            transport_kernel,
            out_shape=[jax.ShapeDtypeStruct(s, F32) for s in (turned, rows, rows)],
            in_specs=[vmem] * len(middle),
            out_specs=[hbm] * 3,
            scratch_shapes=[pltpu.VMEM(turned, F32), pltpu.VMEM(rows, F32), pltpu.VMEM((7, RX, NZ, LY), F32), dma((6,))],
            compiler_params=pltpu.CompilerParams(vmem_limit_bytes=16 * 2**20),
            name="transport",
        )(*shared)
        return conc.reshape(species), pressure.reshape(tile), porosity.reshape(tile)

    return shards


def solution(mesh):
    specs = (P(None, None, "gx", "gy"),) + (P(None, "gx", "gy"),) * 5
    outs = (P(None, None, "gx", "gy"), P(None, "gx", "gy"), P(None, "gx", "gy"))
    sizes = (mesh.shape["gx"], mesh.shape["gy"])
    return jax.shard_map(build(sizes), mesh=mesh, in_specs=specs, out_specs=outs, check_vma=False)
```

```python
import math

import jax
import jax.numpy as jnp
from jax import lax
from jax.experimental import pallas as pl
from jax.experimental.pallas import tpu as pltpu
from jax.sharding import PartitionSpec as P

SWEEPS = 3
NSPEC, NZ, RX, LY = 8, 16, 16, 128
EX = RX + 8
FIELDS = 5
TINY = 1e-30
CUTS = (1, 1)
PLANES = [(f, d) for f in range(FIELDS) for d in range(4 if f < 2 else 3)]

ZONE_RATES = (0.02, 0.05, 0.1, 0.2)
ZONE_PERMEABILITY = (5.0, 10.0, 20.0, 40.0)
SOLUBILITY = 0.5
MOLAR_VOLUME = 0.05
STORAGE_COEF = 0.2
TIME_STEP = 0.2
CHEB_SPREAD = 0.92
STOICHIOMETRY = (-1.0, -1.0, 0.0, 0.0, 0.0, 0.0, 0.0, 0.0)

F32 = jnp.float32
MESH = pl.DeviceIdType.MESH
DIRS = ((-1, 0), (1, 0), (0, -1), (0, 1), (-1, -1), (1, -1), (-1, 1), (1, 1))
OPPOSITE = tuple(DIRS.index((-a, -b)) for a, b in DIRS)


def relax_weight(iteration):
    return 1.0 / (1.0 + CHEB_SPREAD * math.cos(math.pi * (2 * iteration + 1) / (2 * SWEEPS)))


def lookup(labels, table):
    out = jnp.where(labels == 0, F32(table[0]), F32(table[1]))
    out = jnp.where(labels == 2, F32(table[2]), out)
    return jnp.where(labels == 3, F32(table[3]), out)


def inverse(x):
    guess = pl.reciprocal(x, approx=True)
    return guess * (2.0 - x * guess)


def harmonic(a, b):
    return (2.0 * a * b) * inverse(jnp.maximum(a + b, TINY))


def lanes(x, shift):
    return pltpu.roll(x, shift % LY if isinstance(shift, int) else lax.rem(shift + 2 * LY, LY), 1)


def before(x):
    return pltpu.roll(x, 1, 0)


def after(x):
    return pltpu.roll(x, x.shape[0] - 1, 0)


def iota(rows, dim):
    return lax.broadcasted_iota(jnp.int32, (rows, LY), dim)


def flow_kernel(sizes, sp_in, por_in, old_in, src_in, zone_in, fix_in,
                spx, left, right, phi, rea, final, weight, side,
                pd, tx, ty, tz, cross, sp, por, zone, fix, old, src, pa, p1, p2, perm, stor, rhs, gain, step, known,
                sx, sy, sc, ssx, ssy, rx, ry, rc, rsx, rsy,
                in_sem, send_sem, recv_sem, s_send, s_recv, ready):
    gx, gy = lax.axis_index("gx"), lax.axis_index("gy")
    spots = []
    for dx, dy in DIRS:
        there = None
        for here, move, size in ((gx, dx, sizes[0]), (gy, dy, sizes[1])):
            if move:
                ok = here > 0 if move < 0 else here < size - 1
                there = ok if there is None else there & ok
        spots.append(((gx + dx, gy + dy), there))

    seam = sizes[1] // 2
    split = jnp.bool_(sizes[1] >= 4)
    at_lo, at_hi = (gy == seam - 1) & split, (gy == seam) & split
    at_seam = at_lo | at_hi
    barrier = pltpu.get_barrier_semaphore()
    expected = 0
    for i, (where, there) in enumerate(spots):
        far = (at_lo & (DIRS[i][1] > 0)) | (at_hi & (DIRS[i][1] < 0))
        counts = split & ((where[1] == seam - 1) | (where[1] == seam))
        beside = there & (far | jnp.logical_not(counts))

        @pl.when(beside)
        def _():
            pl.semaphore_signal(barrier, inc=1, device_id=where, device_id_type=MESH)
        expected = expected + (there & (far | jnp.logical_not(at_seam))).astype(jnp.int32)

    loads = [
        pltpu.make_async_copy(sp_in.at[pl.ds(0, 2)], sp.at[pl.ds(0, 2)], in_sem.at[0]),
        pltpu.make_async_copy(zone_in, zone, in_sem.at[1]),
        pltpu.make_async_copy(por_in, por, in_sem.at[2]),
        pltpu.make_async_copy(old_in, old, in_sem.at[3]),
        pltpu.make_async_copy(src_in, src, in_sem.at[4]),
        pltpu.make_async_copy(fix_in, fix, in_sem.at[5]),
        pltpu.make_async_copy(sp_in.at[pl.ds(2, NSPEC - 2)], sp.at[pl.ds(2, NSPEC - 2)], in_sem.at[6]),
    ]
    for c in loads:
        c.start()

    for i in range(8):
        @pl.when(jnp.logical_not(spots[i][1]))
        def _():
            if i < 2:
                rx[i] = jnp.zeros(rx.shape[1:], F32)
                rsx[i] = jnp.zeros(rsx.shape[1:], F32)
            elif i < 4:
                ry[i - 2] = jnp.zeros(ry.shape[1:], F32)
                rsy[i - 2] = jnp.zeros(rsy.shape[1:], F32)
            else:
                rc[i - 4] = jnp.zeros(rc.shape[1:], F32)
    plane = jnp.zeros((EX, LY), F32)
    for ref in (perm, pa, p1, p2, pd):
        ref[pl.ds(0, EX)] = plane
        ref[pl.ds((NZ + 1) * EX, EX)] = plane
    for ref in (stor, rhs, gain):
        for z in range(NZ):
            ref[pl.ds(z * EX + RX, 8)] = plane[:8]

    lane = iota(RX, 1)
    group = lax.shift_right_logical(lane, 3)
    low = (lane & 7) < 4
    for c in loads[:6]:
        c.wait()

    def at(z, rows=EX, skip=0):
        return pl.ds(pl.multiple_of(z * EX + skip, 8), rows)

    def plane_at(r, up=0):
        return pl.ds((1 + up) * EX + r % EX, NZ, stride=EX)

    def feed_mask(z):
        spot = (iota(8, 1) - 8 * z) & (LY - 1)
        return (spot == 8) | (spot == LY - 1)

    def own(z, packs):
        rows = pl.ds(pl.multiple_of(z * RX, 8), RX)
        c0, c1 = sp[0, rows], sp[1, rows]
        label = zone[z]
        reaction = lookup(label, ZONE_RATES) * (c0 * c1 - SOLUBILITY)
        new = por[z] - MOLAR_VOLUME * reaction
        solid = 1.0 - new
        k = lookup(label, ZONE_PERMEABILITY) * (new * new * new) * inverse(solid * solid)
        s = STORAGE_COEF * new
        free = 1.0 - fix[z].astype(F32)
        p, q = old[z], src[z]
        rea[rows] = reaction
        phi[rows] = new
        perm[at(z + 1, RX)] = k
        pa[at(z + 1, RX)] = p
        stor[at(z, RX)] = s
        rhs[at(z, RX)] = q
        gain[at(z, RX)] = free
        turned = [lanes(v, 8 * z + 4) for v in (k, p, s, q, free)]
        mask = feed_mask(z)
        fed_new = [jnp.where(mask, turned[f][8 * t:8 * t + 8], packs[FIELDS + 2 * f + t]) for f in range(2) for t in range(2)]
        return tuple(jnp.where(group == z, v, pack) for v, pack in zip(turned, packs)) + tuple(fed_new)

    zero, zero8 = jnp.zeros((RX, LY), F32), jnp.zeros((8, LY), F32)
    packs = lax.fori_loop(0, NZ, own, (zero,) * FIELDS + (zero8,) * 4, unroll=8)
    own_fed = packs[FIELDS:]
    packs = packs[:FIELDS]
    k, p, s, q, free = packs
    low8 = low[:8]
    for side_y in range(2):
        if side_y == 0:
            a, b = jnp.where(low, lanes(k, -4), p), jnp.where(low, lanes(s, -4), q)
            m = jnp.where(low8, lanes(free[:8], -4), free[8:])
        else:
            a, b = jnp.where(low, k, lanes(p, 4)), jnp.where(low, s, lanes(q, 4))
            m = jnp.where(low8, free[:8], lanes(free[8:], 4))
        sy[side_y, pl.ds(0, RX)] = a
        sy[side_y, pl.ds(RX, RX)] = b
        sy[side_y, pl.ds(2 * RX, 8)] = m
        for side_x in range(2):
            j = 2 * side_y + side_x
            if side_x == 0:
                parts_c = (a[:3], b[:2], free[:2])
            else:
                parts_c = (a[RX - 3:], b[RX - 2:], free[RX - 2:])
            sc[j, pl.ds(0, 3)] = parts_c[0]
            sc[j, pl.ds(3, 2)] = parts_c[1]
            sc[j, pl.ds(5, 2)] = parts_c[2]
            sc[j, pl.ds(7, 1)] = parts_c[2][:1]

    def strided(ref, z0, row):
        return ref.at[pl.ds(z0 * EX + row, NZ, stride=EX)]

    fields = ((perm, 1), (pa, 1), (stor, 0), (rhs, 0), (gain, 0))
    for n, (f, d) in enumerate(PLANES):
        ref, z0 = fields[f]
        sx[0, n] = strided(ref, z0, d)[...]
        sx[1, n] = strided(ref, z0, RX - 1 - d)[...]

    def parts(i):
        if i < 2:
            return sx.at[i], rx, i
        if i < 4:
            return sy.at[i - 2], ry, i - 2
        return sc.at[i - 4], rc, i - 4

    def pieces(i, from_ref, dst, slot, spans, sems):
        return [
            pltpu.make_async_remote_copy(
                src_ref=from_ref.at[span], dst_ref=dst.at[slot, span], send_sem=sems[0].at[i],
                recv_sem=sems[1].at[OPPOSITE[i]], device_id=spots[i][0], device_id_type=MESH)
            for span in spans]

    def spans(length, parts_of):
        cuts = [length * n // parts_of for n in range(parts_of + 1)]
        return [pl.ds(a, b - a) for a, b in zip(cuts[:-1], cuts[1:])]

    def copy(i):
        from_ref, _, _ = parts(i)
        _, dst, slot = parts(OPPOSITE[i])
        cut = spans(len(PLANES), CUTS[0]) if i < 2 else spans(from_ref.shape[0], 1)
        return pieces(i, from_ref, dst, slot, cut, (send_sem, recv_sem))

    def arrival(i):
        from_ref, dst, slot = parts(i)
        return pltpu.make_async_remote_copy(
            src_ref=from_ref, dst_ref=dst.at[slot], send_sem=send_sem.at[i],
            recv_sem=recv_sem.at[i], device_id=spots[i][0], device_id_type=MESH)

    def sparts(i):
        return (ssx.at[i], rsx, i) if i < 2 else (ssy.at[i - 2], rsy, i - 2)

    def scopy(i):
        from_ref, _, _ = sparts(i)
        _, dst, slot = sparts(OPPOSITE[i])
        cut = spans(NSPEC, CUTS[1]) if i < 2 else spans(NZ, 1)
        return pieces(i, from_ref, dst, slot, cut, (s_send, s_recv))

    def sarrival(i):
        from_ref, dst, slot = sparts(i)
        return pltpu.make_async_remote_copy(
            src_ref=from_ref, dst_ref=dst.at[slot], send_sem=s_send.at[i],
            recv_sem=s_recv.at[i], device_id=spots[i][0], device_id_type=MESH)

    def send(only, order, make):
        for i in order:
            @pl.when(spots[i][1] & only)
            def _():
                for c in make(i):
                    c.start()

    inner = jnp.logical_not(at_seam)

    @pl.when(at_hi)
    def _():
        pl.semaphore_wait(barrier, expected)
    send(at_hi, (2, 4, 5), copy)

    loads[6].wait()
    for s in range(NSPEC):
        ssx[0, s] = sp[s, pl.ds(0, NZ, stride=RX)]
        ssx[1, s] = sp[s, pl.ds(RX - 1, NZ, stride=RX)]
    pair = lax.shift_right_logical(lane, 1)
    odd = (lane & 1) == 1

    halves = [zero, zero]
    for x in range(RX):
        for s in range(NSPEC):
            m = (x % 8) * 8 + s
            turned = lanes(sp[s, pl.ds(x, NZ, stride=RX)], 2 * m + 1)
            halves[x // 8] = jnp.where(pair == m, turned, halves[x // 8])
    lo, hi = halves
    ssy[0] = jnp.where(odd, lo, lanes(hi, -1))
    ssy[1] = jnp.where(odd, lanes(hi, 1), lo)
    send(at_hi, (2,), scopy)

    @pl.when(inner)
    def _():
        pl.semaphore_wait(barrier, expected)
    for edge_row, toward in ((seam - 2, 1), (seam + 1, -1)):
        @pl.when((gy == edge_row) & split)
        def _():
            pl.semaphore_signal(ready, inc=1, device_id=(gx, gy + toward), device_id_type=MESH)

    @pl.when(at_seam)
    def _():
        pl.semaphore_wait(ready, 1)
    later = lax.rem(gx, 16) == 14
    soon = jnp.logical_not(later)
    send(True, (1,), copy)
    send(soon, (0,), copy)
    send(inner | at_lo, (2, 4, 5), copy)
    send(inner | at_hi, (3, 6, 7), copy)

    send(True, (1,), scopy)
    send(soon, (0,), scopy)
    send(inner | at_lo, (2,), scopy)
    send(inner | at_hi, (3,), scopy)

    for s in range(NSPEC):
        for x in range(RX):
            c = sp[s, pl.ds(x, NZ, stride=RX)]
            spx[s, pl.ds(NZ * (x + 1), NZ)] = c
            left[s, pl.ds(NZ * x, NZ)] = lanes(c, 1)
            right[s, pl.ds(NZ * x, NZ)] = lanes(c, -1)

    def face_x(r):
        tx[r % EX] = harmonic(perm[plane_at(r)], perm[plane_at(r - 1)])

    def in_plane(r):
        k = perm[plane_at(r)]
        ty[0, r % EX] = jnp.where(lane > 0, harmonic(k, lanes(k, 1)), 0.0)
        ty[1, r % EX] = jnp.where(lane < LY - 1, harmonic(k, lanes(k, -1)), 0.0)
        tz[0, r % EX] = harmonic(k, perm[plane_at(r, -1)])
        tz[1, r % EX] = harmonic(k, perm[plane_at(r, 1)])

    def coefficients(r):
        at_r = r % EX
        s = stor[plane_at(r, -1)]
        total = (s + tx[at_r] + tx[(r + 1) % EX]) + (ty[0, at_r] + ty[1, at_r]) + (tz[0, at_r] + tz[1, at_r])
        step[at_r] = gain[plane_at(r, -1)] * inverse(jnp.maximum(total, TINY))
        known[at_r] = s * pa[plane_at(r)] + rhs[plane_at(r, -1)]

    def relax(it, r):
        now, new, at_r = levels[it], levels[it + 1], r % EX
        p = now[plane_at(r)]
        out = stor[plane_at(r, -1)] * p
        out = out + tx[at_r] * (p - now[plane_at(r - 1)])
        out = out + tx[(r + 1) % EX] * (p - now[plane_at(r + 1)])
        out = out + tz[0, at_r] * (p - now[plane_at(r, -1)])
        out = out + tz[1, at_r] * (p - now[plane_at(r, 1)])
        out = out + ty[0, at_r] * (p - lanes(p, 1))
        out = out + ty[1, at_r] * (p - lanes(p, -1))
        new[plane_at(r)] = p + F32(relax_weight(it)) * step[at_r] * (known[at_r] - out)

    levels = (pa, p1, p2, pd)
    for r in range(1, RX):
        face_x(r)
    for r in range(RX):
        in_plane(r)
    for r in range(1, RX - 1):
        coefficients(r)
    for it in range(SWEEPS):
        for r in range(1 + it, RX - 1 - it):
            relax(it, r)

    send(later, (0,), copy)
    send(later, (0,), scopy)

    @pl.when(at_lo)
    def _():
        pl.semaphore_wait(barrier, expected)
    send(at_lo, (3, 6, 7), copy)
    send(at_lo, (3,), scopy)

    for i in range(2):
        @pl.when(spots[i][1])
        def _():
            arrival(i).wait_recv()
    for n, (f, d) in enumerate(PLANES):
        ref, z0 = fields[f]
        strided(ref, z0, RX + d)[...] = rx[1, n]
        strided(ref, z0, EX - 1 - d)[...] = rx[0, n]
    for r in (-3, -2, -1, 0, RX, RX + 1, RX + 2, RX + 3):
        face_x(r)
    for r in (-3, -2, -1, RX, RX + 1, RX + 2):
        in_plane(r)
    for r in (-3, -2, -1, 0, RX - 1, RX, RX + 1, RX + 2):
        coefficients(r)
    for it in range(SWEEPS):
        for j in range(4):
            relax(it, it - 3 + j)
            relax(it, RX - 1 - it + j)

    lane24 = iota(EX, 1)
    group8 = lax.shift_right_logical(iota(8, 1), 3)
    tails, tail_fed, fed_1, fed_2 = [zero8] * FIELDS, [zero8] * 2, [zero8] * 3, [zero8] * 3
    for z in range(NZ):
        mask = feed_mask(z)
        for f, (ref, z0) in enumerate(fields):
            turned = lanes(ref[at(z + z0, 8, RX)], 8 * z + 4)
            tails[f] = jnp.where(group8 == z, turned, tails[f])
            if f < 2:
                tail_fed[f] = jnp.where(mask, turned, tail_fed[f])
        for ref, pack in ((p1, fed_1), (p2, fed_2)):
            for t in range(3):
                pack[t] = jnp.where(mask, lanes(ref[at(z + 1, 8, 8 * t)], 8 * z + 4), pack[t])
    whole = [jnp.concatenate([a, b], axis=0) for a, b in zip(packs, tails)]
    fed_k = jnp.concatenate([own_fed[0], own_fed[1], tail_fed[0]], axis=0)
    fed = [
        jnp.concatenate([own_fed[2], own_fed[3], tail_fed[1]], axis=0),
        jnp.concatenate(fed_1, axis=0), jnp.concatenate(fed_2, axis=0),
    ]

    for i in range(2, 8):
        @pl.when(spots[i][1])
        def _():
            arrival(i).wait_recv()

    column = lane24 & 7
    low24 = column < 4
    pad2, pad4 = jnp.zeros((2, LY), F32), jnp.zeros((4, LY), F32)
    strips = []
    for d in range(2):
        minus, plus = rc.at[2 * d], rc.at[2 * d + 1]
        a = jnp.concatenate([ry[d, pl.ds(0, RX)], plus[pl.ds(0, 3)], pad2, minus[pl.ds(0, 3)]], axis=0)
        b = jnp.concatenate([ry[d, pl.ds(RX, RX)], plus[pl.ds(3, 2)], pad4, minus[pl.ds(3, 2)]], axis=0)
        m = ry[d, pl.ds(2 * RX, 8)]
        m_tail = [plus[pl.ds(5, 2)], pad4, minus[pl.ds(5, 2)]]
        if d == 0:
            halos = (a, lanes(a, -4), b, lanes(b, -4), jnp.concatenate([m, lanes(m, -4)] + m_tail, axis=0))
        else:
            halos = (lanes(a, 4), a, lanes(b, 4), b, jnp.concatenate([lanes(m, 4), m] + m_tail, axis=0))
        k, p, s, q, free = (
            jnp.where(low24, h, w) if d == 0 else jnp.where(low24, w, h) for h, w in zip(halos, whole))
        end = column == (7 if d == 0 else 0)
        turn = -1 if d == 0 else 1
        beyond = [lanes(v, turn) for v in [fed_k] + fed]

        def sides(v, outer_v):
            lo, hi = lanes(v, 1), lanes(v, -1)
            if d == 0:
                hi = jnp.where(end, outer_v, hi)
            else:
                lo = jnp.where(end, outer_v, lo)
            return before(v), after(v), lo, hi, lanes(v, 8), lanes(v, -8)

        terms = [harmonic(k, v) for v in sides(k, beyond[0])]
        terms[4] = jnp.where(lane24 < 8, 0.0, terms[4])
        terms[5] = jnp.where(lane24 < LY - 8, terms[5], 0.0)
        total = s + ((terms[0] + terms[1]) + (terms[2] + terms[3])) + (terms[4] + terms[5])
        g = free * inverse(jnp.maximum(total, TINY))
        right_side = s * p + q
        for it in range(SWEEPS):
            flows = [t * (p - v) for t, v in zip(terms, sides(p, beyond[1 + it]))]
            r = (right_side - s * p) - ((flows[0] + flows[1]) + (flows[2] + flows[3])) - (flows[4] + flows[5])
            p = p + F32(relax_weight(it)) * g * r
        across = terms[2] * (p - lanes(p, 1)) if d == 0 else terms[3] * (p - lanes(p, -1))
        strips.append((across, p))
    own_edge = jnp.where(low24, strips[1][1], strips[0][1])
    own_flow = jnp.where(low24, strips[1][0], strips[0][0])
    outer = (lane24 < 3) | (lane24 > LY - 4)
    for z in range(NZ):
        pd[at(z + 1)] = jnp.where(outer, lanes(own_edge, -(8 * z + 4)), pd[at(z + 1)])
        cross[at(z, RX)] = lanes(own_flow[:RX], -(8 * z + 4))

    first, last = lane == 0, lane == LY - 1
    for x in range(RX):
        p = pd[plane_at(x)]
        final[pl.ds(x, NZ, stride=RX)] = p
        through = cross[plane_at(x, -1)]
        flows = [
            tx[x] * (p - pd[plane_at(x - 1)]),
            tx[x + 1] * (p - pd[plane_at(x + 1)]),
            jnp.where(first, through, ty[0, x] * (p - lanes(p, 1))),
            jnp.where(last, through, ty[1, x] * (p - lanes(p, -1))),
            tz[0, x] * (p - pd[plane_at(x, -1)]),
            tz[1, x] * (p - pd[plane_at(x, 1)]),
        ]
        scale = TIME_STEP * inverse(phi[pl.ds(x, NZ, stride=RX)])
        out = [jnp.maximum(f, 0.0) for f in flows]
        out = ((out[0] + out[1]) + (out[2] + out[3])) + (out[4] + out[5])
        weight[0, x] = 1.0 - scale * out
        for n, f in enumerate(flows):
            weight[n + 1, x] = -scale * jnp.minimum(f, 0.0)

    for i in range(4):
        @pl.when(spots[i][1])
        def _():
            sarrival(i).wait_recv()
    m_lo, m_hi = rsy[0], rsy[1]
    side[0] = jnp.where(odd, lanes(m_lo, 1), lanes(m_hi, -1))
    side[1] = jnp.where(odd, m_lo, m_hi)
    for s in range(NSPEC):
        spx[s, pl.ds(0, NZ)] = rsx[0, s]
        spx[s, pl.ds(NZ * (RX + 1), NZ)] = rsx[1, s]
    for i in range(8):
        @pl.when(spots[i][1])
        def _():
            arrival(i).wait_send()
            if i < 4:
                sarrival(i).wait_send()


def transport_kernel(spx, left, right, phi, rea, final, weight, side, conc_out, p_out, phi_out, conc, sem):
    outs = [pltpu.make_async_copy(phi, phi_out, sem.at[0]), pltpu.make_async_copy(final, p_out, sem.at[1])]
    for c in outs:
        c.start()
    lane = iota(RX, 1)
    first, last = lane == 0, lane == LY - 1
    group = 2
    for s0 in range(0, NSPEC, group):
        for x in range(RX):
            w = [weight[n, x] for n in range(7)]
            for s in range(s0, s0 + group):
                def row(shift):
                    return spx[s, pl.ds(NZ * (x + 1) + shift, NZ)]

                turned = lanes(side[x // 8], -(2 * ((x % 8) * 8 + s) + 1))
                around = [
                    row(-NZ), row(NZ),
                    jnp.where(first, turned, left[s, pl.ds(NZ * x, NZ)]),
                    jnp.where(last, turned, right[s, pl.ds(NZ * x, NZ)]),
                    row(-1), row(1),
                ]
                total = row(0) * w[0]
                for a, b in zip(w[1:], around):
                    total = total + a * b
                if STOICHIOMETRY[s]:
                    total = total + STOICHIOMETRY[s] * rea[pl.ds(x, NZ, stride=RX)]
                conc[s, pl.ds(x, NZ, stride=RX)] = total
        some = pl.ds(s0, group)
        c = pltpu.make_async_copy(conc.at[some], conc_out.at[some], sem.at[2 + s0 // group])
        c.start()
        outs.append(c)
    for c in outs:
        c.wait()


def build(sizes):
    tile, rows = (NZ, RX, LY), (NZ * RX, LY)
    flat, padded, planes = (NZ * EX, LY), ((NZ + 2) * EX, LY), (EX, NZ, LY)
    species, turned = (NSPEC, NZ, RX, LY), (NSPEC, NZ * RX, LY)
    halo = [
        (2, len(PLANES), NZ, LY), (2, 2 * RX + 8, LY), (4, 8, LY), (2, NSPEC, NZ, LY), (2, NZ, LY),
    ]
    vmem = pl.BlockSpec(memory_space=pltpu.VMEM)
    hbm = pl.BlockSpec(memory_space=pltpu.HBM)
    middle = [
        (NSPEC, (RX + 2) * NZ, LY), turned, turned, rows, rows, rows, (7, RX, NZ, LY), (2, NZ, LY),
    ]
    dma = pltpu.SemaphoreType.DMA

    def shards(sp, *args):
        args = [pltpu.with_memory_space_constraint(a, pltpu.HBM) for a in (sp.reshape(turned), *args)]
        shared = pl.pallas_call(
            lambda *refs: flow_kernel(sizes, *refs),
            out_shape=[pltpu.VMEM(shape, F32) for shape in middle],
            in_specs=[hbm] * 6,
            out_specs=[vmem] * len(middle),
            scratch_shapes=[
                pltpu.VMEM(padded, F32), pltpu.VMEM(planes, F32), pltpu.VMEM((2,) + planes, F32),
                pltpu.VMEM((2,) + planes, F32), pltpu.VMEM(flat, F32), pltpu.VMEM(turned, F32),
                pltpu.VMEM(tile, F32), pltpu.VMEM(tile, jnp.int32), pltpu.VMEM(tile, jnp.int32),
                pltpu.VMEM(tile, F32), pltpu.VMEM(tile, F32),
                *[pltpu.VMEM(padded, F32)] * 4, *[pltpu.VMEM(flat, F32)] * 3, *[pltpu.VMEM(planes, F32)] * 2,
                *[pltpu.VMEM(shape, F32) for shape in halo + halo],
                dma((7,)), dma((8,)), dma((8,)), dma((4,)), dma((4,)), pltpu.SemaphoreType.REGULAR,
            ],
            compiler_params=pltpu.CompilerParams(
                collective_id=0, has_side_effects=True, vmem_limit_bytes=32 * 2**20),
            name="flow",
        )(*args)
        conc, pressure, porosity = pl.pallas_call(
            transport_kernel,
            out_shape=[jax.ShapeDtypeStruct(s, F32) for s in (turned, rows, rows)],
            in_specs=[vmem] * len(middle),
            out_specs=[hbm] * 3,
            scratch_shapes=[pltpu.VMEM(turned, F32), dma((6,))],
            compiler_params=pltpu.CompilerParams(vmem_limit_bytes=16 * 2**20),
            name="transport",
        )(*shared)
        return conc.reshape(species), pressure.reshape(tile), porosity.reshape(tile)

    return shards


def solution(mesh):
    specs = (P(None, None, "gx", "gy"),) + (P(None, "gx", "gy"),) * 5
    outs = (P(None, None, "gx", "gy"), P(None, "gx", "gy"), P(None, "gx", "gy"))
    sizes = (mesh.shape["gx"], mesh.shape["gy"])
    return jax.shard_map(build(sizes), mesh=mesh, in_specs=specs, out_specs=outs, check_vma=False)
```

```python
import math

import jax
import jax.numpy as jnp
from jax import lax
from jax.experimental import pallas as pl
from jax.experimental.pallas import tpu as pltpu
from jax.sharding import PartitionSpec as P

SWEEPS = 3
NSPEC, NZ, RX, LY = 8, 16, 16, 128
EX = RX + 8
FIELDS = 5
TINY = 1e-30
CUTS = (1, 1)
PLANES = [(f, d) for f in range(FIELDS) for d in range(4 if f < 2 else 3)]

ZONE_RATES = (0.02, 0.05, 0.1, 0.2)
ZONE_PERMEABILITY = (5.0, 10.0, 20.0, 40.0)
SOLUBILITY = 0.5
MOLAR_VOLUME = 0.05
STORAGE_COEF = 0.2
TIME_STEP = 0.2
CHEB_SPREAD = 0.92
STOICHIOMETRY = (-1.0, -1.0, 0.0, 0.0, 0.0, 0.0, 0.0, 0.0)

F32 = jnp.float32
MESH = pl.DeviceIdType.MESH
DIRS = ((-1, 0), (1, 0), (0, -1), (0, 1), (-1, -1), (1, -1), (-1, 1), (1, 1))
OPPOSITE = tuple(DIRS.index((-a, -b)) for a, b in DIRS)


def relax_weight(iteration):
    return 1.0 / (1.0 + CHEB_SPREAD * math.cos(math.pi * (2 * iteration + 1) / (2 * SWEEPS)))


def lookup(labels, table):
    out = jnp.where(labels == 0, F32(table[0]), F32(table[1]))
    out = jnp.where(labels == 2, F32(table[2]), out)
    return jnp.where(labels == 3, F32(table[3]), out)


def inverse(x):
    guess = pl.reciprocal(x, approx=True)
    return guess * (2.0 - x * guess)


def harmonic(a, b):
    return (2.0 * a * b) * inverse(jnp.maximum(a + b, TINY))


def lanes(x, shift):
    return pltpu.roll(x, shift % LY if isinstance(shift, int) else lax.rem(shift + 2 * LY, LY), 1)


def before(x):
    return pltpu.roll(x, 1, 0)


def after(x):
    return pltpu.roll(x, x.shape[0] - 1, 0)


def iota(rows, dim):
    return lax.broadcasted_iota(jnp.int32, (rows, LY), dim)


def flow_kernel(sizes, sp_in, por_in, old_in, src_in, zone_in, fix_in,
                spx, left, right, phi, rea, final, weight, side,
                pd, tx, ty, tz, cross, sp, por, zone, fix, old, src, pa, p1, p2, perm, stor, rhs, gain, step, known,
                sx, sy, sc, ssx, ssy, rx, ry, rc, rsx, rsy,
                in_sem, send_sem, recv_sem, s_send, s_recv, ready):
    gx, gy = lax.axis_index("gx"), lax.axis_index("gy")
    spots = []
    for dx, dy in DIRS:
        there = None
        for here, move, size in ((gx, dx, sizes[0]), (gy, dy, sizes[1])):
            if move:
                ok = here > 0 if move < 0 else here < size - 1
                there = ok if there is None else there & ok
        spots.append(((gx + dx, gy + dy), there))

    loads = [
        pltpu.make_async_copy(sp_in.at[pl.ds(0, 2)], sp.at[pl.ds(0, 2)], in_sem.at[0]),
        pltpu.make_async_copy(zone_in, zone, in_sem.at[1]),
        pltpu.make_async_copy(por_in, por, in_sem.at[2]),
        pltpu.make_async_copy(old_in, old, in_sem.at[3]),
        pltpu.make_async_copy(src_in, src, in_sem.at[4]),
        pltpu.make_async_copy(fix_in, fix, in_sem.at[5]),
        pltpu.make_async_copy(sp_in.at[pl.ds(2, NSPEC - 2)], sp.at[pl.ds(2, NSPEC - 2)], in_sem.at[6]),
    ]
    for c in loads:
        c.start()

    seam = sizes[1] // 2
    split = jnp.bool_(sizes[1] >= 4)
    at_lo, at_hi = (gy == seam - 1) & split, (gy == seam) & split
    at_seam = at_lo | at_hi
    barrier = pltpu.get_barrier_semaphore()
    expected = 0
    for i, (where, there) in enumerate(spots):
        far = (at_lo & (DIRS[i][1] > 0)) | (at_hi & (DIRS[i][1] < 0))
        counts = split & ((where[1] == seam - 1) | (where[1] == seam))
        beside = there & (far | jnp.logical_not(counts))

        @pl.when(beside)
        def _():
            pl.semaphore_signal(barrier, inc=1, device_id=where, device_id_type=MESH)
        expected = expected + (there & (far | jnp.logical_not(at_seam))).astype(jnp.int32)

    for i in range(8):
        @pl.when(jnp.logical_not(spots[i][1]))
        def _():
            if i < 2:
                rx[i] = jnp.zeros(rx.shape[1:], F32)
                rsx[i] = jnp.zeros(rsx.shape[1:], F32)
            elif i < 4:
                ry[i - 2] = jnp.zeros(ry.shape[1:], F32)
                rsy[i - 2] = jnp.zeros(rsy.shape[1:], F32)
            else:
                rc[i - 4] = jnp.zeros(rc.shape[1:], F32)
    plane = jnp.zeros((EX, LY), F32)
    for ref in (perm, pa, p1, p2, pd):
        ref[pl.ds(0, EX)] = plane
        ref[pl.ds((NZ + 1) * EX, EX)] = plane
    for ref in (stor, rhs, gain):
        for z in range(NZ):
            ref[pl.ds(z * EX + RX, 8)] = plane[:8]

    lane = iota(RX, 1)
    group = lax.shift_right_logical(lane, 3)
    low = (lane & 7) < 4
    for c in loads[:6]:
        c.wait()

    def at(z, rows=EX, skip=0):
        return pl.ds(pl.multiple_of(z * EX + skip, 8), rows)

    def plane_at(r, up=0):
        return pl.ds((1 + up) * EX + r % EX, NZ, stride=EX)

    def feed_mask(z):
        spot = (iota(8, 1) - 8 * z) & (LY - 1)
        return (spot == 8) | (spot == LY - 1)

    def own(z, packs):
        rows = pl.ds(pl.multiple_of(z * RX, 8), RX)
        c0, c1 = sp[0, rows], sp[1, rows]
        label = zone[z]
        reaction = lookup(label, ZONE_RATES) * (c0 * c1 - SOLUBILITY)
        new = por[z] - MOLAR_VOLUME * reaction
        solid = 1.0 - new
        k = lookup(label, ZONE_PERMEABILITY) * (new * new * new) * inverse(solid * solid)
        s = STORAGE_COEF * new
        free = 1.0 - fix[z].astype(F32)
        p, q = old[z], src[z]
        rea[rows] = reaction
        phi[rows] = new
        perm[at(z + 1, RX)] = k
        pa[at(z + 1, RX)] = p
        stor[at(z, RX)] = s
        rhs[at(z, RX)] = q
        gain[at(z, RX)] = free
        turned = [lanes(v, 8 * z + 4) for v in (k, p, s, q, free)]
        mask = feed_mask(z)
        fed_new = [jnp.where(mask, turned[f][8 * t:8 * t + 8], packs[FIELDS + 2 * f + t]) for f in range(2) for t in range(2)]
        return tuple(jnp.where(group == z, v, pack) for v, pack in zip(turned, packs)) + tuple(fed_new)

    zero, zero8 = jnp.zeros((RX, LY), F32), jnp.zeros((8, LY), F32)
    packs = lax.fori_loop(0, NZ, own, (zero,) * FIELDS + (zero8,) * 4, unroll=NZ)
    own_fed = packs[FIELDS:]
    packs = packs[:FIELDS]
    k, p, s, q, free = packs
    low8 = low[:8]
    y_edges = []
    for side_y in range(2):
        if side_y == 0:
            a, b = jnp.where(low, lanes(k, -4), p), jnp.where(low, lanes(s, -4), q)
            m = jnp.where(low8, lanes(free[:8], -4), free[8:])
        else:
            a, b = jnp.where(low, k, lanes(p, 4)), jnp.where(low, s, lanes(q, 4))
            m = jnp.where(low8, free[:8], lanes(free[8:], 4))
        sy[side_y, pl.ds(0, RX)] = a
        sy[side_y, pl.ds(RX, RX)] = b
        sy[side_y, pl.ds(2 * RX, 8)] = m
        y_edges.append((a, b))

    def parts(i):
        if i < 2:
            return sx.at[i], rx, i
        if i < 4:
            return sy.at[i - 2], ry, i - 2
        return sc.at[i - 4], rc, i - 4

    def pieces(i, from_ref, dst, slot, spans, sems):
        return [
            pltpu.make_async_remote_copy(
                src_ref=from_ref.at[span], dst_ref=dst.at[slot, span], send_sem=sems[0].at[i],
                recv_sem=sems[1].at[OPPOSITE[i]], device_id=spots[i][0], device_id_type=MESH)
            for span in spans]

    def spans(length, parts_of):
        cuts = [length * n // parts_of for n in range(parts_of + 1)]
        return [pl.ds(a, b - a) for a, b in zip(cuts[:-1], cuts[1:])]

    def copy(i):
        from_ref, _, _ = parts(i)
        _, dst, slot = parts(OPPOSITE[i])
        cut = spans(len(PLANES), CUTS[0]) if i < 2 else spans(from_ref.shape[0], 1)
        return pieces(i, from_ref, dst, slot, cut, (send_sem, recv_sem))

    def arrival(i):
        from_ref, dst, slot = parts(i)
        return pltpu.make_async_remote_copy(
            src_ref=from_ref, dst_ref=dst.at[slot], send_sem=send_sem.at[i],
            recv_sem=recv_sem.at[i], device_id=spots[i][0], device_id_type=MESH)

    def sparts(i):
        return (ssx.at[i], rsx, i) if i < 2 else (ssy.at[i - 2], rsy, i - 2)

    def scopy(i):
        from_ref, _, _ = sparts(i)
        _, dst, slot = sparts(OPPOSITE[i])
        cut = spans(NSPEC, CUTS[1]) if i < 2 else spans(NZ, 1)
        return pieces(i, from_ref, dst, slot, cut, (s_send, s_recv))

    def sarrival(i):
        from_ref, dst, slot = sparts(i)
        return pltpu.make_async_remote_copy(
            src_ref=from_ref, dst_ref=dst.at[slot], send_sem=s_send.at[i],
            recv_sem=s_recv.at[i], device_id=spots[i][0], device_id_type=MESH)

    def send(only, order, make):
        for i in order:
            @pl.when(spots[i][1] & only)
            def _():
                for c in make(i):
                    c.start()

    inner = jnp.logical_not(at_seam)


    @pl.when(at_hi)
    def _():
        pl.semaphore_wait(barrier, expected)
    send(at_hi, (2,), copy)

    slot = iota(1, 1) & 7
    half = slot & 3
    for side_y, (a, b) in enumerate(y_edges):
        far_slot = half == (3 if side_y == 0 else 0)
        back = 3 if side_y == 0 else -3
        for side_x in range(2):
            a1, a2, a3 = (v[r:r + 1] for v, r in zip((a,) * 3, (0, 1, 2) if side_x == 0 else (RX - 1, RX - 2, RX - 3)))
            b1, b2, f1, f2 = (
                v[r:r + 1] for v, r in zip((b, b, free, free), (0, 1) * 2 if side_x == 0 else (RX - 1, RX - 2) * 2))
            j = 2 * side_y + side_x
            sc[j, pl.ds(0, 1)] = jnp.where(far_slot, lanes(a3, back), a1)
            sc[j, pl.ds(1, 1)] = jnp.where(far_slot, lanes(b2, back), a2)
            if side_y == 0:
                masks = jnp.where((slot == 2) | (slot == 3), lanes(f1, -2), jnp.where(slot == 6, lanes(f2, 2), b1))
            else:
                masks = jnp.where((slot == 0) | (slot == 1), lanes(f1, -2), jnp.where(slot == 4, lanes(f2, 1), b1))
            sc[j, pl.ds(2, 1)] = masks
            sc[j, pl.ds(3, 1)] = a1
    send(at_hi, (4, 5), copy)

    def strided(ref, z0, row):
        return ref.at[pl.ds(z0 * EX + row, NZ, stride=EX)]

    fields = ((perm, 1), (pa, 1), (stor, 0), (rhs, 0), (gain, 0))
    for n, (f, d) in enumerate(PLANES):
        ref, z0 = fields[f]
        sx[0, n] = strided(ref, z0, d)[...]
        sx[1, n] = strided(ref, z0, RX - 1 - d)[...]

    loads[6].wait()
    for s in range(NSPEC):
        ssx[0, s] = sp[s, pl.ds(0, NZ, stride=RX)]
        ssx[1, s] = sp[s, pl.ds(RX - 1, NZ, stride=RX)]
    pair = lax.shift_right_logical(lane, 1)
    odd = (lane & 1) == 1

    halves = [zero, zero]
    for x in range(RX):
        for s in range(NSPEC):
            m = (x % 8) * 8 + s
            turned = lanes(sp[s, pl.ds(x, NZ, stride=RX)], 2 * m + 1)
            halves[x // 8] = jnp.where(pair == m, turned, halves[x // 8])
    lo, hi = halves
    ssy[0] = jnp.where(odd, lo, lanes(hi, -1))
    ssy[1] = jnp.where(odd, lanes(hi, 1), lo)
    send(at_hi, (2,), scopy)

    @pl.when(inner)
    def _():
        pl.semaphore_wait(barrier, expected)
    for edge_row, toward in ((seam - 2, 1), (seam + 1, -1)):
        @pl.when((gy == edge_row) & split)
        def _():
            pl.semaphore_signal(ready, inc=1, device_id=(gx, gy + toward), device_id_type=MESH)

    @pl.when(at_seam)
    def _():
        pl.semaphore_wait(ready, 1)
    later = lax.rem(gx, 16) == 14
    soon = jnp.logical_not(later)
    send(True, (1,), copy)
    send(soon, (0,), copy)
    send(inner | at_lo, (2, 4, 5), copy)
    send(inner | at_hi, (3, 6, 7), copy)

    send(True, (1,), scopy)
    send(soon, (0,), scopy)
    send(inner | at_lo, (2,), scopy)
    send(inner | at_hi, (3,), scopy)

    for s in range(NSPEC):
        for x in range(RX):
            c = sp[s, pl.ds(x, NZ, stride=RX)]
            spx[s, pl.ds(NZ * (x + 1), NZ)] = c
            left[s, pl.ds(NZ * x, NZ)] = lanes(c, 1)
            right[s, pl.ds(NZ * x, NZ)] = lanes(c, -1)

    def face_x(r):
        tx[r % EX] = harmonic(perm[plane_at(r)], perm[plane_at(r - 1)])

    def in_plane(r):
        k = perm[plane_at(r)]
        ty[0, r % EX] = jnp.where(lane > 0, harmonic(k, lanes(k, 1)), 0.0)
        ty[1, r % EX] = jnp.where(lane < LY - 1, harmonic(k, lanes(k, -1)), 0.0)
        tz[0, r % EX] = harmonic(k, perm[plane_at(r, -1)])
        tz[1, r % EX] = harmonic(k, perm[plane_at(r, 1)])

    def coefficients(r):
        at_r = r % EX
        s = stor[plane_at(r, -1)]
        total = (s + tx[at_r] + tx[(r + 1) % EX]) + (ty[0, at_r] + ty[1, at_r]) + (tz[0, at_r] + tz[1, at_r])
        step[at_r] = gain[plane_at(r, -1)] * inverse(jnp.maximum(total, TINY))
        known[at_r] = s * pa[plane_at(r)] + rhs[plane_at(r, -1)]

    def relax(it, r):
        now, new, at_r = levels[it], levels[it + 1], r % EX
        p = now[plane_at(r)]
        out = stor[plane_at(r, -1)] * p
        out = out + tx[at_r] * (p - now[plane_at(r - 1)])
        out = out + tx[(r + 1) % EX] * (p - now[plane_at(r + 1)])
        out = out + tz[0, at_r] * (p - now[plane_at(r, -1)])
        out = out + tz[1, at_r] * (p - now[plane_at(r, 1)])
        out = out + ty[0, at_r] * (p - lanes(p, 1))
        out = out + ty[1, at_r] * (p - lanes(p, -1))
        new[plane_at(r)] = p + F32(relax_weight(it)) * step[at_r] * (known[at_r] - out)

    levels = (pa, p1, p2, pd)
    for r in range(1, RX):
        face_x(r)
    for r in range(RX):
        in_plane(r)
    for r in range(1, RX - 1):
        coefficients(r)
    for it in range(SWEEPS):
        for r in range(1 + it, RX - 1 - it):
            relax(it, r)

    send(later, (0,), copy)
    send(later, (0,), scopy)

    @pl.when(at_lo)
    def _():
        pl.semaphore_wait(barrier, expected)
    send(at_lo, (3, 6, 7), copy)
    send(at_lo, (3,), scopy)

    for i in range(2):
        @pl.when(spots[i][1])
        def _():
            arrival(i).wait_recv()
    for n, (f, d) in enumerate(PLANES):
        ref, z0 = fields[f]
        strided(ref, z0, RX + d)[...] = rx[1, n]
        strided(ref, z0, EX - 1 - d)[...] = rx[0, n]
    for r in (-3, -2, -1, 0, RX, RX + 1, RX + 2, RX + 3):
        face_x(r)
    for r in (-3, -2, -1, RX, RX + 1, RX + 2):
        in_plane(r)
    for r in (-3, -2, -1, 0, RX - 1, RX, RX + 1, RX + 2):
        coefficients(r)
    for it in range(SWEEPS):
        for j in range(4):
            relax(it, it - 3 + j)
            relax(it, RX - 1 - it + j)

    lane24 = iota(EX, 1)
    group8 = lax.shift_right_logical(iota(8, 1), 3)
    tails, tail_fed, fed_1, fed_2 = [zero8] * FIELDS, [zero8] * 2, [zero8] * 3, [zero8] * 3
    for z in range(NZ):
        mask = feed_mask(z)
        for f, (ref, z0) in enumerate(fields):
            turned = lanes(ref[at(z + z0, 8, RX)], 8 * z + 4)
            tails[f] = jnp.where(group8 == z, turned, tails[f])
            if f < 2:
                tail_fed[f] = jnp.where(mask, turned, tail_fed[f])
        for ref, pack in ((p1, fed_1), (p2, fed_2)):
            for t in range(3):
                pack[t] = jnp.where(mask, lanes(ref[at(z + 1, 8, 8 * t)], 8 * z + 4), pack[t])
    whole = [jnp.concatenate([a, b], axis=0) for a, b in zip(packs, tails)]
    fed_k = jnp.concatenate([own_fed[0], own_fed[1], tail_fed[0]], axis=0)
    fed = [
        jnp.concatenate([own_fed[2], own_fed[3], tail_fed[1]], axis=0),
        jnp.concatenate(fed_1, axis=0), jnp.concatenate(fed_2, axis=0),
    ]

    for i in range(2, 8):
        @pl.when(spots[i][1])
        def _():
            arrival(i).wait_recv()

    column = lane24 & 7
    low24 = column < 4
    pad2, pad4 = jnp.zeros((2, LY), F32), jnp.zeros((4, LY), F32)
    strips = []
    for d in range(2):
        minus, plus = rc.at[2 * d], rc.at[2 * d + 1]
        def corner(ref):
            x, y, z = (ref[pl.ds(n, 1)] for n in range(3))
            if d == 0:
                return (x, y, lanes(x, 3)), (z, lanes(y, 3)), (lanes(z, 2), lanes(z, -1))
            return (x, y, lanes(x, -3)), (z, lanes(y, -3)), (lanes(z, 2), lanes(z, -2))

        (pa1, pa2, pa3), (pb1, pb2), (pm1, pm2) = corner(plus)
        (ma1, ma2, ma3), (mb1, mb2), (mm1, mm2) = corner(minus)
        a = jnp.concatenate([ry[d, pl.ds(0, RX)], pa1, pa2, pa3, pad2, ma3, ma2, ma1], axis=0)
        b = jnp.concatenate([ry[d, pl.ds(RX, RX)], pb1, pb2, pad4, mb2, mb1], axis=0)
        m = ry[d, pl.ds(2 * RX, 8)]
        m_tail = [pm1, pm2, pad4, mm2, mm1]
        if d == 0:
            halos = (a, lanes(a, -4), b, lanes(b, -4), jnp.concatenate([m, lanes(m, -4)] + m_tail, axis=0))
        else:
            halos = (lanes(a, 4), a, lanes(b, 4), b, jnp.concatenate([lanes(m, 4), m] + m_tail, axis=0))
        k, p, s, q, free = (
            jnp.where(low24, h, w) if d == 0 else jnp.where(low24, w, h) for h, w in zip(halos, whole))
        end = column == (7 if d == 0 else 0)
        turn = -1 if d == 0 else 1
        beyond = [lanes(v, turn) for v in [fed_k] + fed]

        def sides(v, outer_v):
            lo, hi = lanes(v, 1), lanes(v, -1)
            if d == 0:
                hi = jnp.where(end, outer_v, hi)
            else:
                lo = jnp.where(end, outer_v, lo)
            return before(v), after(v), lo, hi, lanes(v, 8), lanes(v, -8)

        terms = [harmonic(k, v) for v in sides(k, beyond[0])]
        terms[4] = jnp.where(lane24 < 8, 0.0, terms[4])
        terms[5] = jnp.where(lane24 < LY - 8, terms[5], 0.0)
        total = s + ((terms[0] + terms[1]) + (terms[2] + terms[3])) + (terms[4] + terms[5])
        g = free * inverse(jnp.maximum(total, TINY))
        right_side = s * p + q
        for it in range(SWEEPS):
            flows = [t * (p - v) for t, v in zip(terms, sides(p, beyond[1 + it]))]
            r = (right_side - s * p) - ((flows[0] + flows[1]) + (flows[2] + flows[3])) - (flows[4] + flows[5])
            p = p + F32(relax_weight(it)) * g * r
        across = terms[2] * (p - lanes(p, 1)) if d == 0 else terms[3] * (p - lanes(p, -1))
        strips.append((across, p))
    own_edge = jnp.where(low24, strips[1][1], strips[0][1])
    own_flow = jnp.where(low24, strips[1][0], strips[0][0])
    outer = (lane24 < 3) | (lane24 > LY - 4)
    for z in range(NZ):
        pd[at(z + 1)] = jnp.where(outer, lanes(own_edge, -(8 * z + 4)), pd[at(z + 1)])
        cross[at(z, RX)] = lanes(own_flow[:RX], -(8 * z + 4))

    first, last = lane == 0, lane == LY - 1
    for x in range(RX):
        p = pd[plane_at(x)]
        final[pl.ds(x, NZ, stride=RX)] = p
        through = cross[plane_at(x, -1)]
        flows = [
            tx[x] * (p - pd[plane_at(x - 1)]),
            tx[x + 1] * (p - pd[plane_at(x + 1)]),
            jnp.where(first, through, ty[0, x] * (p - lanes(p, 1))),
            jnp.where(last, through, ty[1, x] * (p - lanes(p, -1))),
            tz[0, x] * (p - pd[plane_at(x, -1)]),
            tz[1, x] * (p - pd[plane_at(x, 1)]),
        ]
        scale = TIME_STEP * inverse(phi[pl.ds(x, NZ, stride=RX)])
        out = [jnp.maximum(f, 0.0) for f in flows]
        out = ((out[0] + out[1]) + (out[2] + out[3])) + (out[4] + out[5])
        weight[0, x] = 1.0 - scale * out
        for n, f in enumerate(flows):
            weight[n + 1, x] = -scale * jnp.minimum(f, 0.0)

    for i in range(4):
        @pl.when(spots[i][1])
        def _():
            sarrival(i).wait_recv()
    m_lo, m_hi = rsy[0], rsy[1]
    side[0] = jnp.where(odd, lanes(m_lo, 1), lanes(m_hi, -1))
    side[1] = jnp.where(odd, m_lo, m_hi)
    for s in range(NSPEC):
        spx[s, pl.ds(0, NZ)] = rsx[0, s]
        spx[s, pl.ds(NZ * (RX + 1), NZ)] = rsx[1, s]
    for i in range(8):
        @pl.when(spots[i][1])
        def _():
            arrival(i).wait_send()
            if i < 4:
                sarrival(i).wait_send()


def transport_kernel(spx, left, right, phi, rea, final, weight, side, conc_out, p_out, phi_out, conc, sem):
    outs = [pltpu.make_async_copy(phi, phi_out, sem.at[0]), pltpu.make_async_copy(final, p_out, sem.at[1])]
    for c in outs:
        c.start()
    lane = iota(RX, 1)
    first, last = lane == 0, lane == LY - 1
    group = 2
    for s0 in range(0, NSPEC, group):
        for x in range(RX):
            w = [weight[n, x] for n in range(7)]
            for s in range(s0, s0 + group):
                def row(shift):
                    return spx[s, pl.ds(NZ * (x + 1) + shift, NZ)]

                turned = lanes(side[x // 8], -(2 * ((x % 8) * 8 + s) + 1))
                around = [
                    row(-NZ), row(NZ),
                    jnp.where(first, turned, left[s, pl.ds(NZ * x, NZ)]),
                    jnp.where(last, turned, right[s, pl.ds(NZ * x, NZ)]),
                    row(-1), row(1),
                ]
                total = row(0) * w[0]
                for a, b in zip(w[1:], around):
                    total = total + a * b
                if STOICHIOMETRY[s]:
                    total = total + STOICHIOMETRY[s] * rea[pl.ds(x, NZ, stride=RX)]
                conc[s, pl.ds(x, NZ, stride=RX)] = total
        some = pl.ds(s0, group)
        c = pltpu.make_async_copy(conc.at[some], conc_out.at[some], sem.at[2 + s0 // group])
        c.start()
        outs.append(c)
    for c in outs:
        c.wait()


def build(sizes):
    tile, rows = (NZ, RX, LY), (NZ * RX, LY)
    flat, padded, planes = (NZ * EX, LY), ((NZ + 2) * EX, LY), (EX, NZ, LY)
    species, turned = (NSPEC, NZ, RX, LY), (NSPEC, NZ * RX, LY)
    halo = [
        (2, len(PLANES), NZ, LY), (2, 2 * RX + 8, LY), (4, 4, LY), (2, NSPEC, NZ, LY), (2, NZ, LY),
    ]
    vmem = pl.BlockSpec(memory_space=pltpu.VMEM)
    hbm = pl.BlockSpec(memory_space=pltpu.HBM)
    middle = [
        (NSPEC, (RX + 2) * NZ, LY), turned, turned, rows, rows, rows, (7, RX, NZ, LY), (2, NZ, LY),
    ]
    dma = pltpu.SemaphoreType.DMA

    def shards(sp, *args):
        args = [pltpu.with_memory_space_constraint(a, pltpu.HBM) for a in (sp.reshape(turned), *args)]
        shared = pl.pallas_call(
            lambda *refs: flow_kernel(sizes, *refs),
            out_shape=[pltpu.VMEM(shape, F32) for shape in middle],
            in_specs=[hbm] * 6,
            out_specs=[vmem] * len(middle),
            scratch_shapes=[
                pltpu.VMEM(padded, F32), pltpu.VMEM(planes, F32), pltpu.VMEM((2,) + planes, F32),
                pltpu.VMEM((2,) + planes, F32), pltpu.VMEM(flat, F32), pltpu.VMEM(turned, F32),
                pltpu.VMEM(tile, F32), pltpu.VMEM(tile, jnp.int32), pltpu.VMEM(tile, jnp.int32),
                pltpu.VMEM(tile, F32), pltpu.VMEM(tile, F32),
                *[pltpu.VMEM(padded, F32)] * 4, *[pltpu.VMEM(flat, F32)] * 3, *[pltpu.VMEM(planes, F32)] * 2,
                *[pltpu.VMEM(shape, F32) for shape in halo + halo],
                dma((7,)), dma((8,)), dma((8,)), dma((4,)), dma((4,)), pltpu.SemaphoreType.REGULAR,
            ],
            compiler_params=pltpu.CompilerParams(
                collective_id=0, has_side_effects=True, vmem_limit_bytes=32 * 2**20),
            name="flow",
        )(*args)
        conc, pressure, porosity = pl.pallas_call(
            transport_kernel,
            out_shape=[jax.ShapeDtypeStruct(s, F32) for s in (turned, rows, rows)],
            in_specs=[vmem] * len(middle),
            out_specs=[hbm] * 3,
            scratch_shapes=[pltpu.VMEM(turned, F32), dma((6,))],
            compiler_params=pltpu.CompilerParams(vmem_limit_bytes=16 * 2**20),
            name="transport",
        )(*shared)
        return conc.reshape(species), pressure.reshape(tile), porosity.reshape(tile)

    return shards


def solution(mesh):
    specs = (P(None, None, "gx", "gy"),) + (P(None, "gx", "gy"),) * 5
    outs = (P(None, None, "gx", "gy"), P(None, "gx", "gy"), P(None, "gx", "gy"))
    sizes = (mesh.shape["gx"], mesh.shape["gy"])
    return jax.shard_map(build(sizes), mesh=mesh, in_specs=specs, out_specs=outs, check_vma=False)
```

```python
import math

import jax
import jax.numpy as jnp
from jax import lax
from jax.experimental import pallas as pl
from jax.experimental.pallas import tpu as pltpu
from jax.sharding import PartitionSpec as P

SWEEPS = 3
NSPEC, NZ, RX, LY = 8, 16, 16, 128
EX = RX + 8
FIELDS = 5
TINY = 1e-30
CUTS = (1, 1)
PLANES = [(f, d) for f in range(FIELDS) for d in range(4 if f < 2 else 3)]

ZONE_RATES = (0.02, 0.05, 0.1, 0.2)
ZONE_PERMEABILITY = (5.0, 10.0, 20.0, 40.0)
SOLUBILITY = 0.5
MOLAR_VOLUME = 0.05
STORAGE_COEF = 0.2
TIME_STEP = 0.2
CHEB_SPREAD = 0.92
STOICHIOMETRY = (-1.0, -1.0, 0.0, 0.0, 0.0, 0.0, 0.0, 0.0)

F32 = jnp.float32
MESH = pl.DeviceIdType.MESH
DIRS = ((-1, 0), (1, 0), (0, -1), (0, 1), (-1, -1), (1, -1), (-1, 1), (1, 1))
OPPOSITE = tuple(DIRS.index((-a, -b)) for a, b in DIRS)


def relax_weight(iteration):
    return 1.0 / (1.0 + CHEB_SPREAD * math.cos(math.pi * (2 * iteration + 1) / (2 * SWEEPS)))


def lookup(labels, table):
    out = jnp.where(labels == 0, F32(table[0]), F32(table[1]))
    out = jnp.where(labels == 2, F32(table[2]), out)
    return jnp.where(labels == 3, F32(table[3]), out)


def inverse(x):
    guess = pl.reciprocal(x, approx=True)
    return guess * (2.0 - x * guess)


def harmonic(a, b):
    return (2.0 * a * b) * inverse(jnp.maximum(a + b, TINY))


def lanes(x, shift):
    return pltpu.roll(x, shift % LY if isinstance(shift, int) else lax.rem(shift + 2 * LY, LY), 1)


def before(x):
    return pltpu.roll(x, 1, 0)


def after(x):
    return pltpu.roll(x, x.shape[0] - 1, 0)


def iota(rows, dim):
    return lax.broadcasted_iota(jnp.int32, (rows, LY), dim)


def flow_kernel(sizes, sp_in, por_in, old_in, src_in, zone_in, fix_in,
                spx, left, right, phi, rea, final, weight, side,
                pd, tx, ty, tz, cross, sp, por, zone, fix, old, src, pa, p1, p2, perm, stor, rhs, gain, step, known,
                sx, sy, sc, ssx, ssy, rx, ry, rc, rsx, rsy,
                in_sem, send_sem, recv_sem, s_send, s_recv, ready):
    gx, gy = lax.axis_index("gx"), lax.axis_index("gy")
    spots = []
    for dx, dy in DIRS:
        there = None
        for here, move, size in ((gx, dx, sizes[0]), (gy, dy, sizes[1])):
            if move:
                ok = here > 0 if move < 0 else here < size - 1
                there = ok if there is None else there & ok
        spots.append(((gx + dx, gy + dy), there))

    loads = [
        pltpu.make_async_copy(sp_in.at[pl.ds(0, 2)], sp.at[pl.ds(0, 2), pl.ds(0, NZ * RX)], in_sem.at[0]),
        pltpu.make_async_copy(zone_in, zone, in_sem.at[1]),
        pltpu.make_async_copy(por_in, por, in_sem.at[2]),
        pltpu.make_async_copy(old_in, old, in_sem.at[3]),
        pltpu.make_async_copy(src_in, src, in_sem.at[4]),
        pltpu.make_async_copy(fix_in, fix, in_sem.at[5]),
        pltpu.make_async_copy(sp_in.at[pl.ds(2, NSPEC - 2)], sp.at[pl.ds(2, NSPEC - 2), pl.ds(0, NZ * RX)], in_sem.at[6]),
    ]
    for c in loads:
        c.start()

    seam = sizes[1] // 2
    split = jnp.bool_(sizes[1] >= 4)
    at_lo, at_hi = (gy == seam - 1) & split, (gy == seam) & split
    at_seam = at_lo | at_hi
    barrier = pltpu.get_barrier_semaphore()
    expected = 0
    for i, (where, there) in enumerate(spots):
        far = (at_lo & (DIRS[i][1] > 0)) | (at_hi & (DIRS[i][1] < 0))
        counts = split & ((where[1] == seam - 1) | (where[1] == seam))
        beside = there & (far | jnp.logical_not(counts))

        @pl.when(beside)
        def _():
            pl.semaphore_signal(barrier, inc=1, device_id=where, device_id_type=MESH)
        expected = expected + (there & (far | jnp.logical_not(at_seam))).astype(jnp.int32)

    for i in range(8):
        @pl.when(jnp.logical_not(spots[i][1]))
        def _():
            if i < 2:
                rx[i] = jnp.zeros(rx.shape[1:], F32)
                rsx[i] = jnp.zeros(rsx.shape[1:], F32)
            elif i < 4:
                ry[i - 2] = jnp.zeros(ry.shape[1:], F32)
                rsy[i - 2] = jnp.zeros(rsy.shape[1:], F32)
            else:
                rc[i - 4] = jnp.zeros(rc.shape[1:], F32)
    plane = jnp.zeros((EX, LY), F32)
    for ref in (perm, pa, p1, p2, pd):
        ref[pl.ds(0, EX)] = plane
        ref[pl.ds((NZ + 1) * EX, EX)] = plane
    for ref in (stor, rhs, gain):
        for z in range(NZ):
            ref[pl.ds(z * EX + RX, 8)] = plane[:8]

    lane = iota(RX, 1)
    group = lax.shift_right_logical(lane, 3)
    low = (lane & 7) < 4
    for c in loads[:6]:
        c.wait()

    def at(z, rows=EX, skip=0):
        return pl.ds(pl.multiple_of(z * EX + skip, 8), rows)

    def plane_at(r, up=0):
        return pl.ds((1 + up) * EX + r % EX, NZ, stride=EX)

    def feed_mask(z):
        spot = (iota(8, 1) - 8 * z) & (LY - 1)
        return (spot == 8) | (spot == LY - 1)

    def own(z, packs):
        rows = pl.ds(pl.multiple_of(z * RX, 8), RX)
        c0, c1 = sp[0, rows], sp[1, rows]
        label = zone[z]
        reaction = lookup(label, ZONE_RATES) * (c0 * c1 - SOLUBILITY)
        new = por[z] - MOLAR_VOLUME * reaction
        solid = 1.0 - new
        k = lookup(label, ZONE_PERMEABILITY) * (new * new * new) * inverse(solid * solid)
        s = STORAGE_COEF * new
        free = 1.0 - fix[z].astype(F32)
        p, q = old[z], src[z]
        rea[rows] = reaction
        phi[rows] = new
        perm[at(z + 1, RX)] = k
        pa[at(z + 1, RX)] = p
        stor[at(z, RX)] = s
        rhs[at(z, RX)] = q
        gain[at(z, RX)] = free
        turned = [lanes(v, 8 * z + 4) for v in (k, p, s, q, free)]
        mask = feed_mask(z)
        fed_new = [jnp.where(mask, turned[f][8 * t:8 * t + 8], packs[FIELDS + 2 * f + t]) for f in range(2) for t in range(2)]
        return tuple(jnp.where(group == z, v, pack) for v, pack in zip(turned, packs)) + tuple(fed_new)

    zero, zero8 = jnp.zeros((RX, LY), F32), jnp.zeros((8, LY), F32)
    packs = lax.fori_loop(0, NZ, own, (zero,) * FIELDS + (zero8,) * 4, unroll=NZ)
    own_fed = packs[FIELDS:]
    packs = packs[:FIELDS]
    k, p, s, q, free = packs
    low8 = low[:8]
    y_edges = []
    for side_y in range(2):
        if side_y == 0:
            a, b = jnp.where(low, lanes(k, -4), p), jnp.where(low, lanes(s, -4), q)
            m = jnp.where(low8, lanes(free[:8], -4), free[8:])
        else:
            a, b = jnp.where(low, k, lanes(p, 4)), jnp.where(low, s, lanes(q, 4))
            m = jnp.where(low8, free[:8], lanes(free[8:], 4))
        sy[side_y, pl.ds(0, RX)] = a
        sy[side_y, pl.ds(RX, RX)] = b
        sy[side_y, pl.ds(2 * RX, 8)] = m
        y_edges.append((a, b))

    def parts(i):
        if i < 2:
            return sx.at[i], rx, i
        if i < 4:
            return sy.at[i - 2], ry, i - 2
        return sc.at[i - 4], rc, i - 4

    def pieces(i, from_ref, dst, slot, spans, sems):
        return [
            pltpu.make_async_remote_copy(
                src_ref=from_ref.at[span], dst_ref=dst.at[slot, span], send_sem=sems[0].at[i],
                recv_sem=sems[1].at[OPPOSITE[i]], device_id=spots[i][0], device_id_type=MESH)
            for span in spans]

    def spans(length, parts_of):
        cuts = [length * n // parts_of for n in range(parts_of + 1)]
        return [pl.ds(a, b - a) for a, b in zip(cuts[:-1], cuts[1:])]

    def copy(i):
        from_ref, _, _ = parts(i)
        _, dst, slot = parts(OPPOSITE[i])
        cut = spans(len(PLANES), CUTS[0]) if i < 2 else spans(from_ref.shape[0], 1)
        return pieces(i, from_ref, dst, slot, cut, (send_sem, recv_sem))

    def arrival(i):
        from_ref, dst, slot = parts(i)
        return pltpu.make_async_remote_copy(
            src_ref=from_ref, dst_ref=dst.at[slot], send_sem=send_sem.at[i],
            recv_sem=recv_sem.at[i], device_id=spots[i][0], device_id_type=MESH)

    def sparts(i):
        return (ssx.at[i], rsx, i) if i < 2 else (ssy.at[i - 2], rsy, i - 2)

    def scopy(i):
        from_ref, _, _ = sparts(i)
        _, dst, slot = sparts(OPPOSITE[i])
        cut = spans(NSPEC, CUTS[1]) if i < 2 else spans(NZ, 1)
        return pieces(i, from_ref, dst, slot, cut, (s_send, s_recv))

    def sarrival(i):
        from_ref, dst, slot = sparts(i)
        return pltpu.make_async_remote_copy(
            src_ref=from_ref, dst_ref=dst.at[slot], send_sem=s_send.at[i],
            recv_sem=s_recv.at[i], device_id=spots[i][0], device_id_type=MESH)

    def send(only, order, make):
        for i in order:
            @pl.when(spots[i][1] & only)
            def _():
                for c in make(i):
                    c.start()

    inner = jnp.logical_not(at_seam)


    @pl.when(at_hi)
    def _():
        pl.semaphore_wait(barrier, expected)
    send(at_hi, (2,), copy)

    slot = iota(1, 1) & 7
    half = slot & 3
    for side_y, (a, b) in enumerate(y_edges):
        far_slot = half == (3 if side_y == 0 else 0)
        back = 3 if side_y == 0 else -3
        for side_x in range(2):
            a1, a2, a3 = (v[r:r + 1] for v, r in zip((a,) * 3, (0, 1, 2) if side_x == 0 else (RX - 1, RX - 2, RX - 3)))
            b1, b2, f1, f2 = (
                v[r:r + 1] for v, r in zip((b, b, free, free), (0, 1) * 2 if side_x == 0 else (RX - 1, RX - 2) * 2))
            j = 2 * side_y + side_x
            sc[j, pl.ds(0, 1)] = jnp.where(far_slot, lanes(a3, back), a1)
            sc[j, pl.ds(1, 1)] = jnp.where(far_slot, lanes(b2, back), a2)
            if side_y == 0:
                masks = jnp.where((slot == 2) | (slot == 3), lanes(f1, -2), jnp.where(slot == 6, lanes(f2, 2), b1))
            else:
                masks = jnp.where((slot == 0) | (slot == 1), lanes(f1, -2), jnp.where(slot == 4, lanes(f2, 1), b1))
            sc[j, pl.ds(2, 1)] = masks
            sc[j, pl.ds(3, 1)] = a1
    send(at_hi, (4, 5), copy)

    def strided(ref, z0, row):
        return ref.at[pl.ds(z0 * EX + row, NZ, stride=EX)]

    fields = ((perm, 1), (pa, 1), (stor, 0), (rhs, 0), (gain, 0))
    for n, (f, d) in enumerate(PLANES):
        ref, z0 = fields[f]
        sx[0, n] = strided(ref, z0, d)[...]
        sx[1, n] = strided(ref, z0, RX - 1 - d)[...]

    loads[6].wait()
    for s in range(NSPEC):
        ssx[0, s] = sp[s, pl.ds(0, NZ, stride=RX)]
        ssx[1, s] = sp[s, pl.ds(RX - 1, NZ, stride=RX)]
    pair = lax.shift_right_logical(lane, 1)
    odd = (lane & 1) == 1

    halves = [zero, zero]
    for x in range(RX):
        for s in range(NSPEC):
            m = (x % 8) * 8 + s
            turned = lanes(sp[s, pl.ds(x, NZ, stride=RX)], 2 * m + 1)
            halves[x // 8] = jnp.where(pair == m, turned, halves[x // 8])
    lo, hi = halves
    ssy[0] = jnp.where(odd, lo, lanes(hi, -1))
    ssy[1] = jnp.where(odd, lanes(hi, 1), lo)
    send(at_hi, (2,), scopy)

    @pl.when(inner)
    def _():
        pl.semaphore_wait(barrier, expected)
    for edge_row, toward in ((seam - 2, 1), (seam + 1, -1)):
        @pl.when((gy == edge_row) & split)
        def _():
            pl.semaphore_signal(ready, inc=1, device_id=(gx, gy + toward), device_id_type=MESH)

    @pl.when(at_seam)
    def _():
        pl.semaphore_wait(ready, 1)
    later = lax.rem(gx, 16) == 14
    soon = jnp.logical_not(later)
    send(True, (1,), copy)
    send(soon, (0,), copy)
    send(inner | at_lo, (2, 4, 5), copy)
    send(inner | at_hi, (3, 6, 7), copy)

    send(True, (1,), scopy)
    send(soon, (0,), scopy)
    send(inner | at_lo, (2,), scopy)
    send(inner | at_hi, (3,), scopy)

    for s in range(NSPEC):
        for x in range(RX):
            c = sp[s, pl.ds(x, NZ, stride=RX)]
            spx[s, pl.ds(NZ * (x + 1), NZ)] = c
            left[s, pl.ds(NZ * x, NZ)] = lanes(c, 1)
            right[s, pl.ds(NZ * x, NZ)] = lanes(c, -1)

    def face_x(r):
        tx[r % EX] = harmonic(perm[plane_at(r)], perm[plane_at(r - 1)])

    def in_plane(r):
        k = perm[plane_at(r)]
        ty[0, r % EX] = jnp.where(lane > 0, harmonic(k, lanes(k, 1)), 0.0)
        ty[1, r % EX] = jnp.where(lane < LY - 1, harmonic(k, lanes(k, -1)), 0.0)
        tz[0, r % EX] = harmonic(k, perm[plane_at(r, -1)])
        tz[1, r % EX] = harmonic(k, perm[plane_at(r, 1)])

    def coefficients(r):
        at_r = r % EX
        s = stor[plane_at(r, -1)]
        total = (s + tx[at_r] + tx[(r + 1) % EX]) + (ty[0, at_r] + ty[1, at_r]) + (tz[0, at_r] + tz[1, at_r])
        step[at_r] = gain[plane_at(r, -1)] * inverse(jnp.maximum(total, TINY))
        known[at_r] = s * pa[plane_at(r)] + rhs[plane_at(r, -1)]

    def relax(it, r):
        now, new, at_r = levels[it], levels[it + 1], r % EX
        p = now[plane_at(r)]
        out = stor[plane_at(r, -1)] * p
        out = out + tx[at_r] * (p - now[plane_at(r - 1)])
        out = out + tx[(r + 1) % EX] * (p - now[plane_at(r + 1)])
        out = out + tz[0, at_r] * (p - now[plane_at(r, -1)])
        out = out + tz[1, at_r] * (p - now[plane_at(r, 1)])
        out = out + ty[0, at_r] * (p - lanes(p, 1))
        out = out + ty[1, at_r] * (p - lanes(p, -1))
        new[plane_at(r)] = p + F32(relax_weight(it)) * step[at_r] * (known[at_r] - out)

    levels = (pa, p1, p2, pd)
    for r in range(1, RX):
        face_x(r)
    for r in range(RX):
        in_plane(r)
    for r in range(1, RX - 1):
        coefficients(r)
    for it in range(SWEEPS):
        for r in range(1 + it, RX - 1 - it):
            relax(it, r)

    send(later, (0,), copy)
    send(later, (0,), scopy)

    @pl.when(at_lo)
    def _():
        pl.semaphore_wait(barrier, expected)
    send(at_lo, (3, 6, 7), copy)
    send(at_lo, (3,), scopy)

    for i in range(2):
        @pl.when(spots[i][1])
        def _():
            arrival(i).wait_recv()
    for n, (f, d) in enumerate(PLANES):
        ref, z0 = fields[f]
        strided(ref, z0, RX + d)[...] = rx[1, n]
        strided(ref, z0, EX - 1 - d)[...] = rx[0, n]
    for r in (-3, -2, -1, 0, RX, RX + 1, RX + 2, RX + 3):
        face_x(r)
    for r in (-3, -2, -1, RX, RX + 1, RX + 2):
        in_plane(r)
    for r in (-3, -2, -1, 0, RX - 1, RX, RX + 1, RX + 2):
        coefficients(r)
    for it in range(SWEEPS):
        for j in range(4):
            relax(it, it - 3 + j)
            relax(it, RX - 1 - it + j)

    lane24 = iota(EX, 1)
    group8 = lax.shift_right_logical(iota(8, 1), 3)
    tails, tail_fed, fed_1, fed_2 = [zero8] * FIELDS, [zero8] * 2, [zero8] * 3, [zero8] * 3
    for z in range(NZ):
        mask = feed_mask(z)
        for f, (ref, z0) in enumerate(fields):
            turned = lanes(ref[at(z + z0, 8, RX)], 8 * z + 4)
            tails[f] = jnp.where(group8 == z, turned, tails[f])
            if f < 2:
                tail_fed[f] = jnp.where(mask, turned, tail_fed[f])
        for ref, pack in ((p1, fed_1), (p2, fed_2)):
            for t in range(3):
                pack[t] = jnp.where(mask, lanes(ref[at(z + 1, 8, 8 * t)], 8 * z + 4), pack[t])
    whole = [jnp.concatenate([a, b], axis=0) for a, b in zip(packs, tails)]
    fed_k = jnp.concatenate([own_fed[0], own_fed[1], tail_fed[0]], axis=0)
    fed = [
        jnp.concatenate([own_fed[2], own_fed[3], tail_fed[1]], axis=0),
        jnp.concatenate(fed_1, axis=0), jnp.concatenate(fed_2, axis=0),
    ]

    for i in range(2, 8):
        @pl.when(spots[i][1])
        def _():
            arrival(i).wait_recv()

    column = lane24 & 7
    low24 = column < 4
    pad2, pad4 = jnp.zeros((2, LY), F32), jnp.zeros((4, LY), F32)
    strips = []
    for d in range(2):
        minus, plus = rc.at[2 * d], rc.at[2 * d + 1]
        def corner(ref):
            x, y, z = (ref[pl.ds(n, 1)] for n in range(3))
            if d == 0:
                return (x, y, lanes(x, 3)), (z, lanes(y, 3)), (lanes(z, 2), lanes(z, -1))
            return (x, y, lanes(x, -3)), (z, lanes(y, -3)), (lanes(z, 2), lanes(z, -2))

        (pa1, pa2, pa3), (pb1, pb2), (pm1, pm2) = corner(plus)
        (ma1, ma2, ma3), (mb1, mb2), (mm1, mm2) = corner(minus)
        a = jnp.concatenate([ry[d, pl.ds(0, RX)], pa1, pa2, pa3, pad2, ma3, ma2, ma1], axis=0)
        b = jnp.concatenate([ry[d, pl.ds(RX, RX)], pb1, pb2, pad4, mb2, mb1], axis=0)
        m = ry[d, pl.ds(2 * RX, 8)]
        m_tail = [pm1, pm2, pad4, mm2, mm1]
        if d == 0:
            halos = (a, lanes(a, -4), b, lanes(b, -4), jnp.concatenate([m, lanes(m, -4)] + m_tail, axis=0))
        else:
            halos = (lanes(a, 4), a, lanes(b, 4), b, jnp.concatenate([lanes(m, 4), m] + m_tail, axis=0))
        k, p, s, q, free = (
            jnp.where(low24, h, w) if d == 0 else jnp.where(low24, w, h) for h, w in zip(halos, whole))
        end = column == (7 if d == 0 else 0)
        turn = -1 if d == 0 else 1
        beyond = [lanes(v, turn) for v in [fed_k] + fed]

        def sides(v, outer_v):
            lo, hi = lanes(v, 1), lanes(v, -1)
            if d == 0:
                hi = jnp.where(end, outer_v, hi)
            else:
                lo = jnp.where(end, outer_v, lo)
            return before(v), after(v), lo, hi, lanes(v, 8), lanes(v, -8)

        terms = [harmonic(k, v) for v in sides(k, beyond[0])]
        terms[4] = jnp.where(lane24 < 8, 0.0, terms[4])
        terms[5] = jnp.where(lane24 < LY - 8, terms[5], 0.0)
        total = s + ((terms[0] + terms[1]) + (terms[2] + terms[3])) + (terms[4] + terms[5])
        g = free * inverse(jnp.maximum(total, TINY))
        right_side = s * p + q
        for it in range(SWEEPS):
            flows = [t * (p - v) for t, v in zip(terms, sides(p, beyond[1 + it]))]
            r = (right_side - s * p) - ((flows[0] + flows[1]) + (flows[2] + flows[3])) - (flows[4] + flows[5])
            p = p + F32(relax_weight(it)) * g * r
        across = terms[2] * (p - lanes(p, 1)) if d == 0 else terms[3] * (p - lanes(p, -1))
        strips.append((across, p))
    own_edge = jnp.where(low24, strips[1][1], strips[0][1])
    own_flow = jnp.where(low24, strips[1][0], strips[0][0])
    outer = (lane24 < 3) | (lane24 > LY - 4)
    for z in range(NZ):
        pd[at(z + 1)] = jnp.where(outer, lanes(own_edge, -(8 * z + 4)), pd[at(z + 1)])
        cross[at(z, RX)] = lanes(own_flow[:RX], -(8 * z + 4))

    first, last = lane == 0, lane == LY - 1
    for x in range(RX):
        p = pd[plane_at(x)]
        final[pl.ds(x, NZ, stride=RX)] = p
        through = cross[plane_at(x, -1)]
        flows = [
            tx[x] * (p - pd[plane_at(x - 1)]),
            tx[x + 1] * (p - pd[plane_at(x + 1)]),
            jnp.where(first, through, ty[0, x] * (p - lanes(p, 1))),
            jnp.where(last, through, ty[1, x] * (p - lanes(p, -1))),
            tz[0, x] * (p - pd[plane_at(x, -1)]),
            tz[1, x] * (p - pd[plane_at(x, 1)]),
        ]
        scale = TIME_STEP * inverse(phi[pl.ds(x, NZ, stride=RX)])
        out = [jnp.maximum(f, 0.0) for f in flows]
        out = ((out[0] + out[1]) + (out[2] + out[3])) + (out[4] + out[5])
        weight[0, x] = 1.0 - scale * out
        for n, f in enumerate(flows):
            weight[n + 1, x] = -scale * jnp.minimum(f, 0.0)

    for i in range(4):
        @pl.when(spots[i][1])
        def _():
            sarrival(i).wait_recv()
    m_lo, m_hi = rsy[0], rsy[1]
    side[0] = jnp.where(odd, lanes(m_lo, 1), lanes(m_hi, -1))
    side[1] = jnp.where(odd, m_lo, m_hi)
    for s in range(NSPEC):
        spx[s, pl.ds(0, NZ)] = rsx[0, s]
        spx[s, pl.ds(NZ * (RX + 1), NZ)] = rsx[1, s]
    for i in range(8):
        @pl.when(spots[i][1])
        def _():
            arrival(i).wait_send()
            if i < 4:
                sarrival(i).wait_send()


def transport_kernel(spx, left, right, phi, rea, final, weight, side, conc_out, p_out, phi_out, conc, sem):
    used = pl.ds(0, NZ * RX)
    outs = [
        pltpu.make_async_copy(phi.at[used], phi_out, sem.at[0]),
        pltpu.make_async_copy(final.at[used], p_out, sem.at[1]),
    ]
    for c in outs:
        c.start()
    lane = iota(RX, 1)
    first, last = lane == 0, lane == LY - 1
    group = 2
    for s0 in range(0, NSPEC, group):
        for x in range(RX):
            w = [weight[n, x] for n in range(7)]
            for s in range(s0, s0 + group):
                def row(shift):
                    return spx[s, pl.ds(NZ * (x + 1) + shift, NZ)]

                turned = lanes(side[x // 8], -(2 * ((x % 8) * 8 + s) + 1))
                around = [
                    row(-NZ), row(NZ),
                    jnp.where(first, turned, left[s, pl.ds(NZ * x, NZ)]),
                    jnp.where(last, turned, right[s, pl.ds(NZ * x, NZ)]),
                    row(-1), row(1),
                ]
                total = row(0) * w[0]
                for a, b in zip(w[1:], around):
                    total = total + a * b
                if STOICHIOMETRY[s]:
                    total = total + STOICHIOMETRY[s] * rea[pl.ds(x, NZ, stride=RX)]
                conc[s, pl.ds(x, NZ, stride=RX)] = total
        some = pl.ds(s0, group)
        c = pltpu.make_async_copy(conc.at[some, used], conc_out.at[some], sem.at[2 + s0 // group])
        c.start()
        outs.append(c)
    for c in outs:
        c.wait()


def build(sizes):
    tile, rows, long_rows = (NZ, RX, LY), (NZ * RX, LY), ((NZ + 1) * RX, LY)
    flat, padded, planes = ((NZ + 1) * EX, LY), ((NZ + 3) * EX, LY), (EX, NZ, LY)
    species, turned, long_turned = (NSPEC, NZ, RX, LY), (NSPEC, NZ * RX, LY), (NSPEC, (NZ + 1) * RX, LY)
    halo = [
        (2, len(PLANES), NZ, LY), (2, 2 * RX + 8, LY), (4, 4, LY), (2, NSPEC, NZ, LY), (2, NZ, LY),
    ]
    vmem = pl.BlockSpec(memory_space=pltpu.VMEM)
    hbm = pl.BlockSpec(memory_space=pltpu.HBM)
    middle = [
        (NSPEC, (RX + 2) * NZ, LY), turned, turned, long_rows, long_rows, long_rows, (7, RX, NZ, LY), (2, NZ, LY),
    ]
    dma = pltpu.SemaphoreType.DMA

    def shards(sp, *args):
        args = [pltpu.with_memory_space_constraint(a, pltpu.HBM) for a in (sp.reshape(turned), *args)]
        shared = pl.pallas_call(
            lambda *refs: flow_kernel(sizes, *refs),
            out_shape=[pltpu.VMEM(shape, F32) for shape in middle],
            in_specs=[hbm] * 6,
            out_specs=[vmem] * len(middle),
            scratch_shapes=[
                pltpu.VMEM(padded, F32), pltpu.VMEM(planes, F32), pltpu.VMEM((2,) + planes, F32),
                pltpu.VMEM((2,) + planes, F32), pltpu.VMEM(flat, F32), pltpu.VMEM(long_turned, F32),
                pltpu.VMEM(tile, F32), pltpu.VMEM(tile, jnp.int32), pltpu.VMEM(tile, jnp.int32),
                pltpu.VMEM(tile, F32), pltpu.VMEM(tile, F32),
                *[pltpu.VMEM(padded, F32)] * 4, *[pltpu.VMEM(flat, F32)] * 3, *[pltpu.VMEM(planes, F32)] * 2,
                *[pltpu.VMEM(shape, F32) for shape in halo + halo],
                dma((7,)), dma((8,)), dma((8,)), dma((4,)), dma((4,)), pltpu.SemaphoreType.REGULAR,
            ],
            compiler_params=pltpu.CompilerParams(
                collective_id=0, has_side_effects=True, vmem_limit_bytes=32 * 2**20),
            name="flow",
        )(*args)
        conc, pressure, porosity = pl.pallas_call(
            transport_kernel,
            out_shape=[jax.ShapeDtypeStruct(s, F32) for s in (turned, rows, rows)],
            in_specs=[vmem] * len(middle),
            out_specs=[hbm] * 3,
            scratch_shapes=[pltpu.VMEM(long_turned, F32), dma((6,))],
            compiler_params=pltpu.CompilerParams(vmem_limit_bytes=16 * 2**20),
            name="transport",
        )(*shared)
        return conc.reshape(species), pressure.reshape(tile), porosity.reshape(tile)

    return shards


def solution(mesh):
    specs = (P(None, None, "gx", "gy"),) + (P(None, "gx", "gy"),) * 5
    outs = (P(None, None, "gx", "gy"), P(None, "gx", "gy"), P(None, "gx", "gy"))
    sizes = (mesh.shape["gx"], mesh.shape["gy"])
    return jax.shard_map(build(sizes), mesh=mesh, in_specs=specs, out_specs=outs, check_vma=False)
```
